32 devices in a mesh: rows: 8 (over z, x), cols: 4 (over y, core).
Axes of the slice: x: 2, y: 2, z: 4, core: 2. Of those that a mesh axis runs over, the one named last changes fastest.
Arguments:
- residues: bfloat16 [8192, 640], P(('rows', 'cols')), may hold values from -6 to 6
- segment_ids: int32 [32, 256], P(('rows', 'cols')), may hold values from 0 to 3, never falling along the last dimension, each value on 1 to 128 neighbouring positions
- cotangent: bfloat16 [8192, 640], P(('rows', 'cols')), may hold values from -6 to 6
- qkv_weight: float32 [2, 640, 1920], P(None, 'rows', 'cols'), may hold values from -0.25 to 0.25
- qkv_first: float32 [2, 640, 1920], P(None, 'rows', 'cols'), may hold values from -512 to 512
- qkv_second: float32 [2, 640, 1920], P(None, 'rows', 'cols'), may hold values from 6717.44 to 27033.6
- out_weight: float32 [2, 640, 640], P(None, 'cols', 'rows'), may hold values from -2 to 2
- out_first: float32 [2, 640, 640], P(None, 'cols', 'rows'), may hold values from -96 to 96
- out_second: float32 [2, 640, 640], P(None, 'cols', 'rows'), may hold values from 208 to 832
- up_weight: float32 [2, 640, 2560], P(None, 'rows', 'cols'), may hold values from -0.25 to 0.25
- up_first: float32 [2, 640, 2560], P(None, 'rows', 'cols'), may hold values from -128 to 128
- up_second: float32 [2, 640, 2560], P(None, 'rows', 'cols'), may hold values from 417.792 to 1720.32
- down_weight: float32 [2, 2560, 640], P(None, 'cols', 'rows'), may hold values from -0.125 to 0.125
- down_first: float32 [2, 2560, 640], P(None, 'cols', 'rows'), may hold values from -320 to 320
- down_second: float32 [2, 2560, 640], P(None, 'cols', 'rows'), may hold values from 2867.2 to 11468.8
- vectors: float32 [2, 13, 640], replicated, may hold values from -1.5 to 1.5
- vector_first: float32 [2, 13, 640], replicated, may hold values from -512 to 512
- vector_second: float32 [2, 13, 640], replicated, may hold values from 512 to 131072
Outputs:
- block_out: float32 [8192, 640], P(('rows', 'cols'))
- input_grad: float32 [8192, 640], P(('rows', 'cols'))
- qkv_new: float32 [2, 640, 1920], P(None, 'rows', 'cols')
- qkv_first_new: float32 [2, 640, 1920], P(None, 'rows', 'cols')
- qkv_second_new: float32 [2, 640, 1920], P(None, 'rows', 'cols')
- out_new: float32 [2, 640, 640], P(None, 'cols', 'rows')
- out_first_new: float32 [2, 640, 640], P(None, 'cols', 'rows')
- out_second_new: float32 [2, 640, 640], P(None, 'cols', 'rows')
- up_new: float32 [2, 640, 2560], P(None, 'rows', 'cols')
- up_first_new: float32 [2, 640, 2560], P(None, 'rows', 'cols')
- up_second_new: float32 [2, 640, 2560], P(None, 'rows', 'cols')
- down_new: float32 [2, 2560, 640], P(None, 'cols', 'rows')
- down_first_new: float32 [2, 2560, 640], P(None, 'cols', 'rows')
- down_second_new: float32 [2, 2560, 640], P(None, 'cols', 'rows')
- vectors_new: float32 [2, 13, 640], replicated
- vector_first_new: float32 [2, 13, 640], replicated
- vector_second_new: float32 [2, 13, 640], replicated
The draws below stay inside these ranges and needn't reach their ends.
Inputs may be any that keep to these rules, and one draw needn't show every extreme that they name: `segment_ids`: segment numbers never fall along a packed row.
All inputs are finite; a program needn't handle non-finite values.
Results may differ from the reference program's by a relative error of at most 0.024.
Values may be sent and summed in bfloat16 or wider, within the bound.
No kernel may reach another device: no remote copies, remote signals or barrier semaphores. Data moves between devices by JAX's collectives and lax.ppermute only.
A program may use at most 192 MiB of HBM per device.

```python
import math
import jax
import jax.numpy as jnp
import numpy as np
from jax import lax

D = 640
HEADS = 20
HEAD_DIM = 32
FF = 2560
LAYERS = 2
SEGS = 4
STEP = 5
TOK_DEV = 256
PACKED = 32
TOKENS = 8192
N_ROWS = 8
N_COLS = 4


def draw_vectors(key, part):
    gain_key, shift_key = jax.random.split(jax.random.fold_in(key, 17))
    row_number = jnp.arange(13, dtype=jnp.int32)[None, :, None]
    gain_rows = (row_number == 0) | (row_number == 6)
    gain_part = jnp.clip(1.0 + 0.15 * jax.random.normal(gain_key, (LAYERS, 13, D), jnp.float32), 0.6, 1.4)
    shift_part = jnp.clip(0.3 * jax.random.normal(shift_key, (LAYERS, 13, D), jnp.float32), -1.5, 1.5)
    return jnp.where(gain_rows, gain_part, shift_part)


def draw_vector_second(key, part):
    moment_key = jax.random.fold_in(key, 29)
    low_end = math.log(1.0 / 16.0)
    high_end = math.log(16.0)
    logs = jnp.clip(1.3 * jax.random.normal(moment_key, (LAYERS, 13, D), jnp.float32), low_end, high_end)
    total = jnp.float32(TOKENS)
    return jnp.clip(total * jnp.exp(logs), total / 16.0, total * 16.0)


def block_levels(key, shape, cuts, low, high):
    factor_of, own = 1.0, jax.random.fold_in(key, 6)
    for dim, shards_of in cuts:
        heights = jnp.exp(jax.random.uniform(jax.random.fold_in(own, dim), (shards_of,), jnp.float32, low / len(cuts), high / len(cuts)))
        factor_of = factor_of * jnp.repeat(heights, shape[dim] // shards_of).reshape([-1 if axis == dim else 1 for axis in range(len(shape))])
    return factor_of


def profile(count, total, limit, lean):
    loads = [(1 << 20) // math.isqrt(grade ** lean) + 1 for grade in range(2, count + 1)]
    surplus, given = total - limit - (count - 1), [1] * (count - 1)
    while surplus > 0:
        free = [i for i in range(count - 1) if given[i] < limit]
        pool, budget = sum([loads[i] for i in free]), surplus
        for i in free:
            more = min(limit - given[i], max(1, budget * loads[i] // pool), surplus)
            given[i] = given[i] + more
            surplus = surplus - more
    return np.array([limit] + given)


def ragged(rng, count, total, limit, slope):
    if count == 2:
        one = jax.random.randint(rng, (), max(1, total - limit), min(limit, total - 1) + 1)
        return jnp.stack([one, total - one])
    lengths = jnp.asarray(profile(count, total, limit, slope), jnp.int32)
    couples = (count - 1) // 2
    donor, sink = lengths[1:1 + 2 * couples:2], lengths[2:2 + 2 * couples:2]
    room = jnp.minimum(donor - 1, limit - sink)
    moved = jax.random.randint(jax.random.fold_in(rng, 1), (couples,), 0, 1 << 20) % (room + 1)
    lengths = lengths.at[1:1 + 2 * couples:2].set(donor - moved).at[2:2 + 2 * couples:2].set(sink + moved)
    return lengths[jax.random.permutation(jax.random.fold_in(rng, 2), count)]


def centred(own_key, extent, spread, limit, cuts=(), held_as=jnp.bfloat16):
    loudness = block_levels(own_key, extent, cuts, -0.22, 0.18) if cuts else 1.0
    entries = jax.random.normal(own_key, extent, jnp.float32) * spread * loudness
    return jnp.minimum(jnp.maximum(entries, -limit), limit).astype(held_as)


def setup_inputs(seed: int = 0) -> dict:
    key_of = jax.random.split(jax.random.key(seed), 19)
    return {
        "residues": centred(key_of[0], (TOKENS, D), 1.0, 6.0, ((0, 32),)),
        "segment_ids": jax.vmap(lambda own: jnp.searchsorted(jnp.cumsum(ragged(own, SEGS, TOK_DEV, TOK_DEV // 2, 1)), jnp.arange(TOK_DEV), side="right"))(jax.random.split(key_of[1], PACKED)).reshape((PACKED, TOK_DEV)).astype(jnp.int32),
        "cotangent": centred(key_of[2], (TOKENS, D), 1.0, 6.0, ((0, 32),)),
        "qkv_weight": centred(key_of[3], (LAYERS, D, 3 * D), D ** -0.5, 0.25, ((1, 8), (2, 4)), jnp.float32),
        "qkv_first": centred(key_of[4], (LAYERS, D, 3 * D), (TOKENS ** 0.5), 512.0, ((1, 8), (2, 4)), jnp.float32),
        "qkv_second": jnp.clip(jnp.exp(math.log(27033.6) - 1.3923734 * jax.random.uniform(key_of[5], (LAYERS, D, 3 * D), jnp.float32) ** block_levels(key_of[5], (LAYERS, D, 3 * D), ((1, 8), (2, 4)), -0.2, 0.2)), 6717.44, 27033.6),
        "out_weight": centred(key_of[6], (LAYERS, D, D), (D * 4 // TOK_DEV) ** -0.5, 2.0, ((1, 4), (2, 8)), jnp.float32),
        "out_first": centred(key_of[7], (LAYERS, D, D), ((8 * N_ROWS * N_COLS) ** 0.5), 96.0, ((1, 4), (2, 8)), jnp.float32),
        "out_second": jnp.clip(jnp.exp(math.log(832.0) - 1.3862944 * jax.random.uniform(key_of[8], (LAYERS, D, D), jnp.float32) ** block_levels(key_of[8], (LAYERS, D, D), ((1, 4), (2, 8)), -0.2, 0.2)), 208.0, 832.0),
        "up_weight": centred(key_of[9], (LAYERS, D, FF), D ** -0.5, 0.25, ((1, 8), (2, 4)), jnp.float32),
        "up_first": centred(key_of[10], (LAYERS, D, FF), (0.25 * TOKENS ** 0.5), 128.0, ((1, 8), (2, 4)), jnp.float32),
        "up_second": jnp.clip(jnp.exp(math.log(1720.32) - 1.4152819 * jax.random.uniform(key_of[11], (LAYERS, D, FF), jnp.float32) ** block_levels(key_of[11], (LAYERS, D, FF), ((1, 8), (2, 4)), -0.2, 0.2)), 417.792, 1720.32),
        "down_weight": centred(key_of[12], (LAYERS, FF, D), FF ** -0.5, 0.125, ((1, 4), (2, 8)), jnp.float32),
        "down_first": centred(key_of[13], (LAYERS, FF, D), (0.65 * TOKENS ** 0.5), 320.0, ((1, 4), (2, 8)), jnp.float32),
        "down_second": jnp.clip(jnp.exp(math.log(11468.8) - 1.3862944 * jax.random.uniform(key_of[14], (LAYERS, FF, D), jnp.float32) ** block_levels(key_of[14], (LAYERS, FF, D), ((1, 4), (2, 8)), -0.2, 0.2)), 2867.2, 11468.8),
        "vectors": draw_vectors(jax.random.fold_in(key_of[18], 71), 0),
        "vector_first": centred(key_of[16], (LAYERS, 13, D), (TOKENS ** 0.5), 512.0, (), jnp.float32),
        "vector_second": draw_vector_second(jax.random.fold_in(key_of[18], 71), 0),
    }


HIGH = lax.Precision.HIGHEST
norm_eps = 1e-05
beta_one = 0.5
beta_two = 0.55
adam_eps = 1e-08
decay_rate = 0.01

@jax.custom_vjp
def low(v):
    return lax.optimization_barrier(v.astype(jnp.bfloat16)).astype(jnp.float32)

@jax.custom_vjp
def low_back(v):
    return v

def low_keep(v):
    return (low(v), None)

def low_pass(kept, grad):
    return (grad,)

def back_keep(v):
    return (v, None)

def back_low(kept, grad):
    return (low(grad),)
low.defvjp(low_keep, low_pass)
low_back.defvjp(back_keep, back_low)

def layer_norm(values_in, norm_gain, norm_shift):
    average = lax.optimization_barrier(jnp.mean(values_in, axis=-1, keepdims=True))
    centered = values_in - average
    variance = lax.optimization_barrier(jnp.mean(centered * centered, axis=-1, keepdims=True))
    return centered * lax.rsqrt(variance + norm_eps) * norm_gain + norm_shift

def positions_of(segment_rows):
    length_now = segment_rows.shape[-1]
    places = jnp.arange(length_now, dtype=jnp.int32) * jnp.ones_like(segment_rows)
    previous = jnp.concatenate([segment_rows[..., :1] - 1, segment_rows[..., :-1]], axis=-1)
    starts = jnp.where(segment_rows != previous, places, jnp.zeros_like(places))
    segment_start = lax.cummax(starts, axis=segment_rows.ndim - 1)
    return places - segment_start

def rotary_tables(places):
    freq_index = jnp.arange(HEAD_DIM // 2, dtype=jnp.float32)
    inverse = jnp.exp(freq_index * (-2.0 * math.log(10000.0) / HEAD_DIM))
    angles = places.astype(jnp.float32)[..., None] * inverse
    cosine = jnp.cos(angles)
    sine = jnp.sin(angles)
    return (jnp.concatenate([cosine, cosine], axis=-1), jnp.concatenate([sine, sine], axis=-1))

def rotate(vectors_in, cosine, sine):
    half_width = vectors_in.shape[-1] // 2
    turned = jnp.concatenate([-vectors_in[..., half_width:], vectors_in[..., :half_width]], axis=-1)
    return vectors_in * cosine + turned * sine

def block_forward(hidden, segment_rows, qkv_weight, out_weight, up_weight, down_weight, vectors):
    group_rows, length_now = segment_rows.shape
    cosine, sine = rotary_tables(positions_of(segment_rows))
    cosine = cosine[:, :, None, :]
    sine = sine[:, :, None, :]
    allowed = segment_rows[:, :, None] == segment_rows[:, None, :]
    for ordinal in range(LAYERS):
        layer_vectors = vectors[ordinal]
        normed = low(layer_norm(hidden, layer_vectors[0], layer_vectors[1]))
        projected = jnp.einsum('rsd,de->rse', normed, low(qkv_weight[ordinal]), precision=HIGH)
        projected = low_back(projected + layer_vectors[2:5].reshape(3 * D))
        split_view = projected.reshape(group_rows, length_now, 3, HEADS, HEAD_DIM)
        queries = low(rotate(split_view[:, :, 0], cosine, sine) * HEAD_DIM ** (-0.5))
        keys_rot = low(rotate(split_view[:, :, 1], cosine, sine))
        values = low(split_view[:, :, 2])
        scores = jnp.einsum('rqhd,rkhd->rhqk', queries, keys_rot, precision=HIGH)
        scores = low_back(jnp.where(allowed[:, None], scores, -1e+30))
        probabilities = low(jax.nn.softmax(scores, axis=-1))
        context = jnp.einsum('rhqk,rkhd->rqhd', probabilities, values, precision=HIGH)
        context = low(low_back(context.reshape(group_rows, length_now, D)))
        attended = jnp.einsum('rsd,de->rse', context, low(out_weight[ordinal]), precision=HIGH)
        attended = low_back(attended + layer_vectors[5])
        middle = hidden + attended
        ffn_in = low(layer_norm(middle, layer_vectors[6], layer_vectors[7]))
        pre_act = jnp.einsum('rsd,df->rsf', ffn_in, low(up_weight[ordinal]), precision=HIGH)
        pre_act = low_back(pre_act + layer_vectors[8:12].reshape(FF))
        activated = low(jax.nn.gelu(pre_act, approximate=False))
        branch = jnp.einsum('rsf,fd->rsd', activated, low(down_weight[ordinal]), precision=HIGH)
        branch = low_back(branch + layer_vectors[12])
        hidden = middle + branch
    return hidden

def adamw(weight, gradient, first, second, rate, step_count):
    first_new = beta_one * first + (1.0 - beta_one) * gradient
    second_new = beta_two * second + (1.0 - beta_two) * gradient * gradient
    first_hat = first_new / (1.0 - beta_one ** step_count)
    second_hat = second_new / (1.0 - beta_two ** step_count)
    weight_new = weight - rate * (first_hat / (jnp.sqrt(second_hat) + adam_eps) + decay_rate * weight)
    return (weight_new, first_new, second_new)

def reference(residues, segment_ids, cotangent, qkv_weight, qkv_first, qkv_second, out_weight, out_first, out_second, up_weight, up_first, up_second, down_weight, down_first, down_second, vectors, vector_first, vector_second):
    params = (qkv_weight, out_weight, up_weight, down_weight, vectors)
    group_rows = math.gcd(PACKED, max(1, 2048 // TOK_DEV))
    block_count = PACKED // group_rows
    inputs = residues.astype(jnp.float32).reshape(block_count, group_rows, TOK_DEV, D)
    block_segments = segment_ids.reshape(block_count, group_rows, TOK_DEV)
    block_cotangents = cotangent.astype(jnp.float32).reshape(block_count, group_rows, TOK_DEV, D)

    def visit(totals, block_items):
        block_in, segment_rows, block_cot = block_items

        def apply_block(hidden, *weights):
            return block_forward(hidden, segment_rows, *weights)
        result, pullback = jax.vjp(apply_block, block_in, *params)
        gradients = pullback(block_cot)
        totals = tuple((total + extra for total, extra in zip(totals, gradients[1:])))
        return (totals, (result, gradients[0]))
    zero_sums = tuple((jnp.zeros_like(weight) for weight in params))
    totals, (outputs, input_grads) = lax.scan(visit, zero_sums, (inputs, block_segments, block_cotangents))
    step_count = float(STEP)
    rate_qkv = 0.5 / math.sqrt(D)
    rate_out = 0.5 / math.sqrt(max(D * 4 // TOK_DEV, 1))
    rate_down = 0.5 / math.sqrt(FF)
    qkv_new = adamw(qkv_weight, totals[0], qkv_first, qkv_second, rate_qkv, step_count)
    out_new = adamw(out_weight, totals[1], out_first, out_second, rate_out, step_count)
    up_new = adamw(up_weight, totals[2], up_first, up_second, rate_qkv, step_count)
    down_new = adamw(down_weight, totals[3], down_first, down_second, rate_down, step_count)
    vec_new = adamw(vectors, totals[4], vector_first, vector_second, 0.1, step_count)
    return (outputs.reshape(TOKENS, D), input_grads.reshape(TOKENS, D), qkv_new[0], qkv_new[1], qkv_new[2], out_new[0], out_new[1], out_new[2], up_new[0], up_new[1], up_new[2], down_new[0], down_new[1], down_new[2], vec_new[0], vec_new[1], vec_new[2])
```

```python
import functools
import math

import jax
import jax.numpy as jnp
from jax import lax
from jax.experimental import pallas as pl
from jax.experimental.pallas import tpu as pltpu
from jax.sharding import PartitionSpec as P

HEAD_DIM = 32
LAYERS = 2
STEP = 5
TOK_DEV = 256

norm_eps = 1e-05
beta_one = 0.5
beta_two = 0.55
adam_eps = 1e-08
decay_rate = 0.01

f32 = jnp.float32
bf16 = jnp.bfloat16
VMEM = pltpu.VMEM
ANY = pl.ANY
SQRT_HALF = math.sqrt(0.5)
INV_SQRT_2PI = 1.0 / math.sqrt(2.0 * math.pi)
HEADS_A_STEP = 4


class Net:
    def __init__(self, rows, cols):
        self.rows, self.cols = rows, cols
        self.group = [(rr, rc) for rc in range(0, cols, 4) for rr in range(0, rows, 2)]
        self.g = len(self.group)
        self.half = self.g // 2

    def send(self, x, rr, rc):
        mask = rr * self.cols + rc
        pairs = [(i, i ^ mask) for i in range(self.rows * self.cols)]
        return lax.ppermute(x, ("rows", "cols"), pairs)

    def rels(self, kind, core):
        dr, dc = {"o": (0, 0), "x": (1, 0), "y": (0, 2), "d": (1, 2)}[kind]
        return [(rr ^ dr, rc ^ dc ^ core) for rr, rc in self.group]

    def gather(self, unit):
        h = self.half
        own = jnp.stack([unit] + [self.send(unit, rr, rc) for rr, rc in self.group[1:]])
        xr = self.send(own, 1, 0)
        yr = self.send(own, 0, 2)
        d0 = self.send(xr[:h], 0, 2)
        d1 = self.send(yr[h:], 1, 0)
        arrays = [own, xr, yr, d0, d1]
        arrays += [self.send(a, 0, 1) for a in arrays]
        return arrays

    def gather_rels(self):
        h = self.half
        places = []
        for core in (0, 1):
            places += [self.rels("o", core), self.rels("x", core), self.rels("y", core)]
            places += [self.rels("d", core)[:h], self.rels("d", core)[h:]]
        return places

    def reduce_rels(self):
        far = [self.rels("d", 1), sum([self.rels(k, 1) for k in "xyo"], [])]
        return far + [sum([self.rels(k, 0) for k in "dxyo"], [])]

    def reduce(self, far_d, far_xyo, keep):
        g, h = self.g, self.half

        def total(*terms):
            return sum(t.astype(f32) for t in terms).astype(bf16)

        got_d = self.send(far_d, 0, 1)
        got = self.send(far_xyo, 0, 1)
        b0 = self.send(total(keep[:h], got_d[:h]), 1, 0)
        b1 = self.send(total(keep[h:g], got_d[h:]), 0, 2)
        x0 = self.send(total(keep[g : g + h], got[:h]), 1, 0)
        y1 = self.send(total(keep[2 * g + h : 3 * g], got[g + h : 2 * g]), 0, 2)
        x1 = self.send(total(keep[g + h : 2 * g], got[h:g], b1), 1, 0)
        y0 = self.send(total(keep[2 * g : 2 * g + h], got[g : g + h], b0), 0, 2)
        terms = []
        for i, (rr, rc) in enumerate(self.group):
            xi, yi = (x0[i], y0[i]) if i < h else (x1[i - h], y1[i - h])
            parts = (keep[3 * g + i], got[2 * g + i], xi, yi)
            if i == 0:
                terms.append(sum(t.astype(f32) for t in parts))
            else:
                terms.append(self.send(total(*parts), rr, rc).astype(f32))
        return sum(terms)

    def sum_all(self, v):
        v = v + self.send(v, 0, 1)
        v = (v + self.send(v, 1, 0)) + (self.send(v, 0, 2) + self.send(v, 1, 2))
        terms = [v] + [self.send(v, rr, rc) for rr, rc in self.group[1:]]
        while len(terms) > 1:
            terms = [a + b for a, b in zip(terms[::2], terms[1::2])]
        return terms[0]


def dot(a, b, ca=1, cb=0):
    return lax.dot_general(a, b, (((ca,), (cb,)), ((), ())), preferred_element_type=f32)


def norm_parts(x):
    mean = jnp.mean(x, axis=-1, keepdims=True)
    centered = x - mean
    scale = lax.rsqrt(jnp.mean(centered * centered, axis=-1, keepdims=True) + norm_eps)
    return centered * scale, scale


def norm_back(x, gain, grad):
    unit, scale = norm_parts(x)
    gain_grad = jnp.sum(grad * unit, axis=0, keepdims=True)
    shift_grad = jnp.sum(grad, axis=0, keepdims=True)
    g = grad * gain
    moved = g - jnp.mean(g, axis=-1, keepdims=True) - unit * jnp.mean(g * unit, axis=-1, keepdims=True)
    return moved * scale, gain_grad, shift_grad


class Load:
    def __init__(self, me, refs, places, w, sems, u):
        self.w, self.sems = w, sems
        for ref, rels in zip(refs, places):
            for i, (rr, rc) in enumerate(rels):
                row = pl.multiple_of((me[0] ^ rr) * u, u)
                pltpu.make_async_copy(ref.at[i], w.at[rc, pl.ds(row, u)], sems.at[rc]).start()

    def wait(self, rc):
        pltpu.make_async_copy(self.w.at[rc], self.w.at[rc], self.sems.at[rc]).wait()


class Store:
    def __init__(self, me, refs, places, w, sems, u):
        self.me, self.w, self.sems, self.u = me, w, sems, u
        self.jobs = [(ref, i, rr, rc) for ref, rels in zip(refs, places) for i, (rr, rc) in enumerate(rels)]

    def start(self, now):
        for ref, i, rr, rc in self.jobs:
            if rc == now:
                row = pl.multiple_of((self.me[0] ^ rr) * self.u, self.u)
                pltpu.make_async_copy(self.w.at[rc, pl.ds(row, self.u)], ref.at[i], self.sems.at[rc]).start()

    def wait(self, rc):
        pltpu.make_async_copy(self.w.at[rc], self.w.at[rc], self.sems.at[rc]).wait()


class Sizes:
    def __init__(self, net, tok, d, ff):
        self.net, self.tok, self.d, self.ff = net, tok, d, ff
        self.R, self.C = net.rows, net.cols
        self.u = d // self.R
        self.qc, self.oc, self.fc = 3 * d // self.C, d // self.C, ff // self.C
        self.an, self.fn = self.qc + self.oc, 2 * self.fc
        self.heads = d // HEAD_DIM
        self.get, self.put = net.gather_rels(), net.reduce_rels()


def attend_in(s, layer, n, me, x, vec, qb, cos, sin, seg_row, seg_col, *refs):
    pieces, refs = refs[:n], refs[n:]
    mid, ffn, qkv_t, ctx_t, lse, w, proj_t, mask, sems = refs
    load = Load(me, pieces, s.get, w, sems, s.u)
    mask[...] = jnp.where(seg_col[...] == seg_row[...], 0.0, -1e30)
    hidden = x[...].astype(f32)
    unit, _ = norm_parts(hidden)
    normed = (unit * vec[layer, 0:1] + vec[layer, 1:2]).astype(bf16)
    for rc in range(s.C):
        load.wait(rc)
        c = me[1] ^ rc
        part = dot(normed, w[rc, :, : s.qc]) + qb[layer, c]
        proj_t[pl.ds(pl.multiple_of(c * s.qc, 8), s.qc), :] = part.T
    cosine, sine = cos[...], sin[...]
    hh = HEAD_DIM // 2
    scaling = HEAD_DIM ** (-0.5)
    for h in range(2 * s.heads):
        a = h * HEAD_DIM
        u1, u2 = proj_t[a : a + hh, :], proj_t[a + hh : a + 2 * hh, :]
        r1, r2 = u1 * cosine - u2 * sine, u2 * cosine + u1 * sine
        if h < s.heads:
            r1, r2 = r1 * scaling, r2 * scaling
        qkv_t[a : a + HEAD_DIM, :] = jnp.concatenate([r1, r2], axis=0).astype(bf16)
    qkv_t[2 * s.d :, :] = proj_t[2 * s.d :, :].astype(bf16)

    def heads(step, carry):
        for k in range(HEADS_A_STEP):
            h = step * HEADS_A_STEP + k
            at = pl.multiple_of(h * HEAD_DIM, HEAD_DIM)
            q = qkv_t[pl.ds(at, HEAD_DIM), :]
            key = qkv_t[pl.ds(s.d + at, HEAD_DIM), :]
            val = qkv_t[pl.ds(2 * s.d + at, HEAD_DIM), :]
            scores = dot(key, q, 0, 0) + mask[...]
            peak = jnp.max(scores, axis=0, keepdims=True)
            e = jnp.exp(scores - peak)
            total = jnp.sum(e, axis=0, keepdims=True)
            out = dot(val, e.astype(bf16)) * (1.0 / total)
            ctx_t[pl.ds(at, HEAD_DIM), :] = out.astype(bf16)
            lse[h] = peak + jnp.log(total)
        return carry

    lax.fori_loop(0, s.heads // HEADS_A_STEP, heads, 0)
    att_t = jnp.zeros((s.d, s.tok), f32)
    for rc in range(s.C):
        c = me[1] ^ rc
        att_t += dot(w[rc, :, s.qc :], ctx_t[pl.ds(pl.multiple_of(c * s.oc, 8), s.oc), :])
    middle = hidden + att_t.T + vec[layer, 5:6]
    mid[...] = middle
    unit, _ = norm_parts(middle)
    ffn[...] = (unit * vec[layer, 6:7] + vec[layer, 7:8]).astype(bf16)


def gelu_parts(pre):
    phi = 0.5 * (1.0 + lax.erf(pre * SQRT_HALF))
    return pre * phi, phi + pre * (INV_SQRT_2PI * jnp.exp(-0.5 * pre * pre))


def ffn_forward(s, layer, n, me, mid, ffn, vec, hb, *refs):
    pieces, refs = refs[:n], refs[n:]
    out, act, slope, w, sems = refs
    load = Load(me, pieces, s.get, w, sems, s.u)
    total = mid[...] + vec[layer, 12:13]
    for rc in range(s.C):
        load.wait(rc)
        pre = dot(ffn[...], w[rc, :, : s.fc]) + hb[layer, me[1] ^ rc]
        value, back = gelu_parts(pre)
        value = value.astype(bf16)
        act[rc], slope[rc] = value, back
        total += dot(value, w[rc, :, s.fc :], 1, 1)
    out[...] = total


def ffn_backward(s, layer, n, with_forward, me, gx, mid, ffn, vec, hb, *refs):
    pieces, refs = refs[:n], refs[n:]
    if with_forward:
        out, refs = refs[0], refs[1:]
    else:
        act, slope, refs = refs[0], refs[1], refs[2:]
    g_mid, hid_grad, vec_grad, far_d, far_xyo, keep, w, dw, sems, out_sems = refs
    load = Load(me, pieces, s.get, w, sems, s.u)
    store = Store(me, (far_d, far_xyo, keep), s.put, dw, out_sems, s.u)
    g_in = gx[...].astype(f32)
    g = g_in.astype(bf16)
    g_t, ffn_t = g_in.T.astype(bf16), ffn[...].T
    total = mid[...] + vec[layer, 12:13] if with_forward else None
    g_ffn = jnp.zeros((s.tok, s.d), f32)
    for rc in range(s.C):
        load.wait(rc)
        up, down = w[rc, :, : s.fc], w[rc, :, s.fc :]
        if with_forward:
            value, back = gelu_parts(dot(ffn[...], up) + hb[layer, me[1] ^ rc])
            value = value.astype(bf16)
            total += dot(value, down, 1, 1)
        else:
            value, back = act[rc], slope[rc]
        g_pre = (dot(g, down) * back).astype(bf16)
        hid_grad[me[1] ^ rc] = jnp.sum(g_pre.astype(f32), axis=0, keepdims=True)
        dw[rc, :, : s.fc] = dot(ffn_t, g_pre).astype(bf16)
        dw[rc, :, s.fc :] = dot(g_t, value).astype(bf16)
        store.start(rc)
        g_ffn += dot(g_pre, up, 1, 1)
    if with_forward:
        out[...] = total
    moved, gain_grad, shift_grad = norm_back(mid[...], vec[layer, 6:7], g_ffn)
    middle_grad = g_in + moved
    g_mid[...] = middle_grad
    vec_grad[0:1] = jnp.sum(g.astype(f32), axis=0, keepdims=True)
    vec_grad[1:2] = gain_grad
    vec_grad[2:3] = shift_grad
    vec_grad[3:4] = jnp.sum(middle_grad.astype(bf16).astype(f32), axis=0, keepdims=True)
    vec_grad[4:8] = jnp.zeros((4, s.d), f32)
    for rc in range(s.C):
        store.wait(rc)


def attend_back(s, layer, n, me, g_mid, x, vec, cos, sin, seg_row, seg_col, qkv_t, ctx_t, lse, *refs):
    pieces, refs = refs[:n], refs[n:]
    g_in, qkv_grad, vec_grad, far_d, far_xyo, keep, w, dw, gp_t, gctx_t, graw, mask, sems, out_sems = refs
    load = Load(me, pieces, s.get, w, sems, s.u)
    store = Store(me, (far_d, far_xyo, keep), s.put, dw, out_sems, s.u)
    mask[...] = jnp.where(seg_col[...] == seg_row[...], 0.0, -1e30)
    hidden = x[...].astype(f32)
    unit, _ = norm_parts(hidden)
    normed_t = (unit * vec[layer, 0:1] + vec[layer, 1:2]).T.astype(bf16)
    g_att = g_mid[...].astype(bf16)
    g_att_t = g_mid[...].T.astype(bf16)
    for rc in range(s.C):
        load.wait(rc)
        at = pl.multiple_of((me[1] ^ rc) * s.oc, 8)
        dw[rc, :, s.qc :] = dot(g_att_t, ctx_t[pl.ds(at, s.oc), :], 1, 1).astype(bf16)
        gctx_t[pl.ds(at, s.oc), :] = dot(g_att, w[rc, :, s.qc :]).T.astype(bf16)

    def heads(step, carry):
        for k in range(HEADS_A_STEP):
            h = step * HEADS_A_STEP + k
            at = pl.multiple_of(h * HEAD_DIM, HEAD_DIM)
            q = qkv_t[pl.ds(at, HEAD_DIM), :]
            key = qkv_t[pl.ds(s.d + at, HEAD_DIM), :]
            val = qkv_t[pl.ds(2 * s.d + at, HEAD_DIM), :]
            gc = gctx_t[pl.ds(at, HEAD_DIM), :]
            p = jnp.exp(dot(key, q, 0, 0) + mask[...] - lse[h])
            g_p = dot(val, gc, 0, 0)
            inner = jnp.sum(g_p * p, axis=0, keepdims=True)
            g_s = (p * (g_p - inner)).astype(bf16)
            graw[pl.ds(at, HEAD_DIM), :] = dot(key, g_s)
            graw[pl.ds(s.d + at, HEAD_DIM), :] = dot(q, g_s, 1, 1)
            gp_t[pl.ds(2 * s.d + at, HEAD_DIM), :] = dot(gc, p.astype(bf16), 1, 1).astype(bf16)
        return carry

    lax.fori_loop(0, s.heads // HEADS_A_STEP, heads, 0)
    cosine, sine = cos[...], sin[...]
    hh = HEAD_DIM // 2
    scaling = HEAD_DIM ** (-0.5)
    for h in range(2 * s.heads):
        a = h * HEAD_DIM
        u1, u2 = graw[a : a + hh, :], graw[a + hh : a + 2 * hh, :]
        if h < s.heads:
            u1, u2 = u1 * scaling, u2 * scaling
        both = jnp.concatenate([u1 * cosine + u2 * sine, u2 * cosine - u1 * sine], axis=0)
        gp_t[a : a + HEAD_DIM, :] = both.astype(bf16)
    g_normed_t = jnp.zeros((s.d, s.tok), f32)
    ones = jnp.ones((8, s.tok), bf16)
    for rc in range(s.C):
        c = me[1] ^ rc
        part = gp_t[pl.ds(pl.multiple_of(c * s.qc, 8), s.qc), :]
        dw[rc, :, : s.qc] = dot(normed_t, part, 1, 1).astype(bf16)
        store.start(rc)
        qkv_grad[c] = dot(ones, part, 1, 1)[0:1]
        g_normed_t += dot(w[rc, :, : s.qc], part)
    moved, gain_grad, shift_grad = norm_back(hidden, vec[layer, 0:1], g_normed_t.T)
    g_in[...] = g_mid[...] + moved
    vec_grad[0:1] = gain_grad
    vec_grad[1:2] = shift_grad
    vec_grad[2:8] = jnp.zeros((6, s.d), f32)
    for rc in range(s.C):
        store.wait(rc)


def shape(dims, dtype=f32):
    return jax.ShapeDtypeStruct(tuple(dims), dtype)


def call(kernel, kinds, args, outs, scratch, flops, moved):
    space = {"s": pltpu.SMEM, "v": VMEM, "a": ANY}
    return pl.pallas_call(
        kernel,
        in_specs=[pl.BlockSpec(memory_space=space[k]) for k in kinds],
        out_specs=[pl.BlockSpec(memory_space=space[k]) for k, _ in outs],
        out_shape=[o for _, o in outs],
        scratch_shapes=scratch,
        compiler_params=pltpu.CompilerParams(vmem_limit_bytes=44 * 2**20),
        cost_estimate=pl.CostEstimate(flops=flops, bytes_accessed=moved, transcendentals=0),
    )(*args)


def prepare(s, layer, qkv, out, up, down):
    def kernel(q, o, p, d, a_ref, f_ref):
        a_ref[:, : s.qc] = q[0].astype(bf16)
        a_ref[:, s.qc :] = o[0].T.astype(bf16)
        f_ref[:, : s.fc] = p[0].astype(bf16)
        f_ref[:, s.fc :] = d[0].T.astype(bf16)

    def one(a):
        return pl.BlockSpec((1,) + a.shape[1:], lambda i: (layer, 0, 0))

    def whole(n):
        return pl.BlockSpec((s.u, n), lambda i: (0, 0))

    return pl.pallas_call(
        kernel,
        grid=(1,),
        in_specs=[one(qkv), one(out), one(up), one(down)],
        out_specs=[whole(s.an), whole(s.fn)],
        out_shape=[shape((s.u, s.an), bf16), shape((s.u, s.fn), bf16)],
        compiler_params=pltpu.CompilerParams(vmem_limit_bytes=16 * 2**20),
        cost_estimate=pl.CostEstimate(flops=10**6, bytes_accessed=2 * 10**6, transcendentals=0),
    )(qkv, out, up, down)


def adamw(weight, gradient, first, second, rate, step_count):
    first_new = beta_one * first + (1.0 - beta_one) * gradient
    second_new = beta_two * second + (1.0 - beta_two) * gradient * gradient
    first_hat = first_new / (1.0 - beta_one**step_count)
    second_hat = second_new / (1.0 - beta_two**step_count)
    weight_new = weight - rate * (first_hat / (jnp.sqrt(second_hat) + adam_eps) + decay_rate * weight)
    return (weight_new, first_new, second_new)


def update(layer, gradient, split, states, rates, before):
    def kernel(g, *refs):
        ins, outs = refs[:6], refs[-6:]
        for k in range(2):
            grad = g[:, :split] if k == 0 else g[:, split:].T
            w, m, v = (r[0] for r in ins[3 * k : 3 * k + 3])
            for ref, new in zip(outs[3 * k : 3 * k + 3], adamw(w, grad, m, v, rates[k], float(STEP))):
                ref[0] = new

    def one(a):
        return pl.BlockSpec((1,) + a.shape[1:], lambda i: (layer, 0, 0))

    more = [] if before is None else list(before)
    return pl.pallas_call(
        kernel,
        grid=(1,),
        in_specs=[pl.BlockSpec(gradient.shape, lambda i: (0, 0))]
        + [one(a) for a in states]
        + [pl.BlockSpec(memory_space=ANY)] * len(more),
        out_specs=[one(a) for a in states],
        out_shape=[shape(a.shape) for a in states],
        input_output_aliases={7 + i: i for i in range(len(more))},
        compiler_params=pltpu.CompilerParams(vmem_limit_bytes=24 * 2**20),
        cost_estimate=pl.CostEstimate(flops=10**7, bytes_accessed=4 * 10**6, transcendentals=0),
    )(gradient, *states, *more)


def rotary_tables(segment_ids):
    seg = segment_ids[0]
    start = jnp.sum((seg[:, None] < seg[None, :]).astype(jnp.int32), axis=0)
    places = jnp.arange(seg.shape[0], dtype=jnp.int32) - start
    freq_index = jnp.arange(HEAD_DIM // 2, dtype=f32)
    inverse = jnp.exp(freq_index * (-2.0 * math.log(10000.0) / HEAD_DIM))
    angles = inverse[:, None] * places.astype(f32)[None, :]
    return jnp.cos(angles), jnp.sin(angles)


def shards(
    rows,
    cols,
    residues,
    segment_ids,
    cotangent,
    qkv_weight,
    qkv_first,
    qkv_second,
    out_weight,
    out_first,
    out_second,
    up_weight,
    up_first,
    up_second,
    down_weight,
    down_first,
    down_second,
    vectors,
    vector_first,
    vector_second,
):
    net = Net(rows, cols)
    tok, d = residues.shape
    s = Sizes(net, tok, d, up_weight.shape[2] * cols)
    me = jnp.stack([lax.axis_index("rows"), lax.axis_index("cols")]).astype(jnp.int32)
    units = [prepare(s, l, qkv_weight, out_weight, up_weight, down_weight) for l in range(LAYERS)]
    full = []
    for l in range(LAYERS):
        full.append((net.gather(units[l][0]), net.gather(units[l][1])))
    n = len(s.get)
    cos, sin = rotary_tables(segment_ids)
    seg_row, seg_col = segment_ids, segment_ids.reshape(tok, 1)
    qb = vectors[:, 2:5].reshape(LAYERS, cols, 1, s.qc)
    hb = vectors[:, 8:12].reshape(LAYERS, cols, 1, s.fc)
    act = (tok, d)
    g = net.g
    n_a, n_f = 4 * d * d, 2 * d * s.ff
    attn_flops = 4 * tok * tok * HEAD_DIM * s.heads * 8
    sem = pltpu.SemaphoreType.DMA((cols,))

    def grads(width):
        return [("a", shape((k * g, s.u, width), bf16)) for k in (1, 3, 4)]

    hidden = residues
    saved = []
    for l in range(LAYERS):
        a_full, f_full = full[l]
        mid, ffn, qkv_t, ctx_t, lse = call(
            functools.partial(attend_in, s, l, n),
            "s" + "v" * 7 + "a" * n,
            (me, hidden, vectors, qb, cos, sin, seg_row, seg_col, *a_full),
            [
                ("v", shape(act)),
                ("v", shape(act, bf16)),
                ("v", shape((3 * d, tok), bf16)),
                ("v", shape((d, tok), bf16)),
                ("v", shape((s.heads, 1, tok))),
            ],
            [VMEM((cols, d, s.an), bf16), VMEM((3 * d, tok), f32), VMEM((tok, tok), f32), sem],
            2 * tok * n_a + attn_flops,
            2 * n_a + 5 * 10**6,
        )
        last = l == LAYERS - 1
        kept = [hidden, mid, ffn, qkv_t, ctx_t, lse]
        if not last:
            hidden, value, slope = call(
                functools.partial(ffn_forward, s, l, n),
                "s" + "v" * 4 + "a" * n,
                (me, mid, ffn, vectors, hb, *f_full),
                [("v", shape(act)), ("v", shape((cols, tok, s.fc), bf16)), ("v", shape((cols, tok, s.fc)))],
                [VMEM((cols, d, s.fn), bf16), sem],
                2 * tok * n_f,
                2 * n_f + 5 * 10**6,
            )
            kept += [value, slope]
        saved.append(kept)

    gx = cotangent
    block_out = None
    new_a, new_f, vec_rows = None, None, [None] * LAYERS
    a_states = (qkv_weight, qkv_first, qkv_second, out_weight, out_first, out_second)
    f_states = (up_weight, up_first, up_second, down_weight, down_first, down_second)
    rate_qkv = 0.5 / math.sqrt(d)
    rate_out = 0.5 / math.sqrt(max(d * 4 // TOK_DEV, 1))
    rate_down = 0.5 / math.sqrt(s.ff)
    for l in reversed(range(LAYERS)):
        a_full, f_full = full[l]
        hidden_in, mid, ffn, qkv_t, ctx_t, lse, *kept = saved[l]
        last = l == LAYERS - 1
        res = call(
            functools.partial(ffn_backward, s, l, n, last),
            "s" + "v" * 5 + "a" * n + ("" if last else "vv"),
            (me, gx, mid, ffn, vectors, hb, *f_full, *kept),
            ([("v", shape(act))] if last else [])
            + [("v", shape(act)), ("v", shape((cols, 1, s.fc))), ("v", shape((8, d)))]
            + grads(s.fn),
            [VMEM((cols, d, s.fn), bf16), VMEM((cols, d, s.fn), bf16), sem, sem],
            (6 if last else 4) * tok * n_f,
            4 * n_f + 5 * 10**6,
        )
        if last:
            block_out, res = res[0], res[1:]
        g_mid, hid_grad, vec_f, *parts = res
        new_f = update(l, net.reduce(*parts), s.fc, f_states, (rate_qkv, rate_down), new_f)
        gx, qkv_grad, vec_a, *parts = call(
            functools.partial(attend_back, s, l, n),
            "s" + "v" * 10 + "a" * n,
            (me, g_mid, hidden_in, vectors, cos, sin, seg_row, seg_col, qkv_t, ctx_t, lse, *a_full),
            [("v", shape(act)), ("v", shape((cols, 1, s.qc))), ("v", shape((8, d)))] + grads(s.an),
            [
                VMEM((cols, d, s.an), bf16),
                VMEM((cols, d, s.an), bf16),
                VMEM((3 * d, tok), bf16),
                VMEM((d, tok), bf16),
                VMEM((2 * d, tok), f32),
                VMEM((tok, tok), f32),
                sem,
                sem,
            ],
            4 * tok * n_a + 3 * attn_flops,
            4 * n_a + 5 * 10**6,
        )
        new_a = update(l, net.reduce(*parts), s.qc, a_states, (rate_qkv, rate_out), new_a)
        vec_rows[l] = net.sum_all(
            jnp.concatenate(
                [
                    vec_a[0:2],
                    qkv_grad.reshape(3, d),
                    vec_f[3:4],
                    vec_f[1:3],
                    hid_grad.reshape(4, d),
                    vec_f[0:1],
                ]
            )
        )
    vec_new = adamw(vectors, jnp.stack(vec_rows), vector_first, vector_second, 0.1, float(STEP))
    return (block_out, gx, *new_a, *new_f, *vec_new)


def solution(mesh):
    rows, cols = mesh.shape["rows"], mesh.shape["cols"]
    tokens = P(("rows", "cols"), None)
    wide, tall = P(None, "rows", "cols"), P(None, "cols", "rows")
    states = (wide,) * 3 + (tall,) * 3 + (wide,) * 3 + (tall,) * 3
    return jax.shard_map(
        functools.partial(shards, rows, cols),
        mesh=mesh,
        in_specs=(tokens, tokens, tokens) + states + (P(),) * 3,
        out_specs=(tokens, tokens) + states + (P(),) * 3,
        check_vma=False,
    )
```

```python
import functools
import math

import jax
import jax.numpy as jnp
from jax import lax
from jax.experimental import pallas as pl
from jax.experimental.pallas import tpu as pltpu
from jax.sharding import PartitionSpec as P

HEAD_DIM = 32
LAYERS = 2
STEP = 5
TOK_DEV = 256

norm_eps = 1e-05
beta_one = 0.5
beta_two = 0.55
adam_eps = 1e-08
decay_rate = 0.01

f32 = jnp.float32
bf16 = jnp.bfloat16
VMEM = pltpu.VMEM
HBM = pltpu.HBM
SQRT_HALF = math.sqrt(0.5)
INV_SQRT_2PI = 1.0 / math.sqrt(2.0 * math.pi)
HEADS_A_STEP = 4
LONG, LONGER = 2 * 10**10, 10**12


class Clock:
    def __init__(self):
        self.before = []

    def wait(self, *xs):
        self.before += list(xs)
        return list(xs)

    def call(self, kernel, args, in_specs, outs, out_specs, scratch=(), aliases=None, flops=10**6, vmem=60):
        known = {id(x) for x in args}
        more = [x for x in self.before if id(x) not in known]
        n, extra = len(args), len(more)

        def body(*refs):
            kernel(*refs[:n], *refs[n + extra :])

        results = pl.pallas_call(
            body,
            in_specs=list(in_specs) + [pl.BlockSpec(memory_space=pl.ANY)] * extra,
            out_specs=list(out_specs),
            out_shape=list(outs),
            scratch_shapes=list(scratch),
            input_output_aliases=aliases or {},
            compiler_params=pltpu.CompilerParams(vmem_limit_bytes=vmem * 2**20),
            cost_estimate=pl.CostEstimate(flops=flops, bytes_accessed=10**5, transcendentals=0),
        )(*args, *more)
        self.before = [results[0]]
        return results

    def combine(self, arrays, outs, dtype=bf16, long=None, vmem=16):
        wanted = [sorted({j for o in outs for terms in o for a, j in terms if a == i}) for i in range(len(arrays))]
        runs = []
        for i, js in enumerate(wanted):
            for at, j in enumerate(js):
                if at and js[at - 1] == j - 1:
                    runs[-1][3] += 1
                else:
                    runs.append([i, j, at, 1])
        unit = arrays[0].shape[1:]

        def kernel(*refs):
            ins, out_refs = refs[: len(arrays)], refs[len(arrays) : len(arrays) + len(outs)]
            bufs, sems = refs[-1 - len(arrays) : -1], refs[-1]
            copies = [
                pltpu.make_async_copy(ins[i].at[pl.ds(j, k)], bufs[i].at[pl.ds(at, k)], sems.at[r])
                for r, (i, j, at, k) in enumerate(runs)
            ]
            for c in copies:
                c.start()
            for c in copies:
                c.wait()
            for ref, units in zip(out_refs, outs):
                for to, terms in enumerate(units):
                    values = [bufs[i][wanted[i].index(j)] for i, j in terms]
                    if len(values) > 1:
                        values = [sum(v.astype(f32) for v in values)]
                    ref[to] = values[0].astype(dtype)

        return self.call(
            kernel,
            arrays,
            [pl.BlockSpec(memory_space=pl.ANY)] * len(arrays),
            [shape((len(o),) + unit, dtype) for o in outs],
            [pl.BlockSpec(memory_space=VMEM)] * len(outs),
            [VMEM((len(js),) + unit, a.dtype) for js, a in zip(wanted, arrays)] + [pltpu.SemaphoreType.DMA((len(runs),))],
            flops=long or 10**6,
            vmem=vmem,
        )


class Net:
    def __init__(self, rows, cols):
        self.rows, self.cols = rows, cols
        bits = [(0, 1 << k) for k in range(2, cols.bit_length() - 1)] + [(1 << k, 0) for k in range(1, rows.bit_length() - 1)]
        self.steps = bits[::-1]
        self.group = [(0, 0)]
        for rr, rc in self.steps:
            self.group += [(r ^ rr, c ^ rc) for r, c in self.group]
        self.g = len(self.group)
        self.half = self.g // 2

    def send(self, x, rr, rc):
        mask = rr * self.cols + rc
        pairs = [(i, i ^ mask) for i in range(self.rows * self.cols)]
        return lax.ppermute(x, ("rows", "cols"), pairs)

    def rels(self, kind, core):
        dr, dc = {"o": (0, 0), "x": (1, 0), "y": (0, 2), "d": (1, 2)}[kind]
        return [(rr ^ dr, rc ^ dc ^ core) for rr, rc in self.group]

    def gather(self, clock, x, slow=LONG):
        g, h = self.g, self.half
        for rr, rc in self.steps:
            got = self.send(x, rr, rc)
            yield
            clock.wait(got)
            k = x.shape[0]
            (x,) = clock.combine([x, got], [[[(0, i)] for i in range(k)] + [[(1, i)] for i in range(k)]], long=slow)
        own = x
        xr, yr = self.send(own, 1, 0), self.send(own, 0, 2)
        yield
        clock.wait(xr, yr)
        xh, yh = clock.combine([xr, yr], [[[(0, i)] for i in range(h)], [[(1, i)] for i in range(h, g)]], long=slow)
        d0, d1 = self.send(xh, 0, 2), self.send(yh, 1, 0)
        (near,) = clock.combine([own, xr, yr], [[[(a, i)] for a in range(3) for i in range(g)]])
        far = self.send(near, 0, 1)
        yield
        clock.wait(d0, d1)
        rest = [self.send(d0, 0, 1), self.send(d1, 0, 1)]
        yield
        clock.wait(far, *rest)
        yield [near, d0, d1, far, *rest]

    def gather_rels(self):
        h = self.half
        places = []
        for core in (0, 1):
            o, x, y, d = (self.rels(k, core) for k in "oxyd")
            places += [o + x + y, d[:h], d[h:]]
        return places

    def reduce_rels(self):
        return [sum([self.rels(k, core) for k in "dxyo"], []) for core in (1, 0)]

    def reduce(self, clock, far, keep, fast=False, slow=None):
        g, h = self.g, self.half
        got = self.send(far, 0, 1)
        yield
        clock.wait(got)

        def both(at, n):
            return [[(0, i), (1, i)] for i in range(at, at + n)]

        to_x, to_y = clock.combine([keep, got], [both(0, h) + both(g, h), both(h, h) + both(2 * g + h, h)], vmem=60)
        from_x, from_y = self.send(to_x, 1, 0), self.send(to_y, 0, 2)
        yield
        clock.wait(from_x, from_y)
        x1, y0 = clock.combine(
            [keep, got, from_x, from_y],
            [
                [[(0, g + h + i), (1, g + h + i), (3, i)] for i in range(h)],
                [[(0, 2 * g + i), (1, 2 * g + i), (2, i)] for i in range(h)],
            ],
            long=LONGER if slow == 2 else None,
            vmem=60,
        )
        x1, y0 = self.send(x1, 1, 0), self.send(y0, 0, 2)
        yield
        clock.wait(x1, y0)
        held = [keep, got, from_x, from_y, x1, y0]

        def parts(i):
            near = [(2, h + i), (5, i)] if i < h else [(4, i - h), (3, i)]
            return [(0, 3 * g + i), (1, 3 * g + i)] + near

        if fast:
            sent = clock.combine(held, [[parts(i)] for i in range(1, g)])
            more = [self.send(t, rr, rc) for t, (rr, rc) in zip(sent, self.group[1:])]
            yield
            clock.wait(*more)
        else:
            n, more = g, []
            for rr, rc in reversed(self.steps):
                n //= 2
                units = [parts(i) + [(6 + m, i) for m in range(len(more))] for i in range(n, 2 * n)]
                (x,) = clock.combine(held + more, [units], long=LONGER if slow == 3 and not more else None, vmem=60)
                more.append(self.send(x, rr, rc))
                yield
                clock.wait(more[-1])
        yield held + more, parts(0) + [(6 + m, 0) for m in range(len(more))]

    def sum_all(self, clock, v):
        for rr, rc in [(0, 1), *self.steps, (1, 0), (0, 2)]:
            got = self.send(v, rr, rc)
            yield
            clock.wait(got)
            if (rr, rc) != (0, 2):
                (v,) = clock.combine([v, got], [[[(0, i), (1, i)] for i in range(v.shape[0])]], f32)
        yield v, got


def shape(dims, dtype=f32):
    return jax.ShapeDtypeStruct(tuple(dims), dtype)


def dot(a, b, ca=1, cb=0):
    return lax.dot_general(a, b, (((ca,), (cb,)), ((), ())), preferred_element_type=f32)


def norm_parts(x):
    mean = jnp.mean(x, axis=-1, keepdims=True)
    centered = x - mean
    scale = lax.rsqrt(jnp.mean(centered * centered, axis=-1, keepdims=True) + norm_eps)
    return centered * scale, scale


def norm_back(x, gain, grad):
    unit, scale = norm_parts(x)
    gain_grad = jnp.sum(grad * unit, axis=0, keepdims=True)
    shift_grad = jnp.sum(grad, axis=0, keepdims=True)
    g = grad * gain
    moved = g - jnp.mean(g, axis=-1, keepdims=True) - unit * jnp.mean(g * unit, axis=-1, keepdims=True)
    return moved * scale, gain_grad, shift_grad


class Load:
    def __init__(self, s, me, refs, places, w, sems):
        self.w, self.sems = w, sems
        if places is None:
            for r in range(s.R):
                for c in range(s.C):
                    rc = me[1] ^ c
                    part = refs[0].at[r * s.C + c]
                    pltpu.make_async_copy(part, w.at[rc, :, pl.ds(r * s.u, s.u)], sems.at[rc]).start()
            return
        for ref, rels in zip(refs, places):
            for i, (rr, rc) in enumerate(rels):
                row = pl.multiple_of((me[0] ^ rr) * s.u, s.u)
                pltpu.make_async_copy(ref.at[i], w.at[rc, :, pl.ds(row, s.u)], sems.at[rc]).start()

    def wait(self, rc):
        pltpu.make_async_copy(self.w.at[rc], self.w.at[rc], self.sems.at[rc]).wait()


class Store:
    def __init__(self, s, me, refs, places, w, sems, first=0):
        self.first = first
        self.s, self.me, self.refs, self.places, self.w, self.sems = s, me, refs, places, w, sems

    def start(self, now):
        s, me = self.s, self.me
        if self.places is None:
            for r in range(s.R):
                to = self.refs[0].at[r * s.C + (me[1] ^ now)]
                pltpu.make_async_copy(self.w.at[now, :, pl.ds(r * s.u, s.u)], to, self.sems.at[now]).start()
            return
        for ref, rels in zip(self.refs, self.places):
            for i, (rr, rc) in enumerate(rels):
                if rc == now:
                    row = pl.multiple_of((me[0] ^ rr) * s.u, s.u)
                    to = ref.at[i, pl.ds(self.first, self.w.shape[1])]
                    pltpu.make_async_copy(self.w.at[rc, :, pl.ds(row, s.u)], to, self.sems.at[rc]).start()

    def wait(self, rc):
        pltpu.make_async_copy(self.w.at[rc], self.w.at[rc], self.sems.at[rc]).wait()


class Sizes:
    def __init__(self, net, tok, d, ff):
        self.net, self.tok, self.d, self.ff = net, tok, d, ff
        self.R, self.C = net.rows, net.cols
        self.u = d // self.R
        self.qc, self.oc, self.fc = 3 * d // self.C, d // self.C, ff // self.C
        self.an = self.qc + self.oc
        self.heads = d // HEAD_DIM


def attend_in(s, layer, places, n, me, x, vec, qb, cos, sin, mask, *refs):
    pieces, refs = refs[:n], refs[n:]
    mid, ffn, qkv_t, ctx_t, lse, w, proj_t, sems = refs
    load = Load(s, me, pieces, places, w, sems)
    hidden = x[...].astype(f32)
    unit, _ = norm_parts(hidden)
    normed = (unit * vec[layer, 0:1] + vec[layer, 1:2]).astype(bf16)
    for rc in range(s.C):
        load.wait(rc)
        c = me[1] ^ rc
        part = dot(normed, w[rc, 0, :, : s.qc]) + qb[layer, c]
        proj_t[pl.ds(pl.multiple_of(c * s.qc, 8), s.qc), :] = part.T
    cosine, sine = cos[...], sin[...]
    hh = HEAD_DIM // 2
    scaling = HEAD_DIM ** (-0.5)
    for h in range(2 * s.heads):
        a = h * HEAD_DIM
        u1, u2 = proj_t[a : a + hh, :], proj_t[a + hh : a + 2 * hh, :]
        r1, r2 = u1 * cosine - u2 * sine, u2 * cosine + u1 * sine
        if h < s.heads:
            r1, r2 = r1 * scaling, r2 * scaling
        qkv_t[a : a + HEAD_DIM, :] = jnp.concatenate([r1, r2], axis=0).astype(bf16)
    qkv_t[2 * s.d :, :] = proj_t[2 * s.d :, :].astype(bf16)

    def heads(step, carry):
        for k in range(HEADS_A_STEP):
            h = step * HEADS_A_STEP + k
            at = pl.multiple_of(h * HEAD_DIM, HEAD_DIM)
            q = qkv_t[pl.ds(at, HEAD_DIM), :]
            key = qkv_t[pl.ds(s.d + at, HEAD_DIM), :]
            val = qkv_t[pl.ds(2 * s.d + at, HEAD_DIM), :]
            scores = dot(key, q, 0, 0) + mask[...]
            peak = jnp.max(scores, axis=0, keepdims=True)
            e = jnp.exp(scores - peak)
            total = jnp.sum(e, axis=0, keepdims=True)
            out = dot(val, e.astype(bf16)) * (1.0 / total)
            ctx_t[pl.ds(at, HEAD_DIM), :] = out.astype(bf16)
            lse[h] = peak + jnp.log(total)
        return carry

    lax.fori_loop(0, s.heads // HEADS_A_STEP, heads, 0)
    att_t = jnp.zeros((s.d, s.tok), f32)
    for rc in range(s.C):
        c = me[1] ^ rc
        att_t += dot(w[rc, 0, :, s.qc :], ctx_t[pl.ds(pl.multiple_of(c * s.oc, 8), s.oc), :])
    middle = hidden + att_t.T + vec[layer, 5:6]
    mid[...] = middle
    unit, _ = norm_parts(middle)
    ffn[...] = (unit * vec[layer, 6:7] + vec[layer, 7:8]).astype(bf16)


def put_row(ref, at, row):
    n = row.shape[1]
    if n % 128:
        row = jnp.concatenate([row, jnp.zeros((1, -n % 128), f32)], axis=1)
    ref[at, :, : row.shape[1]] = row


def copy_sums(old, new):
    if len(old.shape) == 4:
        new[...] = old[...]
    else:
        new[...] = jnp.zeros(new.shape, f32)


def gelu_parts(pre):
    phi = 0.5 * (1.0 + lax.erf(pre * SQRT_HALF))
    return pre * phi, phi + pre * (INV_SQRT_2PI * jnp.exp(-0.5 * pre * pre))


def ffn_forward(s, layer, places, n, me, mid, ffn, vec, hb, *refs):
    pieces, refs = refs[:n], refs[n:]
    out, act, slope, w, sems = refs
    load = Load(s, me, pieces, places, w, sems)
    total = mid[...] + vec[layer, 12:13]
    for rc in range(s.C):
        load.wait(rc)
        pre = dot(ffn[...], w[rc, 0]) + hb[layer, me[1] ^ rc]
        value, back = gelu_parts(pre)
        value = value.astype(bf16)
        act[rc], slope[rc] = value, back
        total += dot(value, w[rc, 1], 1, 1)
    out[...] = total


def ffn_backward(s, layer, places, puts, n, with_forward, me, gx, mid, ffn, vec, hb, sums, *refs):
    pieces, refs = refs[:n], refs[n:]
    if with_forward:
        out, refs = refs[0], refs[1:]
    else:
        act, slope, refs = refs[0], refs[1], refs[4:]
    g_mid, new_sums, *parts, w, dw, sems, out_sems = refs
    copy_sums(sums, new_sums)
    vec_grad = new_sums.at[2 * layer + 1]
    load = Load(s, me, pieces, places, w, sems)
    store = Store(s, me, parts, puts, dw, out_sems, 0 if with_forward else 1)
    g_in = gx[...].astype(f32)
    g = g_in.astype(bf16)
    g_t, ffn_t = g_in.T.astype(bf16), ffn[...].T
    total = mid[...] + vec[layer, 12:13] if with_forward else None
    g_ffn = jnp.zeros((s.tok, s.d), f32)
    for rc in range(s.C):
        load.wait(rc)
        up, down = w[rc, 0], w[rc, 1]
        if with_forward:
            value, back = gelu_parts(dot(ffn[...], up) + hb[layer, me[1] ^ rc])
            value = value.astype(bf16)
            total += dot(value, down, 1, 1)
        else:
            value, back = act[rc], slope[rc]
        g_pre = (dot(g, down) * back).astype(bf16)
        put_row(vec_grad, 8 + (me[1] ^ rc), jnp.sum(g_pre.astype(f32), axis=0, keepdims=True))
        dw[rc, 0] = dot(ffn_t, g_pre).astype(bf16)
        dw[rc, 1] = dot(g_t, value).astype(bf16)
        store.start(rc)
        g_ffn += dot(g_pre, up, 1, 1)
    if with_forward:
        out[...] = total
    moved, gain_grad, shift_grad = norm_back(mid[...], vec[layer, 6:7], g_ffn)
    middle_grad = g_in + moved
    g_mid[...] = middle_grad
    vec_grad[0] = jnp.sum(g.astype(f32), axis=0, keepdims=True)
    vec_grad[1] = gain_grad
    vec_grad[2] = shift_grad
    vec_grad[3] = jnp.sum(middle_grad.astype(bf16).astype(f32), axis=0, keepdims=True)
    for rc in range(s.C):
        store.wait(rc)


def attend_back(s, layer, places, puts, n, me, g_mid, x, vec, cos, sin, mask, qkv_t, ctx_t, lse, sums, *refs):
    pieces, refs = refs[:n], refs[n:]
    g_in, new_sums, *parts, w, dw, gp_t, gctx_t, graw, sems, out_sems = refs
    copy_sums(sums, new_sums)
    vec_grad = new_sums.at[2 * layer]
    load = Load(s, me, pieces, places, w, sems)
    store = Store(s, me, parts, puts, dw, out_sems)
    hidden = x[...].astype(f32)
    unit, _ = norm_parts(hidden)
    normed_t = (unit * vec[layer, 0:1] + vec[layer, 1:2]).T.astype(bf16)
    g_att = g_mid[...].astype(bf16)
    g_att_t = g_mid[...].T.astype(bf16)
    for rc in range(s.C):
        load.wait(rc)
        at = pl.multiple_of((me[1] ^ rc) * s.oc, 8)
        dw[rc, 0, :, s.qc :] = dot(g_att_t, ctx_t[pl.ds(at, s.oc), :], 1, 1).astype(bf16)
        gctx_t[pl.ds(at, s.oc), :] = dot(g_att, w[rc, 0, :, s.qc :]).T.astype(bf16)

    def heads(step, carry):
        for k in range(HEADS_A_STEP):
            h = step * HEADS_A_STEP + k
            at = pl.multiple_of(h * HEAD_DIM, HEAD_DIM)
            q = qkv_t[pl.ds(at, HEAD_DIM), :]
            key = qkv_t[pl.ds(s.d + at, HEAD_DIM), :]
            val = qkv_t[pl.ds(2 * s.d + at, HEAD_DIM), :]
            gc = gctx_t[pl.ds(at, HEAD_DIM), :]
            p = jnp.exp(dot(key, q, 0, 0) + mask[...] - lse[h])
            g_p = dot(val, gc, 0, 0)
            inner = jnp.sum(g_p * p, axis=0, keepdims=True)
            g_s = (p * (g_p - inner)).astype(bf16)
            graw[pl.ds(at, HEAD_DIM), :] = dot(key, g_s)
            graw[pl.ds(s.d + at, HEAD_DIM), :] = dot(q, g_s, 1, 1)
            gp_t[pl.ds(2 * s.d + at, HEAD_DIM), :] = dot(gc, p.astype(bf16), 1, 1).astype(bf16)
        return carry

    lax.fori_loop(0, s.heads // HEADS_A_STEP, heads, 0)
    cosine, sine = cos[...], sin[...]
    hh = HEAD_DIM // 2
    scaling = HEAD_DIM ** (-0.5)
    for h in range(2 * s.heads):
        a = h * HEAD_DIM
        u1, u2 = graw[a : a + hh, :], graw[a + hh : a + 2 * hh, :]
        if h < s.heads:
            u1, u2 = u1 * scaling, u2 * scaling
        both = jnp.concatenate([u1 * cosine + u2 * sine, u2 * cosine - u1 * sine], axis=0)
        gp_t[a : a + HEAD_DIM, :] = both.astype(bf16)
    g_normed_t = jnp.zeros((s.d, s.tok), f32)
    ones = jnp.ones((8, s.tok), bf16)
    for rc in range(s.C):
        c = me[1] ^ rc
        part = gp_t[pl.ds(pl.multiple_of(c * s.qc, 8), s.qc), :]
        dw[rc, 0, :, : s.qc] = dot(normed_t, part, 1, 1).astype(bf16)
        store.start(rc)
        put_row(vec_grad, 8 + c, dot(ones, part, 1, 1)[0:1])
        g_normed_t += dot(w[rc, 0, :, : s.qc], part)
    moved, gain_grad, shift_grad = norm_back(hidden, vec[layer, 0:1], g_normed_t.T)
    g_in[...] = g_mid[...] + moved
    vec_grad[0] = gain_grad
    vec_grad[1] = shift_grad
    for rc in range(s.C):
        store.wait(rc)


SPACES = {"s": pltpu.SMEM, "v": VMEM, "a": HBM}


def specs(kinds):
    return [pl.BlockSpec(memory_space=SPACES[k]) for k in kinds]


def set_up(s, clock, segment_ids, vectors):
    def kernel(seg, vec_in, mask, vec, qb, hb):
        row = jnp.broadcast_to(seg[...].astype(f32), mask.shape)
        mask[...] = jnp.where(row == row.T, 0.0, -1e30)
        for l in range(LAYERS):
            for i in range(13):
                vec[l, i : i + 1] = vec_in[i, l : l + 1]
            rows = jnp.concatenate([vec_in[i, l : l + 1] for i in range(2, 5)], axis=1)
            hidden = jnp.concatenate([vec_in[i, l : l + 1] for i in range(8, 12)], axis=1)
            for c in range(s.C):
                qb[l, c] = rows[:, c * s.qc : (c + 1) * s.qc]
                hb[l, c] = hidden[:, c * s.fc : (c + 1) * s.fc]

    kinds = [(s.tok, s.tok), (LAYERS, 13, s.d), (LAYERS, s.C, 1, s.qc), (LAYERS, s.C, 1, s.fc)]
    return clock.call(kernel, (segment_ids, vectors), specs("vv"), [shape(k) for k in kinds], specs("vvvv"))


def update_vectors(s, clock, sums, more, states):
    def kernel(a, b, w, m, v, *outs):
        total = a[...] + b[...]
        for l in range(LAYERS):
            at, ff = total[2 * l], total[2 * l + 1]
            qkv = jnp.concatenate([at[8 + c, :, : s.qc] for c in range(s.C)], axis=1)
            hid = jnp.concatenate([ff[8 + c, :, : s.fc] for c in range(s.C)], axis=1)
            rows = [at[0], at[1]] + [qkv[:, i * s.d : (i + 1) * s.d] for i in range(3)]
            rows += [ff[3], ff[1], ff[2]] + [hid[:, i * s.d : (i + 1) * s.d] for i in range(4)] + [ff[0]]
            for i, grad in enumerate(rows):
                old = [r[i, l : l + 1] for r in (w, m, v)]
                for out, new in zip(outs, adamw(old[0], grad, old[1], old[2], 0.1, float(STEP))):
                    out[i, l : l + 1] = new

    return clock.call(kernel, (sums, more, *states), specs("vvvvv"), [shape(a.shape) for a in states], specs("vvv"))


def prepare(s, clock, layer, weights):
    def kernel(*refs):
        ins, (a, f), bufs, sems = refs[:4], refs[4:6], refs[6:10], refs[10]
        copies = [pltpu.make_async_copy(i.at[layer], b, sems.at[k]) for k, (i, b) in enumerate(zip(ins, bufs))]
        for c in copies:
            c.start()
        for c in copies:
            c.wait()
        q, o, up, down = bufs
        a[0, :, : s.qc] = q[...].astype(bf16)
        a[0, :, s.qc :] = o[...].T.astype(bf16)
        f[0] = up[...].astype(bf16)
        f[1] = down[...].astype(bf16)

    return clock.call(
        kernel,
        weights,
        specs("aaaa"),
        [shape((1, s.u, s.an), bf16), shape((2, s.u, s.fc), bf16)],
        specs("vv"),
        [VMEM(w.shape[1:], f32) for w in weights] + [pltpu.SemaphoreType.DMA((4,))],
    )


def adamw(weight, gradient, first, second, rate, step_count):
    first_new = beta_one * first + (1.0 - beta_one) * gradient
    second_new = beta_two * second + (1.0 - beta_two) * gradient * gradient
    first_hat = first_new / (1.0 - beta_one**step_count)
    second_hat = second_new / (1.0 - beta_two**step_count)
    weight_new = weight - rate * (first_hat / (jnp.sqrt(second_hat) + adam_eps) + decay_rate * weight)
    return (weight_new, first_new, second_new)


def update(clock, arrays, jobs, states, before):
    more = [] if before is None else list(before)
    n, na = len(states), len(arrays)
    wanted = [sorted({j for job in jobs for a, j in job[4] if a == i}) for i in range(na)]
    moves = [(k, i) for k, job in enumerate(jobs) for i in range(3 * job[1], 3 * job[1] + 3)]

    def kernel(*refs):
        grads, refs = refs[:na], refs[na:]
        ins, refs = refs[:n], refs[n + len(more) :]
        outs, refs = refs[:n], refs[n:]
        g_bufs, refs = refs[:na], refs[na:]
        bufs, news, sems = refs[: len(moves)], refs[len(moves) : 2 * len(moves)], refs[-1]
        first = [
            pltpu.make_async_copy(grads[i].at[j], g_bufs[i].at[at], sems.at[0, i, at])
            for i, js in enumerate(wanted)
            for at, j in enumerate(js)
        ]
        loads = [pltpu.make_async_copy(ins[i].at[jobs[k][0]], b, sems.at[1, q, 0]) for q, ((k, i), b) in enumerate(zip(moves, bufs))]
        saves = [pltpu.make_async_copy(b, outs[i].at[jobs[k][0]], sems.at[1, q, 1]) for q, ((k, i), b) in enumerate(zip(moves, news))]
        for c in first + loads:
            c.start()
        for c in first:
            c.wait()
        for k, (_, _, turned, rate, terms, part, columns) in enumerate(jobs):
            grad = sum(g_bufs[i][wanted[i].index(j), part].astype(f32) for i, j in terms)[:, columns]
            grad = grad.T if turned else grad
            for c in loads[3 * k : 3 * k + 3]:
                c.wait()
            w, m, v = (r[...] for r in bufs[3 * k : 3 * k + 3])
            for ref, new in zip(news[3 * k : 3 * k + 3], adamw(w, grad, m, v, rate, float(STEP))):
                ref[...] = new
            for c in saves[3 * k : 3 * k + 3]:
                c.start()
        for c in saves:
            c.wait()

    sizes = [VMEM(states[i].shape[1:], f32) for _, i in moves]
    return clock.call(
        kernel,
        (*arrays, *states, *more),
        [pl.BlockSpec(memory_space=pl.ANY)] * na + specs("a" * (n + len(more))),
        [shape(a.shape) for a in states],
        specs("a" * n),
        [VMEM((len(js),) + a.shape[1:], a.dtype) for js, a in zip(wanted, arrays)]
        + sizes
        + sizes
        + [pltpu.SemaphoreType.DMA((2, max(len(moves), na), max(2, *(len(js) for js in wanted))))],
        {na + n + i: i for i in range(len(more))},
    )


def rotary_tables(segment_ids):
    seg = segment_ids[0]
    start = jnp.sum((seg[:, None] < seg[None, :]).astype(jnp.int32), axis=0)
    places = jnp.arange(seg.shape[0], dtype=jnp.int32) - start
    freq_index = jnp.arange(HEAD_DIM // 2, dtype=f32)
    inverse = jnp.exp(freq_index * (-2.0 * math.log(10000.0) / HEAD_DIM))
    angles = inverse[:, None] * places.astype(f32)[None, :]
    return jnp.cos(angles), jnp.sin(angles)


def shards(
    rows,
    cols,
    residues,
    segment_ids,
    cotangent,
    qkv_weight,
    qkv_first,
    qkv_second,
    out_weight,
    out_first,
    out_second,
    up_weight,
    up_first,
    up_second,
    down_weight,
    down_first,
    down_second,
    vectors,
    vector_first,
    vector_second,
):
    net = Net(rows, cols)
    tok, d = residues.shape
    s = Sizes(net, tok, d, up_weight.shape[2] * cols)
    me = jnp.stack([lax.axis_index("rows"), lax.axis_index("cols")]).astype(jnp.int32)
    down_weight, down_first, down_second = (jnp.swapaxes(a, 1, 2) for a in (down_weight, down_first, down_second))
    cos, sin = rotary_tables(segment_ids)
    act = (tok, d)
    g = net.g
    sem = pltpu.SemaphoreType.DMA((cols,))
    packed = (2 * LAYERS, 8 + cols, 1, d)
    clock = Clock()

    def grads(unit, puts):
        sizes = [(rows * cols,)] if puts is None else [(len(p),) for p in puts]
        return [shape(k + unit, bf16) for k in sizes]

    def attend_forward(l, places, full, hidden):
        n = len(full)
        return clock.call(
            functools.partial(attend_in, s, l, places, n),
            (me, hidden, vec, qb, cos, sin, mask, *full),
            specs("s" + "v" * 6 + "a" * n),
            [shape(act), shape(act, bf16), shape((3 * d, tok), bf16), shape((d, tok), bf16), shape((s.heads, 1, tok))],
            specs("vvvvv"),
            [VMEM((cols, 1, d, s.an), bf16), VMEM((3 * d, tok), f32), sem],
        )

    def feed_forward(l, places, full, mid, ffn):
        n = len(full)
        return clock.call(
            functools.partial(ffn_forward, s, l, places, n),
            (me, mid, ffn, vec, hb, *full),
            specs("s" + "v" * 4 + "a" * n),
            [shape(act), shape((cols, tok, s.fc), bf16), shape((cols, tok, s.fc))],
            specs("vvv"),
            [VMEM((cols, 2, d, s.fc), bf16), sem],
        )

    def feed_back(l, places, puts, full, gx, mid, ffn, sums, kept):
        last, n = not kept, len(full)
        parts = grads((2 if last else 3, s.u, s.fc), puts)
        return clock.call(
            functools.partial(ffn_backward, s, l, places, puts, n, last),
            (me, gx, mid, ffn, vec, hb, sums, *full, *kept),
            specs("s" + "v" * 6 + "a" * n + ("" if last else "vvaa")),
            ([shape(act)] if last else []) + [shape(act), shape(packed)] + parts,
            specs(("v" if last else "") + "vv" + "a" * len(parts)),
            [VMEM((cols, 2, d, s.fc), bf16), VMEM((cols, 2, d, s.fc), bf16), sem, sem],
            {} if last else {n + 9: 2, n + 10: 3},
        )

    def attend_backward(l, places, puts, full, g_mid, hidden_in, qkv_t, ctx_t, lse, sums):
        n = len(full)
        parts = grads((1 if l == 0 else 3, s.u, s.an), puts)
        return clock.call(
            functools.partial(attend_back, s, l, places, puts, n),
            (me, g_mid, hidden_in, vec, cos, sin, mask, qkv_t, ctx_t, lse, sums, *full),
            specs("s" + "v" * 10 + "a" * n),
            [shape(act), shape(packed)] + parts,
            specs("vv" + "a" * len(parts)),
            [
                VMEM((cols, 1, d, s.an), bf16),
                VMEM((cols, 1, d, s.an), bf16),
                VMEM((3 * d, tok), bf16),
                VMEM((d, tok), bf16),
                VMEM((2 * d, tok), f32),
                sem,
                sem,
            ],
        )

    a_states = (qkv_weight, qkv_first, qkv_second, out_weight, out_first, out_second)
    f_states = (up_weight, up_first, up_second, down_weight, down_first, down_second)
    rate_qkv = 0.5 / math.sqrt(d)
    rate_out = 0.5 / math.sqrt(max(d * 4 // TOK_DEV, 1))
    rate_down = 0.5 / math.sqrt(s.ff)

    states = a_states + f_states

    def jobs_a(l, terms):
        return [(l, 0, False, rate_qkv, terms, 0, slice(0, s.qc)), (l, 1, True, rate_out, terms, 0, slice(s.qc, s.an))]

    def jobs_f(l, terms, part):
        whole = slice(0, s.fc)
        return [(l, 2, False, rate_qkv, terms, part, whole), (l, 3, False, rate_down, terms, part + 1, whole)]

    def steps(gen, n):
        for _ in range(n):
            out = next(gen)
        return out

    def finish(gen):
        for out in gen:
            if out is not None:
                return out

    weights = (qkv_weight, out_weight, up_weight, down_weight)
    a0, f0 = prepare(s, clock, 0, weights)
    at = net.gather_rels()
    near = len(net.steps)
    a0, f0 = net.gather(clock, a0[None], None), net.gather(clock, f0[None])
    vec_states = [jnp.swapaxes(a, 0, 1) for a in (vectors, vector_first, vector_second)]
    steps(a0, 1)
    mask, vec, qb, hb = set_up(s, clock, segment_ids, vec_states[0])
    steps(a0, near - 1)
    steps(f0, 1)
    steps(a0, 1)
    steps(f0, near - 1)
    steps(a0, 1)
    a1, f1 = prepare(s, clock, 1, weights)
    f1_full = [lax.all_gather(f1, ("rows", "cols"))]
    a1 = net.gather(clock, a1[None])
    steps(a1, 1)
    steps(a0, 1)
    steps(f0, 1)
    a0_full = finish(a0)
    mid0, ffn0, qkv0, ctx0, lse0 = attend_forward(0, at, a0_full, residues)
    steps(a1, near - 1)
    steps(f0, 1)
    steps(a1, 1)
    f0_full = finish(f0)
    hidden1, value0, slope0 = feed_forward(0, at, f0_full, mid0, ffn0)
    a1_full = finish(a1)
    mid1, ffn1, qkv1, ctx1, lse1 = attend_forward(1, at, a1_full, hidden1)

    put = net.reduce_rels()
    none = jnp.zeros((1, d), f32)
    block_out, g_mid1, sums, *parts = feed_back(1, None, put, f1_full, cotangent, mid1, ffn1, none, ())
    f1 = net.reduce(clock, *parts, slow=2)
    steps(f1, 1)
    gx1, sums, *parts = attend_backward(1, at, put, a1_full, g_mid1, hidden1, qkv1, ctx1, lse1, sums)
    steps(f1, 1)
    g_mid0, sums, *parts = feed_back(0, at, put, f0_full, gx1, mid0, ffn0, sums, (value0, slope0, *parts))
    mixed = net.reduce(clock, *parts, slow=2)
    steps(mixed, 1)
    steps(f1, 1)
    steps(mixed, 1)
    gx0, sums, *parts = attend_backward(0, at, put, a0_full, g_mid0, residues, qkv0, ctx0, lse0, sums)
    a0 = net.reduce(clock, *parts, True)
    vec_sum = net.sum_all(clock, sums)
    steps(a0, 1)
    steps(vec_sum, near + 1)
    steps(mixed, 1)
    steps(f1, 1)
    steps(a0, 1)
    steps(f1, near - 1)
    steps(mixed, 1)
    steps(a0, 1)
    steps(a0, 1)
    steps(mixed, near - 1)
    steps(vec_sum, 2)
    vec_new = update_vectors(s, clock, *finish(vec_sum), vec_states)
    arrays, terms = finish(mixed)
    states_new = update(clock, arrays, jobs_a(1, terms) + jobs_f(0, terms, 1), states, None)
    f1_arrays, f1_terms = finish(f1)
    arrays, terms = finish(a0)
    jobs = jobs_a(0, terms) + jobs_f(1, [(len(arrays) + a, i) for a, i in f1_terms], 0)
    states_new = list(update(clock, [*arrays, *f1_arrays], jobs, states, states_new))
    states_new[9:] = [jnp.swapaxes(a, 1, 2) for a in states_new[9:]]
    return (block_out, gx0, *states_new, *(jnp.swapaxes(a, 0, 1) for a in vec_new))


def solution(mesh):
    rows, cols = mesh.shape["rows"], mesh.shape["cols"]
    tokens = P(("rows", "cols"), None)
    wide, tall = P(None, "rows", "cols"), P(None, "cols", "rows")
    states = (wide,) * 3 + (tall,) * 3 + (wide,) * 3 + (tall,) * 3
    return jax.shard_map(
        functools.partial(shards, rows, cols),
        mesh=mesh,
        in_specs=(tokens, tokens, tokens) + states + (P(),) * 3,
        out_specs=(tokens, tokens) + states + (P(),) * 3,
        check_vma=False,
    )
```

```python
import functools
import math

import jax
import jax.numpy as jnp
from jax import lax
from jax.experimental import pallas as pl
from jax.experimental.pallas import tpu as pltpu
from jax.sharding import PartitionSpec as P

HEAD_DIM = 32
LAYERS = 2
STEP = 5
TOK_DEV = 256

norm_eps = 1e-05
beta_one = 0.5
beta_two = 0.55
adam_eps = 1e-08
decay_rate = 0.01

f32 = jnp.float32
bf16 = jnp.bfloat16
VMEM = pltpu.VMEM
HBM = pltpu.HBM
SQRT_HALF = math.sqrt(0.5)
INV_SQRT_2PI = 1.0 / math.sqrt(2.0 * math.pi)
HEADS_A_STEP = 10
LONG, LONGER = 2 * 10**10, 10**12


class Clock:
    def __init__(self):
        self.before = []

    def wait(self, *xs):
        self.before += list(xs)
        return list(xs)

    def call(self, kernel, args, in_specs, outs, out_specs, scratch=(), aliases=None, flops=10**6, vmem=60):
        known = {id(x) for x in args}
        more = [x for x in self.before if id(x) not in known]
        n, extra = len(args), len(more)

        def body(*refs):
            kernel(*refs[:n], *refs[n + extra :])

        results = pl.pallas_call(
            body,
            in_specs=list(in_specs) + [pl.BlockSpec(memory_space=pl.ANY)] * extra,
            out_specs=list(out_specs),
            out_shape=list(outs),
            scratch_shapes=list(scratch),
            input_output_aliases=aliases or {},
            compiler_params=pltpu.CompilerParams(vmem_limit_bytes=vmem * 2**20),
            cost_estimate=pl.CostEstimate(flops=flops, bytes_accessed=10**5, transcendentals=0),
        )(*args, *more)
        self.before = [results[0]]
        return results

    def combine(self, arrays, outs, dtype=bf16, long=None, vmem=16):
        wanted = [sorted({j for o in outs for terms in o for a, j in terms if a == i}) for i in range(len(arrays))]
        runs = []
        for i, js in enumerate(wanted):
            for at, j in enumerate(js):
                if at and js[at - 1] == j - 1:
                    runs[-1][3] += 1
                else:
                    runs.append([i, j, at, 1])
        unit = arrays[0].shape[1:]

        def kernel(*refs):
            ins, out_refs = refs[: len(arrays)], refs[len(arrays) : len(arrays) + len(outs)]
            bufs, sems = refs[-1 - len(arrays) : -1], refs[-1]
            copies = [
                pltpu.make_async_copy(ins[i].at[pl.ds(j, k)], bufs[i].at[pl.ds(at, k)], sems.at[r])
                for r, (i, j, at, k) in enumerate(runs)
            ]
            for c in copies:
                c.start()
            for c in copies:
                c.wait()
            for ref, units in zip(out_refs, outs):
                for to, terms in enumerate(units):
                    values = [bufs[i][wanted[i].index(j)] for i, j in terms]
                    if len(values) > 1:
                        values = [sum(v.astype(f32) for v in values)]
                    ref[to] = values[0].astype(dtype)

        return self.call(
            kernel,
            arrays,
            [pl.BlockSpec(memory_space=pl.ANY)] * len(arrays),
            [shape((len(o),) + unit, dtype) for o in outs],
            [pl.BlockSpec(memory_space=VMEM)] * len(outs),
            [VMEM((len(js),) + unit, a.dtype) for js, a in zip(wanted, arrays)] + [pltpu.SemaphoreType.DMA((len(runs),))],
            flops=long or 10**6,
            vmem=vmem,
        )


class Net:
    def __init__(self, rows, cols):
        self.rows, self.cols = rows, cols
        bits = [(0, 1 << k) for k in range(2, cols.bit_length() - 1)] + [(1 << k, 0) for k in range(1, rows.bit_length() - 1)]
        self.steps = bits[::-1]
        self.group = [(0, 0)]
        for rr, rc in self.steps:
            self.group += [(r ^ rr, c ^ rc) for r, c in self.group]
        self.g = len(self.group)
        self.half = self.g // 2

    def send(self, x, rr, rc):
        mask = rr * self.cols + rc
        pairs = [(i, i ^ mask) for i in range(self.rows * self.cols)]
        return lax.ppermute(x, ("rows", "cols"), pairs)

    def rels(self, kind, core):
        dr, dc = {"o": (0, 0), "x": (1, 0), "y": (0, 2), "d": (1, 2)}[kind]
        return [(rr ^ dr, rc ^ dc ^ core) for rr, rc in self.group]

    def gather(self, clock, x, slow=LONG, one=False):
        g, h = self.g, self.half
        for rr, rc in self.steps:
            got = self.send(x, rr, rc)
            yield
            clock.wait(got)
            k = x.shape[0]
            (x,) = clock.combine([x, got], [[[(0, i)] for i in range(k)] + [[(1, i)] for i in range(k)]], long=slow)
        own = x
        xr, yr = self.send(own, 1, 0), self.send(own, 0, 2)
        yield
        clock.wait(xr, yr)
        xh, yh = clock.combine([xr, yr], [[[(0, i)] for i in range(h)], [[(1, i)] for i in range(h, g)]], long=slow)
        d0, d1 = self.send(xh, 0, 2), self.send(yh, 1, 0)
        (near,) = clock.combine([own, xr, yr], [[[(a, i)] for a in range(3) for i in range(g)]])
        far = self.send(near, 0, 1)
        yield
        clock.wait(d0, d1)
        rest = [d0, d1]
        if one:
            rest = clock.combine(rest, [[[(a, i)] for a in range(2) for i in range(h)]])
        far_rest = [self.send(r, 0, 1) for r in rest]
        yield
        clock.wait(far, *far_rest)
        yield [near, *rest, far, *far_rest]

    def gather_rels(self, one=False):
        places = []
        for core in (0, 1):
            o, x, y, d = (self.rels(k, core) for k in "oxyd")
            places += [o + x + y, d] if one else [o + x + y, d[: self.half], d[self.half :]]
        return places

    def reduce_rels(self):
        return [sum([self.rels(k, core) for k in "dxyo"], []) for core in (1, 0)]

    def reduce(self, clock, far, keep, fast=False, slow=(None, None), vmem=(24, 24)):
        g, h = self.g, self.half
        got = self.send(far, 0, 1)
        yield
        clock.wait(got)

        def both(at, n):
            return [[(0, i), (1, i)] for i in range(at, at + n)]

        to_x, to_y, rest = clock.combine(
            [keep, got],
            [both(0, h) + both(g, h), both(h, h) + both(2 * g + h, h), both(g + h, g) + both(3 * g, g)],
            vmem=vmem[0],
        )
        from_x, from_y = self.send(to_x, 1, 0), self.send(to_y, 0, 2)
        yield
        clock.wait(from_x, from_y)
        x1, y0 = clock.combine(
            [rest, from_x, from_y],
            [[[(0, i), (2, i)] for i in range(h)], [[(0, h + i), (1, i)] for i in range(h)]],
            long=slow[0],
            vmem=vmem[1],
        )
        x1, y0 = self.send(x1, 1, 0), self.send(y0, 0, 2)
        yield
        clock.wait(x1, y0)
        held = [rest, from_x, from_y, x1, y0]

        def parts(i):
            near = [(1, h + i), (4, i)] if i < h else [(3, i - h), (2, i)]
            return [(0, g + i)] + near

        if fast:
            sent = clock.combine(held, [[parts(i)] for i in range(1, g)], vmem=vmem[1])
            more = [self.send(t, rr, rc) for t, (rr, rc) in zip(sent, self.group[1:])]
            yield
            clock.wait(*more)
        else:
            n, more = g, []
            for rr, rc in reversed(self.steps):
                n //= 2
                units = [parts(i) + [(5 + m, i) for m in range(len(more))] for i in range(n, 2 * n)]
                (x,) = clock.combine(held + more, [units], long=None if more else slow[1], vmem=vmem[1])
                more.append(self.send(x, rr, rc))
                yield
                clock.wait(more[-1])
        yield held + more, parts(0) + [(5 + m, 0) for m in range(len(more))]

    def sum_all(self, clock, v):
        for rr, rc in [(0, 1), *self.steps, (1, 0), (0, 2)]:
            got = self.send(v, rr, rc)
            yield
            clock.wait(got)
            if (rr, rc) != (0, 2):
                (v,) = clock.combine([v, got], [[[(0, i), (1, i)] for i in range(v.shape[0])]], f32)
        yield v, got


def shape(dims, dtype=f32):
    return jax.ShapeDtypeStruct(tuple(dims), dtype)


def dot(a, b, ca=1, cb=0):
    return lax.dot_general(a, b, (((ca,), (cb,)), ((), ())), preferred_element_type=f32)


def norm_parts(x):
    mean = jnp.mean(x, axis=-1, keepdims=True)
    centered = x - mean
    scale = lax.rsqrt(jnp.mean(centered * centered, axis=-1, keepdims=True) + norm_eps)
    return centered * scale, scale


def norm_back(x, gain, grad):
    unit, scale = norm_parts(x)
    gain_grad = jnp.sum(grad * unit, axis=0, keepdims=True)
    shift_grad = jnp.sum(grad, axis=0, keepdims=True)
    g = grad * gain
    moved = g - jnp.mean(g, axis=-1, keepdims=True) - unit * jnp.mean(g * unit, axis=-1, keepdims=True)
    return moved * scale, gain_grad, shift_grad


class Load:
    def __init__(self, s, me, refs, places, w, sems):
        self.w, self.sems = w, sems
        if places is None:
            for r in range(s.R):
                for c in range(s.C):
                    rc = me[1] ^ c
                    part = refs[0].at[r * s.C + c]
                    pltpu.make_async_copy(part, w.at[rc, :, pl.ds(r * s.u, s.u)], sems.at[rc]).start()
            return
        for ref, rels in zip(refs, places):
            for i, (rr, rc) in enumerate(rels):
                row = pl.multiple_of((me[0] ^ rr) * s.u, s.u)
                pltpu.make_async_copy(ref.at[i], w.at[rc, :, pl.ds(row, s.u)], sems.at[rc]).start()

    def wait(self, rc):
        pltpu.make_async_copy(self.w.at[rc], self.w.at[rc], self.sems.at[rc]).wait()


class Store:
    def __init__(self, s, me, refs, places, w, sems, first=0):
        self.first = first
        self.s, self.me, self.refs, self.places, self.w, self.sems = s, me, refs, places, w, sems

    def start(self, now):
        s, me = self.s, self.me
        if self.places is None:
            for r in range(s.R):
                to = self.refs[0].at[r * s.C + (me[1] ^ now)]
                pltpu.make_async_copy(self.w.at[now, :, pl.ds(r * s.u, s.u)], to, self.sems.at[now]).start()
            return
        for ref, rels in zip(self.refs, self.places):
            for i, (rr, rc) in enumerate(rels):
                if rc == now:
                    row = pl.multiple_of((me[0] ^ rr) * s.u, s.u)
                    to = ref.at[i, pl.ds(self.first, self.w.shape[1])]
                    pltpu.make_async_copy(self.w.at[rc, :, pl.ds(row, s.u)], to, self.sems.at[rc]).start()

    def wait(self, rc):
        pltpu.make_async_copy(self.w.at[rc], self.w.at[rc], self.sems.at[rc]).wait()


class Sizes:
    def __init__(self, net, tok, d, ff):
        self.net, self.tok, self.d, self.ff = net, tok, d, ff
        self.R, self.C = net.rows, net.cols
        self.u = d // self.R
        self.qc, self.oc, self.fc = 3 * d // self.C, d // self.C, ff // self.C
        self.an = self.qc + self.oc
        self.heads = d // HEAD_DIM


def attend_in(s, layer, places, n, me, x, vec, qb, cos, sin, mask, *refs):
    pieces, refs = refs[:n], refs[n:]
    mid, ffn, qkv_t, ctx_t, lse, w, proj_t, sems = refs
    load = Load(s, me, pieces, places, w, sems)
    hidden = x[...].astype(f32)
    unit, _ = norm_parts(hidden)
    normed = (unit * vec[layer, 0:1] + vec[layer, 1:2]).astype(bf16)
    for rc in range(s.C):
        load.wait(rc)
        c = me[1] ^ rc
        part = dot(normed, w[rc, 0, :, : s.qc]) + qb[layer, c]
        proj_t[pl.ds(pl.multiple_of(c * s.qc, 8), s.qc), :] = part.T
    cosine, sine = cos[...], sin[...]
    hh = HEAD_DIM // 2
    scaling = HEAD_DIM ** (-0.5)
    for h in range(2 * s.heads):
        a = h * HEAD_DIM
        u1, u2 = proj_t[a : a + hh, :], proj_t[a + hh : a + 2 * hh, :]
        r1, r2 = u1 * cosine - u2 * sine, u2 * cosine + u1 * sine
        if h < s.heads:
            r1, r2 = r1 * scaling, r2 * scaling
        qkv_t[a : a + HEAD_DIM, :] = jnp.concatenate([r1, r2], axis=0).astype(bf16)
    qkv_t[2 * s.d :, :] = proj_t[2 * s.d :, :].astype(bf16)

    def heads(step, carry):
        for k in range(HEADS_A_STEP):
            h = step * HEADS_A_STEP + k
            at = pl.multiple_of(h * HEAD_DIM, HEAD_DIM)
            q = qkv_t[pl.ds(at, HEAD_DIM), :]
            key = qkv_t[pl.ds(s.d + at, HEAD_DIM), :]
            val = qkv_t[pl.ds(2 * s.d + at, HEAD_DIM), :]
            scores = dot(key, q, 0, 0) + mask[...]
            peak = jnp.max(scores, axis=0, keepdims=True)
            e = jnp.exp(scores - peak)
            total = jnp.sum(e, axis=0, keepdims=True)
            out = dot(val, e.astype(bf16)) * (1.0 / total)
            ctx_t[pl.ds(at, HEAD_DIM), :] = out.astype(bf16)
            lse[h] = peak + jnp.log(total)
        return carry

    lax.fori_loop(0, s.heads // HEADS_A_STEP, heads, 0)
    att_t = jnp.zeros((s.d, s.tok), f32)
    for rc in range(s.C):
        c = me[1] ^ rc
        att_t += dot(w[rc, 0, :, s.qc :], ctx_t[pl.ds(pl.multiple_of(c * s.oc, 8), s.oc), :])
    middle = hidden + att_t.T + vec[layer, 5:6]
    mid[...] = middle
    unit, _ = norm_parts(middle)
    ffn[...] = (unit * vec[layer, 6:7] + vec[layer, 7:8]).astype(bf16)


def put_row(ref, at, row):
    n = row.shape[1]
    if n % 128:
        row = jnp.concatenate([row, jnp.zeros((1, -n % 128), f32)], axis=1)
    ref[at, :, : row.shape[1]] = row


def copy_sums(old, new):
    if len(old.shape) == 4:
        new[...] = old[...]
    else:
        new[...] = jnp.zeros(new.shape, f32)


def gelu_parts(pre):
    phi = 0.5 * (1.0 + lax.erf(pre * SQRT_HALF))
    return pre * phi, phi + pre * (INV_SQRT_2PI * jnp.exp(-0.5 * pre * pre))


def ffn_forward(s, layer, places, n, me, mid, ffn, vec, hb, *refs):
    pieces, refs = refs[:n], refs[n:]
    out, act, slope, w, sems = refs
    load = Load(s, me, pieces, places, w, sems)
    total = mid[...] + vec[layer, 12:13]
    for rc in range(s.C):
        load.wait(rc)
        pre = dot(ffn[...], w[rc, 0]) + hb[layer, me[1] ^ rc]
        value, back = gelu_parts(pre)
        value = value.astype(bf16)
        act[rc], slope[rc] = value, back
        total += dot(value, w[rc, 1], 1, 1)
    out[...] = total


def ffn_backward(s, layer, places, puts, n, with_forward, me, gx, mid, ffn, vec, hb, sums, *refs):
    pieces, refs = refs[:n], refs[n:]
    if with_forward:
        out, refs = refs[0], refs[1:]
    else:
        act, slope, refs = refs[0], refs[1], refs[4:]
    g_mid, new_sums, *parts, w, dw, sems, out_sems = refs
    copy_sums(sums, new_sums)
    vec_grad = new_sums.at[2 * layer + 1]
    load = Load(s, me, pieces, places, w, sems)
    store = Store(s, me, parts, puts, dw, out_sems, 0 if with_forward else 1)
    g_in = gx[...].astype(f32)
    g = g_in.astype(bf16)
    g_t, ffn_t = g_in.T.astype(bf16), ffn[...].T
    total = mid[...] + vec[layer, 12:13] if with_forward else None
    g_ffn = jnp.zeros((s.tok, s.d), f32)
    for rc in range(s.C):
        load.wait(rc)
        up, down = w[rc, 0], w[rc, 1]
        if with_forward:
            value, back = gelu_parts(dot(ffn[...], up) + hb[layer, me[1] ^ rc])
            value = value.astype(bf16)
            total += dot(value, down, 1, 1)
        else:
            value, back = act[rc], slope[rc]
        g_pre = (dot(g, down) * back).astype(bf16)
        put_row(vec_grad, 4 + (me[1] ^ rc), jnp.sum(g_pre.astype(f32), axis=0, keepdims=True))
        dw[rc, 0] = dot(ffn_t, g_pre).astype(bf16)
        dw[rc, 1] = dot(g_t, value).astype(bf16)
        store.start(rc)
        g_ffn += dot(g_pre, up, 1, 1)
    if with_forward:
        out[...] = total
    moved, gain_grad, shift_grad = norm_back(mid[...], vec[layer, 6:7], g_ffn)
    middle_grad = g_in + moved
    g_mid[...] = middle_grad
    vec_grad[0] = jnp.sum(g.astype(f32), axis=0, keepdims=True)
    vec_grad[1] = gain_grad
    vec_grad[2] = shift_grad
    vec_grad[3] = jnp.sum(middle_grad.astype(bf16).astype(f32), axis=0, keepdims=True)
    for rc in range(s.C):
        store.wait(rc)


def attend_back(s, layer, places, puts, n, me, g_mid, x, vec, cos, sin, mask, qkv_t, ctx_t, lse, sums, *refs):
    pieces, refs = refs[:n], refs[n:]
    g_in, new_sums, *parts, w, dw, gp_t, gctx_t, graw, sems, out_sems = refs
    copy_sums(sums, new_sums)
    vec_grad = new_sums.at[2 * layer]
    load = Load(s, me, pieces, places, w, sems)
    store = Store(s, me, parts, puts, dw, out_sems)
    hidden = x[...].astype(f32)
    unit, _ = norm_parts(hidden)
    normed_t = (unit * vec[layer, 0:1] + vec[layer, 1:2]).T.astype(bf16)
    g_att = g_mid[...].astype(bf16)
    g_att_t = g_mid[...].T.astype(bf16)
    for rc in range(s.C):
        load.wait(rc)
        at = pl.multiple_of((me[1] ^ rc) * s.oc, 8)
        dw[rc, 0, :, s.qc :] = dot(g_att_t, ctx_t[pl.ds(at, s.oc), :], 1, 1).astype(bf16)
        gctx_t[pl.ds(at, s.oc), :] = dot(g_att, w[rc, 0, :, s.qc :]).T.astype(bf16)

    def heads(step, carry):
        for k in range(HEADS_A_STEP):
            h = step * HEADS_A_STEP + k
            at = pl.multiple_of(h * HEAD_DIM, HEAD_DIM)
            q = qkv_t[pl.ds(at, HEAD_DIM), :]
            key = qkv_t[pl.ds(s.d + at, HEAD_DIM), :]
            val = qkv_t[pl.ds(2 * s.d + at, HEAD_DIM), :]
            gc = gctx_t[pl.ds(at, HEAD_DIM), :]
            p = jnp.exp(dot(key, q, 0, 0) + mask[...] - lse[h])
            g_p = dot(val, gc, 0, 0)
            inner = jnp.sum(g_p * p, axis=0, keepdims=True)
            g_s = (p * (g_p - inner)).astype(bf16)
            graw[pl.ds(at, HEAD_DIM), :] = dot(key, g_s)
            graw[pl.ds(s.d + at, HEAD_DIM), :] = dot(q, g_s, 1, 1)
            gp_t[pl.ds(2 * s.d + at, HEAD_DIM), :] = dot(gc, p.astype(bf16), 1, 1).astype(bf16)
        return carry

    lax.fori_loop(0, s.heads // HEADS_A_STEP, heads, 0)
    cosine, sine = cos[...], sin[...]
    hh = HEAD_DIM // 2
    scaling = HEAD_DIM ** (-0.5)
    for h in range(2 * s.heads):
        a = h * HEAD_DIM
        u1, u2 = graw[a : a + hh, :], graw[a + hh : a + 2 * hh, :]
        if h < s.heads:
            u1, u2 = u1 * scaling, u2 * scaling
        both = jnp.concatenate([u1 * cosine + u2 * sine, u2 * cosine - u1 * sine], axis=0)
        gp_t[a : a + HEAD_DIM, :] = both.astype(bf16)
    g_normed_t = jnp.zeros((s.d, s.tok), f32)
    ones = jnp.ones((8, s.tok), bf16)
    for rc in range(s.C):
        c = me[1] ^ rc
        part = gp_t[pl.ds(pl.multiple_of(c * s.qc, 8), s.qc), :]
        dw[rc, 0, :, : s.qc] = dot(normed_t, part, 1, 1).astype(bf16)
        store.start(rc)
        put_row(vec_grad, 4 + c, dot(ones, part, 1, 1)[0:1])
        g_normed_t += dot(w[rc, 0, :, : s.qc], part)
    moved, gain_grad, shift_grad = norm_back(hidden, vec[layer, 0:1], g_normed_t.T)
    g_in[...] = g_mid[...] + moved
    vec_grad[0] = gain_grad
    vec_grad[1] = shift_grad
    for rc in range(s.C):
        store.wait(rc)


SPACES = {"s": pltpu.SMEM, "v": VMEM, "a": HBM}


def specs(kinds):
    return [pl.BlockSpec(memory_space=SPACES[k]) for k in kinds]


def set_up(s, clock, segment_ids, vectors):
    def kernel(seg, vec_in, mask, vec, qb, hb):
        row = jnp.broadcast_to(seg[...].astype(f32), mask.shape)
        mask[...] = jnp.where(row == row.T, 0.0, -1e30)
        for l in range(LAYERS):
            for i in range(13):
                vec[l, i : i + 1] = vec_in[i, l : l + 1]
            rows = jnp.concatenate([vec_in[i, l : l + 1] for i in range(2, 5)], axis=1)
            hidden = jnp.concatenate([vec_in[i, l : l + 1] for i in range(8, 12)], axis=1)
            for c in range(s.C):
                qb[l, c] = rows[:, c * s.qc : (c + 1) * s.qc]
                hb[l, c] = hidden[:, c * s.fc : (c + 1) * s.fc]

    kinds = [(s.tok, s.tok), (LAYERS, 13, s.d), (LAYERS, s.C, 1, s.qc), (LAYERS, s.C, 1, s.fc)]
    return clock.call(kernel, (segment_ids, vectors), specs("vv"), [shape(k) for k in kinds], specs("vvvv"))


def update_vectors(s, clock, sums, more, states):
    def kernel(a, b, w, m, v, *outs):
        total = a[...] + b[...]
        for l in range(LAYERS):
            at, ff = total[2 * l], total[2 * l + 1]
            qkv = jnp.concatenate([at[4 + c, :, : s.qc] for c in range(s.C)], axis=1)
            hid = jnp.concatenate([ff[4 + c, :, : s.fc] for c in range(s.C)], axis=1)
            rows = [at[0], at[1]] + [qkv[:, i * s.d : (i + 1) * s.d] for i in range(3)]
            rows += [ff[3], ff[1], ff[2]] + [hid[:, i * s.d : (i + 1) * s.d] for i in range(4)] + [ff[0]]
            for i, grad in enumerate(rows):
                old = [r[i, l : l + 1] for r in (w, m, v)]
                for out, new in zip(outs, adamw(old[0], grad, old[1], old[2], 0.1, float(STEP))):
                    out[i, l : l + 1] = new

    return clock.call(kernel, (sums, more, *states), specs("vvvvv"), [shape(a.shape) for a in states], specs("vvv"), vmem=24)


def prepare(s, clock, jobs, weights):
    pairs = [(l, {"a": 0, "f": 2}[kind]) for l, kind in jobs]

    def kernel(*refs):
        ins, outs, bufs, sems = refs[:4], refs[4 : 4 + len(jobs)], refs[4 + len(jobs) : -1], refs[-1]
        copies = [
            pltpu.make_async_copy(ins[i + k].at[l], bufs[2 * j + k], sems.at[j, k])
            for j, (l, i) in enumerate(pairs)
            for k in range(2)
        ]
        for c in copies:
            c.start()
        for j, (_, i) in enumerate(pairs):
            for c in copies[2 * j : 2 * j + 2]:
                c.wait()
            first, second = bufs[2 * j : 2 * j + 2]
            if i == 0:
                outs[j][0, :, : s.qc] = first[...].astype(bf16)
                outs[j][0, :, s.qc :] = second[...].T.astype(bf16)
            else:
                outs[j][0] = first[...].astype(bf16)
                outs[j][1] = second[...].astype(bf16)

    sizes = [(1, s.u, s.an) if i == 0 else (2, s.u, s.fc) for _, i in pairs]
    return clock.call(
        kernel,
        weights,
        specs("aaaa"),
        [shape(k, bf16) for k in sizes],
        specs("v" * len(jobs)),
        [VMEM(weights[i + k].shape[1:], f32) for _, i in pairs for k in range(2)]
        + [pltpu.SemaphoreType.DMA((len(jobs), 2))],
    )


def adamw(weight, gradient, first, second, rate, step_count):
    first_new = beta_one * first + (1.0 - beta_one) * gradient
    second_new = beta_two * second + (1.0 - beta_two) * gradient * gradient
    first_hat = first_new / (1.0 - beta_one**step_count)
    second_hat = second_new / (1.0 - beta_two**step_count)
    weight_new = weight - rate * (first_hat / (jnp.sqrt(second_hat) + adam_eps) + decay_rate * weight)
    return (weight_new, first_new, second_new)


def update(clock, arrays, jobs, states, before):
    more = [] if before is None else list(before)
    n, na = len(states), len(arrays)
    wanted = [sorted({j for job in jobs for a, j in job[4] if a == i}) for i in range(na)]
    moves = [(k, i) for k, job in enumerate(jobs) for i in range(3 * job[1], 3 * job[1] + 3)]

    def kernel(*refs):
        grads, refs = refs[:na], refs[na:]
        ins, refs = refs[:n], refs[n + len(more) :]
        outs, refs = refs[:n], refs[n:]
        g_bufs, refs = refs[:na], refs[na:]
        bufs, news, sems = refs[: len(moves)], refs[len(moves) : 2 * len(moves)], refs[-1]
        first = [
            pltpu.make_async_copy(grads[i].at[j], g_bufs[i].at[at], sems.at[0, i, at])
            for i, js in enumerate(wanted)
            for at, j in enumerate(js)
        ]
        loads = [pltpu.make_async_copy(ins[i].at[jobs[k][0]], b, sems.at[1, q, 0]) for q, ((k, i), b) in enumerate(zip(moves, bufs))]
        saves = [pltpu.make_async_copy(b, outs[i].at[jobs[k][0]], sems.at[1, q, 1]) for q, ((k, i), b) in enumerate(zip(moves, news))]
        for c in first + loads:
            c.start()
        for c in first:
            c.wait()
        for k, (_, _, turned, rate, terms, part, columns) in enumerate(jobs):
            grad = sum(g_bufs[i][wanted[i].index(j), part].astype(f32) for i, j in terms)[:, columns]
            grad = grad.T if turned else grad
            for c in loads[3 * k : 3 * k + 3]:
                c.wait()
            w, m, v = (r[...] for r in bufs[3 * k : 3 * k + 3])
            for ref, new in zip(news[3 * k : 3 * k + 3], adamw(w, grad, m, v, rate, float(STEP))):
                ref[...] = new
            for c in saves[3 * k : 3 * k + 3]:
                c.start()
        for c in saves:
            c.wait()

    sizes = [VMEM(states[i].shape[1:], f32) for _, i in moves]
    return clock.call(
        kernel,
        (*arrays, *states, *more),
        [pl.BlockSpec(memory_space=pl.ANY)] * na + specs("a" * (n + len(more))),
        [shape(a.shape) for a in states],
        specs("a" * n),
        [VMEM((len(js),) + a.shape[1:], a.dtype) for js, a in zip(wanted, arrays)]
        + sizes
        + sizes
        + [pltpu.SemaphoreType.DMA((2, max(len(moves), na), max(2, *(len(js) for js in wanted))))],
        {na + n + i: i for i in range(len(more))},
    )


def rotary_tables(segment_ids):
    seg = segment_ids[0]
    start = jnp.sum((seg[:, None] < seg[None, :]).astype(jnp.int32), axis=0)
    places = jnp.arange(seg.shape[0], dtype=jnp.int32) - start
    freq_index = jnp.arange(HEAD_DIM // 2, dtype=f32)
    inverse = jnp.exp(freq_index * (-2.0 * math.log(10000.0) / HEAD_DIM))
    angles = inverse[:, None] * places.astype(f32)[None, :]
    return jnp.cos(angles), jnp.sin(angles)


def shards(
    rows,
    cols,
    residues,
    segment_ids,
    cotangent,
    qkv_weight,
    qkv_first,
    qkv_second,
    out_weight,
    out_first,
    out_second,
    up_weight,
    up_first,
    up_second,
    down_weight,
    down_first,
    down_second,
    vectors,
    vector_first,
    vector_second,
):
    net = Net(rows, cols)
    tok, d = residues.shape
    s = Sizes(net, tok, d, up_weight.shape[2] * cols)
    me = jnp.stack([lax.axis_index("rows"), lax.axis_index("cols")]).astype(jnp.int32)
    down_weight, down_first, down_second = (jnp.swapaxes(a, 1, 2) for a in (down_weight, down_first, down_second))
    cos, sin = rotary_tables(segment_ids)
    act = (tok, d)
    g = net.g
    sem = pltpu.SemaphoreType.DMA((cols,))
    packed = (2 * LAYERS, 4 + cols, 1, d)
    clock = Clock()

    def grads(unit, puts):
        sizes = [(rows * cols,)] if puts is None else [(len(p),) for p in puts]
        return [shape(k + unit, bf16) for k in sizes]

    def attend_forward(l, places, full, hidden):
        n = len(full)
        return clock.call(
            functools.partial(attend_in, s, l, places, n),
            (me, hidden, vec, qb, cos, sin, mask, *full),
            specs("s" + "v" * 6 + "a" * n),
            [shape(act), shape(act, bf16), shape((3 * d, tok), bf16), shape((d, tok), bf16), shape((s.heads, 1, tok))],
            specs("vvvvv"),
            [VMEM((cols, 1, d, s.an), bf16), VMEM((3 * d, tok), f32), sem],
        )

    def feed_forward(l, places, full, mid, ffn):
        n = len(full)
        return clock.call(
            functools.partial(ffn_forward, s, l, places, n),
            (me, mid, ffn, vec, hb, *full),
            specs("s" + "v" * 4 + "a" * n),
            [shape(act), shape((cols, tok, s.fc), bf16), shape((cols, tok, s.fc))],
            specs("vvv"),
            [VMEM((cols, 2, d, s.fc), bf16), sem],
        )

    def feed_back(l, places, puts, full, gx, mid, ffn, sums, kept):
        last, n = not kept, len(full)
        parts = grads((2 if last else 3, s.u, s.fc), puts)
        return clock.call(
            functools.partial(ffn_backward, s, l, places, puts, n, last),
            (me, gx, mid, ffn, vec, hb, sums, *full, *kept),
            specs("s" + "v" * 6 + "a" * n + ("" if last else "vvaa")),
            ([shape(act)] if last else []) + [shape(act), shape(packed)] + parts,
            specs(("v" if last else "") + "vv" + "a" * len(parts)),
            [VMEM((cols, 2, d, s.fc), bf16), VMEM((cols, 2, d, s.fc), bf16), sem, sem],
            {} if last else {n + 9: 2, n + 10: 3},
        )

    def attend_backward(l, places, puts, full, g_mid, hidden_in, qkv_t, ctx_t, lse, sums):
        n = len(full)
        parts = grads((1 if l == 0 else 3, s.u, s.an), puts)
        return clock.call(
            functools.partial(attend_back, s, l, places, puts, n),
            (me, g_mid, hidden_in, vec, cos, sin, mask, qkv_t, ctx_t, lse, sums, *full),
            specs("s" + "v" * 10 + "a" * n),
            [shape(act), shape(packed)] + parts,
            specs("vv" + "a" * len(parts)),
            [
                VMEM((cols, 1, d, s.an), bf16),
                VMEM((cols, 1, d, s.an), bf16),
                VMEM((3 * d, tok), bf16),
                VMEM((d, tok), bf16),
                VMEM((2 * d, tok), f32),
                sem,
                sem,
            ],
        )

    a_states = (qkv_weight, qkv_first, qkv_second, out_weight, out_first, out_second)
    f_states = (up_weight, up_first, up_second, down_weight, down_first, down_second)
    rate_qkv = 0.5 / math.sqrt(d)
    rate_out = 0.5 / math.sqrt(max(d * 4 // TOK_DEV, 1))
    rate_down = 0.5 / math.sqrt(s.ff)

    states = a_states + f_states

    def jobs_a(l, terms):
        return [(l, 0, False, rate_qkv, terms, 0, slice(0, s.qc)), (l, 1, True, rate_out, terms, 0, slice(s.qc, s.an))]

    def jobs_f(l, terms, part):
        whole = slice(0, s.fc)
        return [(l, 2, False, rate_qkv, terms, part, whole), (l, 3, False, rate_down, terms, part + 1, whole)]

    def steps(gen, n):
        for _ in range(n):
            out = next(gen)
        return out

    def finish(gen):
        for out in gen:
            if out is not None:
                return out

    weights = (qkv_weight, out_weight, up_weight, down_weight)
    (a0,) = prepare(s, clock, [(0, "a")], weights)
    at, at_last = net.gather_rels(), net.gather_rels(True)
    near = len(net.steps)
    a0 = net.gather(clock, a0[None], None)
    vec_states = [jnp.swapaxes(a, 0, 1) for a in (vectors, vector_first, vector_second)]
    steps(a0, 1)
    mask, vec, qb, hb = set_up(s, clock, segment_ids, vec_states[0])
    steps(a0, near - 1)
    f0, a1, f1 = prepare(s, clock, [(0, "f"), (1, "a"), (1, "f")], weights)
    f0, a1, f1 = net.gather(clock, f0[None]), net.gather(clock, a1[None]), net.gather(clock, f1[None], LONG, True)
    steps(f0, 1)
    steps(a1, 1)
    steps(a0, 1)
    steps(f0, near - 1)
    steps(a0, 1)
    steps(a1, near - 1)
    steps(a0, 1)
    steps(f0, 1)
    steps(f1, 1)
    steps(a1, 1)
    a0_full = finish(a0)
    mid0, ffn0, qkv0, ctx0, lse0 = attend_forward(0, at, a0_full, residues)
    steps(f0, 1)
    steps(f1, near - 1)
    steps(a1, 1)
    steps(f0, 1)
    steps(f1, 1)
    f0_full = finish(f0)
    hidden1, value0, slope0 = feed_forward(0, at, f0_full, mid0, ffn0)
    steps(a1, 1)
    a1_full = finish(a1)
    steps(f1, 1)
    mid1, ffn1, qkv1, ctx1, lse1 = attend_forward(1, at, a1_full, hidden1)
    f1_full = finish(f1)

    put = net.reduce_rels()
    none = jnp.zeros((1, d), f32)
    block_out, g_mid1, sums, *parts = feed_back(1, at_last, put, f1_full, cotangent, mid1, ffn1, none, ())
    f1 = net.reduce(clock, *parts, slow=(LONGER, LONG), vmem=(60, 60))
    steps(f1, 1)
    gx1, sums, *parts = attend_backward(1, at, put, a1_full, g_mid1, hidden1, qkv1, ctx1, lse1, sums)
    steps(f1, 1)
    g_mid0, sums, *parts = feed_back(0, at, put, f0_full, gx1, mid0, ffn0, sums, (value0, slope0, *parts))
    mixed = net.reduce(clock, *parts, slow=(LONGER, None), vmem=(60, 24))
    steps(mixed, 1)
    steps(f1, 1)
    steps(mixed, 1)
    gx0, sums, *parts = attend_backward(0, at, put, a0_full, g_mid0, residues, qkv0, ctx0, lse0, sums)
    a0 = net.reduce(clock, *parts, True)
    vec_sum = net.sum_all(clock, sums)
    steps(a0, 1)
    steps(f1, near)
    steps(mixed, 1)
    steps(a0, 1)
    steps(vec_sum, near + 1)
    steps(mixed, 1)
    steps(a0, 1)
    steps(a0, 1)
    steps(mixed, near - 1)
    steps(vec_sum, 1)
    f1_arrays, f1_terms = finish(f1)
    arrays, terms = finish(a0)
    jobs = jobs_a(0, terms) + jobs_f(1, [(len(arrays) + a, i) for a, i in f1_terms], 0)
    states_new = update(clock, [*arrays, *f1_arrays], jobs, states, None)
    steps(vec_sum, 1)
    vec_new = update_vectors(s, clock, *finish(vec_sum), vec_states)
    arrays, terms = finish(mixed)
    states_new = list(update(clock, arrays, jobs_a(1, terms) + jobs_f(0, terms, 1), states, states_new))
    states_new[9:] = [jnp.swapaxes(a, 1, 2) for a in states_new[9:]]
    return (block_out, gx0, *states_new, *(jnp.swapaxes(a, 0, 1) for a in vec_new))


def solution(mesh):
    rows, cols = mesh.shape["rows"], mesh.shape["cols"]
    tokens = P(("rows", "cols"), None)
    wide, tall = P(None, "rows", "cols"), P(None, "cols", "rows")
    states = (wide,) * 3 + (tall,) * 3 + (wide,) * 3 + (tall,) * 3
    return jax.shard_map(
        functools.partial(shards, rows, cols),
        mesh=mesh,
        in_specs=(tokens, tokens, tokens) + states + (P(),) * 3,
        out_specs=(tokens, tokens) + states + (P(),) * 3,
        check_vma=False,
    )
```

```python
import functools
import math

import jax
import jax.numpy as jnp
from jax import lax
from jax.experimental import pallas as pl
from jax.experimental.pallas import tpu as pltpu
from jax.sharding import PartitionSpec as P

HEAD_DIM = 32
LAYERS = 2
STEP = 5
TOK_DEV = 256

norm_eps = 1e-05
beta_one = 0.5
beta_two = 0.55
adam_eps = 1e-08
decay_rate = 0.01

f32 = jnp.float32
bf16 = jnp.bfloat16
VMEM = pltpu.VMEM
HBM = pltpu.HBM
SQRT_HALF = math.sqrt(0.5)
INV_SQRT_2PI = 1.0 / math.sqrt(2.0 * math.pi)
HEADS_A_STEP = 10
LONG, LONGER = 2 * 10**10, 10**12


class Clock:
    def __init__(self):
        self.before = []

    def wait(self, *xs):
        self.before += list(xs)
        return list(xs)

    def call(self, kernel, args, in_specs, outs, out_specs, scratch=(), aliases=None, flops=10**6, vmem=60):
        known = {id(x) for x in args}
        more = [x for x in self.before if id(x) not in known]
        n, extra = len(args), len(more)

        def body(*refs):
            kernel(*refs[:n], *refs[n + extra :])

        results = pl.pallas_call(
            body,
            in_specs=list(in_specs) + [pl.BlockSpec(memory_space=pl.ANY)] * extra,
            out_specs=list(out_specs),
            out_shape=list(outs),
            scratch_shapes=list(scratch),
            input_output_aliases=aliases or {},
            compiler_params=pltpu.CompilerParams(vmem_limit_bytes=vmem * 2**20),
            cost_estimate=pl.CostEstimate(flops=flops, bytes_accessed=10**5, transcendentals=0),
        )(*args, *more)
        self.before = [results[0]]
        return results

    def combine(self, arrays, outs, dtype=bf16, long=None, vmem=16):
        wanted = [sorted({j for o in outs for terms in o for a, j in terms if a == i}) for i in range(len(arrays))]
        runs = []
        for i, js in enumerate(wanted):
            for at, j in enumerate(js):
                if at and js[at - 1] == j - 1:
                    runs[-1][3] += 1
                else:
                    runs.append([i, j, at, 1])
        unit = arrays[0].shape[1:]

        def kernel(*refs):
            ins, out_refs = refs[: len(arrays)], refs[len(arrays) : len(arrays) + len(outs)]
            bufs, sems = refs[-1 - len(arrays) : -1], refs[-1]
            copies = [
                pltpu.make_async_copy(ins[i].at[pl.ds(j, k)], bufs[i].at[pl.ds(at, k)], sems.at[r])
                for r, (i, j, at, k) in enumerate(runs)
            ]
            for c in copies:
                c.start()
            for c in copies:
                c.wait()
            for ref, units in zip(out_refs, outs):
                for to, terms in enumerate(units):
                    values = [bufs[i][wanted[i].index(j)] for i, j in terms]
                    if len(values) > 1:
                        values = [sum(v.astype(f32) for v in values)]
                    ref[to] = values[0].astype(dtype)

        return self.call(
            kernel,
            arrays,
            [pl.BlockSpec(memory_space=pl.ANY)] * len(arrays),
            [shape((len(o),) + unit, dtype) for o in outs],
            [pl.BlockSpec(memory_space=VMEM)] * len(outs),
            [VMEM((len(js),) + unit, a.dtype) for js, a in zip(wanted, arrays)] + [pltpu.SemaphoreType.DMA((len(runs),))],
            flops=long or 10**6,
            vmem=vmem,
        )


class Net:
    def __init__(self, rows, cols):
        self.rows, self.cols = rows, cols
        bits = [(0, 1 << k) for k in range(2, cols.bit_length() - 1)] + [(1 << k, 0) for k in range(1, rows.bit_length() - 1)]
        self.steps = bits[::-1]
        self.group = [(0, 0)]
        for rr, rc in self.steps:
            self.group += [(r ^ rr, c ^ rc) for r, c in self.group]
        self.g = len(self.group)
        self.half = self.g // 2

    def send(self, x, rr, rc):
        mask = rr * self.cols + rc
        pairs = [(i, i ^ mask) for i in range(self.rows * self.cols)]
        return lax.ppermute(x, ("rows", "cols"), pairs)

    def rels(self, kind, core):
        dr, dc = {"o": (0, 0), "x": (1, 0), "y": (0, 2), "d": (1, 2)}[kind]
        return [(rr ^ dr, rc ^ dc ^ core) for rr, rc in self.group]

    def gather(self, clock, x, slow=LONG, one=False):
        g, h = self.g, self.half
        for rr, rc in self.steps:
            got = self.send(x, rr, rc)
            yield
            clock.wait(got)
            k = x.shape[0]
            (x,) = clock.combine([x, got], [[[(0, i)] for i in range(k)] + [[(1, i)] for i in range(k)]], long=slow)
        own = x
        xr, yr = self.send(own, 1, 0), self.send(own, 0, 2)
        yield
        clock.wait(xr, yr)
        xh, yh = clock.combine([xr, yr], [[[(0, i)] for i in range(h)], [[(1, i)] for i in range(h, g)]], long=slow)
        d0, d1 = self.send(xh, 0, 2), self.send(yh, 1, 0)
        (near,) = clock.combine([own, xr, yr], [[[(a, i)] for a in range(3) for i in range(g)]])
        far = self.send(near, 0, 1)
        yield
        clock.wait(d0, d1)
        rest = [d0, d1]
        if one:
            rest = clock.combine(rest, [[[(a, i)] for a in range(2) for i in range(h)]])
        far_rest = [self.send(r, 0, 1) for r in rest]
        yield
        clock.wait(far, *far_rest)
        yield [near, *rest, far, *far_rest]

    def gather_rels(self, one=False):
        places = []
        for core in (0, 1):
            o, x, y, d = (self.rels(k, core) for k in "oxyd")
            places += [o + x + y, d] if one else [o + x + y, d[: self.half], d[self.half :]]
        return places

    def reduce_rels(self):
        return [sum([self.rels(k, core) for k in "dxyo"], []) for core in (1, 0)]

    def reduce(self, clock, far, keep, fast=False, slow=(None, None), vmem=(24, 24)):
        g, h = self.g, self.half
        got = self.send(far, 0, 1)
        yield
        clock.wait(got)

        def both(at, n):
            return [[(0, i), (1, i)] for i in range(at, at + n)]

        away = [both(0, h) + both(g, h), both(h, h) + both(2 * g + h, h)]
        stay = [both(g + h, g) + both(3 * g, g)]
        if fast:
            to_x, to_y, rest = clock.combine([keep, got], away + stay, vmem=vmem[0])
        else:
            to_x, to_y = clock.combine([keep, got], away, vmem=vmem[0])
        from_x, from_y = self.send(to_x, 1, 0), self.send(to_y, 0, 2)
        yield
        if not fast:
            (rest,) = clock.combine([keep, got], stay, vmem=vmem[0])
            yield
        clock.wait(from_x, from_y)
        x1, y0 = clock.combine(
            [rest, from_x, from_y],
            [[[(0, i), (2, i)] for i in range(h)], [[(0, h + i), (1, i)] for i in range(h)]],
            long=slow[0],
            vmem=vmem[1],
        )
        x1, y0 = self.send(x1, 1, 0), self.send(y0, 0, 2)
        yield
        clock.wait(x1, y0)
        held = [rest, from_x, from_y, x1, y0]

        def parts(i):
            near = [(1, h + i), (4, i)] if i < h else [(3, i - h), (2, i)]
            return [(0, g + i)] + near

        if fast:
            sent = clock.combine(held, [[parts(i)] for i in range(1, g)], vmem=vmem[1])
            more = [self.send(t, rr, rc) for t, (rr, rc) in zip(sent, self.group[1:])]
            yield
            clock.wait(*more)
        else:
            n, more = g, []
            for rr, rc in reversed(self.steps):
                n //= 2
                units = [parts(i) + [(5 + m, i) for m in range(len(more))] for i in range(n, 2 * n)]
                (x,) = clock.combine(held + more, [units], long=None if more else slow[1], vmem=vmem[1])
                more.append(self.send(x, rr, rc))
                yield
                clock.wait(more[-1])
        yield held + more, parts(0) + [(5 + m, 0) for m in range(len(more))]

    def sum_all(self, clock, v):
        for rr, rc in [(0, 1), *self.steps, (1, 0), (0, 2)]:
            got = self.send(v, rr, rc)
            yield
            clock.wait(got)
            if (rr, rc) != (0, 2):
                (v,) = clock.combine([v, got], [[[(0, i), (1, i)] for i in range(v.shape[0])]], f32)
        yield v, got


def shape(dims, dtype=f32):
    return jax.ShapeDtypeStruct(tuple(dims), dtype)


def dot(a, b, ca=1, cb=0):
    return lax.dot_general(a, b, (((ca,), (cb,)), ((), ())), preferred_element_type=f32)


def norm_parts(x):
    mean = jnp.mean(x, axis=-1, keepdims=True)
    centered = x - mean
    scale = lax.rsqrt(jnp.mean(centered * centered, axis=-1, keepdims=True) + norm_eps)
    return centered * scale, scale


def norm_back(x, gain, grad):
    unit, scale = norm_parts(x)
    gain_grad = jnp.sum(grad * unit, axis=0, keepdims=True)
    shift_grad = jnp.sum(grad, axis=0, keepdims=True)
    g = grad * gain
    moved = g - jnp.mean(g, axis=-1, keepdims=True) - unit * jnp.mean(g * unit, axis=-1, keepdims=True)
    return moved * scale, gain_grad, shift_grad


class Load:
    def __init__(self, s, me, refs, places, w, sems):
        self.w, self.sems = w, sems
        if places is None:
            for r in range(s.R):
                for c in range(s.C):
                    rc = me[1] ^ c
                    part = refs[0].at[r * s.C + c]
                    pltpu.make_async_copy(part, w.at[rc, :, pl.ds(r * s.u, s.u)], sems.at[rc]).start()
            return
        for ref, rels in zip(refs, places):
            for i, (rr, rc) in enumerate(rels):
                row = pl.multiple_of((me[0] ^ rr) * s.u, s.u)
                pltpu.make_async_copy(ref.at[i], w.at[rc, :, pl.ds(row, s.u)], sems.at[rc]).start()

    def wait(self, rc):
        pltpu.make_async_copy(self.w.at[rc], self.w.at[rc], self.sems.at[rc]).wait()


class Store:
    def __init__(self, s, me, refs, places, w, sems, first=0):
        self.first = first
        self.s, self.me, self.refs, self.places, self.w, self.sems = s, me, refs, places, w, sems

    def start(self, now):
        s, me = self.s, self.me
        if self.places is None:
            for r in range(s.R):
                to = self.refs[0].at[r * s.C + (me[1] ^ now)]
                pltpu.make_async_copy(self.w.at[now, :, pl.ds(r * s.u, s.u)], to, self.sems.at[now]).start()
            return
        for ref, rels in zip(self.refs, self.places):
            for i, (rr, rc) in enumerate(rels):
                if rc == now:
                    row = pl.multiple_of((me[0] ^ rr) * s.u, s.u)
                    to = ref.at[i, pl.ds(self.first, self.w.shape[1])]
                    pltpu.make_async_copy(self.w.at[rc, :, pl.ds(row, s.u)], to, self.sems.at[rc]).start()

    def wait(self, rc):
        pltpu.make_async_copy(self.w.at[rc], self.w.at[rc], self.sems.at[rc]).wait()


class Sizes:
    def __init__(self, net, tok, d, ff):
        self.net, self.tok, self.d, self.ff = net, tok, d, ff
        self.R, self.C = net.rows, net.cols
        self.u = d // self.R
        self.qc, self.oc, self.fc = 3 * d // self.C, d // self.C, ff // self.C
        self.an = self.qc + self.oc
        self.heads = d // HEAD_DIM


def attend_in(s, layer, places, n, me, x, vec, qb, cos, sin, mask, *refs):
    pieces, refs = refs[:n], refs[n:]
    mid, ffn, qkv_t, ctx_t, lse, w, proj_t, sems = refs
    load = Load(s, me, pieces, places, w, sems)
    hidden = x[...].astype(f32)
    unit, _ = norm_parts(hidden)
    normed = (unit * vec[layer, 0:1] + vec[layer, 1:2]).astype(bf16)
    for rc in range(s.C):
        load.wait(rc)
        c = me[1] ^ rc
        part = dot(normed, w[rc, 0, :, : s.qc]) + qb[layer, c]
        proj_t[pl.ds(pl.multiple_of(c * s.qc, 8), s.qc), :] = part.T
    cosine, sine = cos[...], sin[...]
    hh = HEAD_DIM // 2
    scaling = HEAD_DIM ** (-0.5)
    for h in range(2 * s.heads):
        a = h * HEAD_DIM
        u1, u2 = proj_t[a : a + hh, :], proj_t[a + hh : a + 2 * hh, :]
        r1, r2 = u1 * cosine - u2 * sine, u2 * cosine + u1 * sine
        if h < s.heads:
            r1, r2 = r1 * scaling, r2 * scaling
        qkv_t[a : a + HEAD_DIM, :] = jnp.concatenate([r1, r2], axis=0).astype(bf16)
    qkv_t[2 * s.d :, :] = proj_t[2 * s.d :, :].astype(bf16)

    def heads(step, carry):
        for k in range(HEADS_A_STEP):
            h = step * HEADS_A_STEP + k
            at = pl.multiple_of(h * HEAD_DIM, HEAD_DIM)
            q = qkv_t[pl.ds(at, HEAD_DIM), :]
            key = qkv_t[pl.ds(s.d + at, HEAD_DIM), :]
            val = qkv_t[pl.ds(2 * s.d + at, HEAD_DIM), :]
            scores = dot(key, q, 0, 0) + mask[...]
            peak = jnp.max(scores, axis=0, keepdims=True)
            e = jnp.exp(scores - peak)
            total = jnp.sum(e, axis=0, keepdims=True)
            out = dot(val, e.astype(bf16)) * (1.0 / total)
            ctx_t[pl.ds(at, HEAD_DIM), :] = out.astype(bf16)
            lse[h] = peak + jnp.log(total)
        return carry

    lax.fori_loop(0, s.heads // HEADS_A_STEP, heads, 0)
    att_t = jnp.zeros((s.d, s.tok), f32)
    for rc in range(s.C):
        c = me[1] ^ rc
        att_t += dot(w[rc, 0, :, s.qc :], ctx_t[pl.ds(pl.multiple_of(c * s.oc, 8), s.oc), :])
    middle = hidden + att_t.T + vec[layer, 5:6]
    mid[...] = middle
    unit, _ = norm_parts(middle)
    ffn[...] = (unit * vec[layer, 6:7] + vec[layer, 7:8]).astype(bf16)


def put_row(ref, at, row):
    n = row.shape[1]
    if n % 128:
        row = jnp.concatenate([row, jnp.zeros((1, -n % 128), f32)], axis=1)
    ref[at, :, : row.shape[1]] = row


def copy_sums(old, new):
    if len(old.shape) == 4:
        new[...] = old[...]
    else:
        new[...] = jnp.zeros(new.shape, f32)


def gelu_parts(pre):
    phi = 0.5 * (1.0 + lax.erf(pre * SQRT_HALF))
    return pre * phi, phi + pre * (INV_SQRT_2PI * jnp.exp(-0.5 * pre * pre))


def ffn_forward(s, layer, places, n, me, mid, ffn, vec, hb, *refs):
    pieces, refs = refs[:n], refs[n:]
    out, act, slope, w, sems = refs
    load = Load(s, me, pieces, places, w, sems)
    total = mid[...] + vec[layer, 12:13]
    for rc in range(s.C):
        load.wait(rc)
        pre = dot(ffn[...], w[rc, 0]) + hb[layer, me[1] ^ rc]
        value, back = gelu_parts(pre)
        value = value.astype(bf16)
        act[rc], slope[rc] = value, back
        total += dot(value, w[rc, 1], 1, 1)
    out[...] = total


def ffn_backward(s, layer, places, puts, n, with_forward, me, gx, mid, ffn, vec, hb, sums, *refs):
    pieces, refs = refs[:n], refs[n:]
    if with_forward:
        out, refs = refs[0], refs[1:]
    else:
        act, slope, refs = refs[0], refs[1], refs[4:]
    g_mid, new_sums, *parts, w, dw, sems, out_sems = refs
    copy_sums(sums, new_sums)
    vec_grad = new_sums.at[2 * layer + 1]
    load = Load(s, me, pieces, places, w, sems)
    store = Store(s, me, parts, puts, dw, out_sems, 0 if with_forward else 1)
    g_in = gx[...].astype(f32)
    g = g_in.astype(bf16)
    g_t, ffn_t = g_in.T.astype(bf16), ffn[...].T
    total = mid[...] + vec[layer, 12:13] if with_forward else None
    g_ffn = jnp.zeros((s.tok, s.d), f32)
    for rc in range(s.C):
        load.wait(rc)
        up, down = w[rc, 0], w[rc, 1]
        if with_forward:
            value, back = gelu_parts(dot(ffn[...], up) + hb[layer, me[1] ^ rc])
            value = value.astype(bf16)
            total += dot(value, down, 1, 1)
        else:
            value, back = act[rc], slope[rc]
        g_pre = (dot(g, down) * back).astype(bf16)
        put_row(vec_grad, 4 + (me[1] ^ rc), jnp.sum(g_pre.astype(f32), axis=0, keepdims=True))
        dw[rc, 0] = dot(ffn_t, g_pre).astype(bf16)
        dw[rc, 1] = dot(g_t, value).astype(bf16)
        store.start(rc)
        g_ffn += dot(g_pre, up, 1, 1)
    if with_forward:
        out[...] = total
    moved, gain_grad, shift_grad = norm_back(mid[...], vec[layer, 6:7], g_ffn)
    middle_grad = g_in + moved
    g_mid[...] = middle_grad
    vec_grad[0] = jnp.sum(g.astype(f32), axis=0, keepdims=True)
    vec_grad[1] = gain_grad
    vec_grad[2] = shift_grad
    vec_grad[3] = jnp.sum(middle_grad.astype(bf16).astype(f32), axis=0, keepdims=True)
    for rc in range(s.C):
        store.wait(rc)


def attend_back(s, layer, places, puts, n, me, g_mid, x, vec, cos, sin, mask, qkv_t, ctx_t, lse, sums, *refs):
    pieces, refs = refs[:n], refs[n:]
    g_in, new_sums, *parts, w, dw, gp_t, gctx_t, graw, sems, out_sems = refs
    copy_sums(sums, new_sums)
    vec_grad = new_sums.at[2 * layer]
    load = Load(s, me, pieces, places, w, sems)
    store = Store(s, me, parts, puts, dw, out_sems)
    hidden = x[...].astype(f32)
    unit, _ = norm_parts(hidden)
    normed_t = (unit * vec[layer, 0:1] + vec[layer, 1:2]).T.astype(bf16)
    g_att = g_mid[...].astype(bf16)
    g_att_t = g_mid[...].T.astype(bf16)
    for rc in range(s.C):
        load.wait(rc)
        at = pl.multiple_of((me[1] ^ rc) * s.oc, 8)
        dw[rc, 0, :, s.qc :] = dot(g_att_t, ctx_t[pl.ds(at, s.oc), :], 1, 1).astype(bf16)
        gctx_t[pl.ds(at, s.oc), :] = dot(g_att, w[rc, 0, :, s.qc :]).T.astype(bf16)

    def heads(step, carry):
        for k in range(HEADS_A_STEP):
            h = step * HEADS_A_STEP + k
            at = pl.multiple_of(h * HEAD_DIM, HEAD_DIM)
            q = qkv_t[pl.ds(at, HEAD_DIM), :]
            key = qkv_t[pl.ds(s.d + at, HEAD_DIM), :]
            val = qkv_t[pl.ds(2 * s.d + at, HEAD_DIM), :]
            gc = gctx_t[pl.ds(at, HEAD_DIM), :]
            p = jnp.exp(dot(key, q, 0, 0) + mask[...] - lse[h])
            g_p = dot(val, gc, 0, 0)
            inner = jnp.sum(g_p * p, axis=0, keepdims=True)
            g_s = (p * (g_p - inner)).astype(bf16)
            graw[pl.ds(at, HEAD_DIM), :] = dot(key, g_s)
            graw[pl.ds(s.d + at, HEAD_DIM), :] = dot(q, g_s, 1, 1)
            gp_t[pl.ds(2 * s.d + at, HEAD_DIM), :] = dot(gc, p.astype(bf16), 1, 1).astype(bf16)
        return carry

    lax.fori_loop(0, s.heads // HEADS_A_STEP, heads, 0)
    cosine, sine = cos[...], sin[...]
    hh = HEAD_DIM // 2
    scaling = HEAD_DIM ** (-0.5)
    for h in range(2 * s.heads):
        a = h * HEAD_DIM
        u1, u2 = graw[a : a + hh, :], graw[a + hh : a + 2 * hh, :]
        if h < s.heads:
            u1, u2 = u1 * scaling, u2 * scaling
        both = jnp.concatenate([u1 * cosine + u2 * sine, u2 * cosine - u1 * sine], axis=0)
        gp_t[a : a + HEAD_DIM, :] = both.astype(bf16)
    g_normed_t = jnp.zeros((s.d, s.tok), f32)
    ones = jnp.ones((8, s.tok), bf16)
    for rc in range(s.C):
        c = me[1] ^ rc
        part = gp_t[pl.ds(pl.multiple_of(c * s.qc, 8), s.qc), :]
        dw[rc, 0, :, : s.qc] = dot(normed_t, part, 1, 1).astype(bf16)
        store.start(rc)
        put_row(vec_grad, 4 + c, dot(ones, part, 1, 1)[0:1])
        g_normed_t += dot(w[rc, 0, :, : s.qc], part)
    moved, gain_grad, shift_grad = norm_back(hidden, vec[layer, 0:1], g_normed_t.T)
    g_in[...] = g_mid[...] + moved
    vec_grad[0] = gain_grad
    vec_grad[1] = shift_grad
    for rc in range(s.C):
        store.wait(rc)


SPACES = {"s": pltpu.SMEM, "v": VMEM, "a": HBM}


def specs(kinds):
    return [pl.BlockSpec(memory_space=SPACES[k]) for k in kinds]


def set_up(s, clock, segment_ids, vectors):
    def kernel(seg, vec_in, mask, vec, qb, hb):
        row = jnp.broadcast_to(seg[...].astype(f32), mask.shape)
        mask[...] = jnp.where(row == row.T, 0.0, -1e30)
        for l in range(LAYERS):
            for i in range(13):
                vec[l, i : i + 1] = vec_in[i, l : l + 1]
            rows = jnp.concatenate([vec_in[i, l : l + 1] for i in range(2, 5)], axis=1)
            hidden = jnp.concatenate([vec_in[i, l : l + 1] for i in range(8, 12)], axis=1)
            for c in range(s.C):
                qb[l, c] = rows[:, c * s.qc : (c + 1) * s.qc]
                hb[l, c] = hidden[:, c * s.fc : (c + 1) * s.fc]

    kinds = [(s.tok, s.tok), (LAYERS, 13, s.d), (LAYERS, s.C, 1, s.qc), (LAYERS, s.C, 1, s.fc)]
    return clock.call(kernel, (segment_ids, vectors), specs("vv"), [shape(k) for k in kinds], specs("vvvv"))


def update_vectors(s, clock, sums, more, states):
    def kernel(a, b, w, m, v, *outs):
        total = a[...] + b[...]
        for l in range(LAYERS):
            at, ff = total[2 * l], total[2 * l + 1]
            qkv = jnp.concatenate([at[4 + c, :, : s.qc] for c in range(s.C)], axis=1)
            hid = jnp.concatenate([ff[4 + c, :, : s.fc] for c in range(s.C)], axis=1)
            rows = [at[0], at[1]] + [qkv[:, i * s.d : (i + 1) * s.d] for i in range(3)]
            rows += [ff[3], ff[1], ff[2]] + [hid[:, i * s.d : (i + 1) * s.d] for i in range(4)] + [ff[0]]
            for i, grad in enumerate(rows):
                old = [r[i, l : l + 1] for r in (w, m, v)]
                for out, new in zip(outs, adamw(old[0], grad, old[1], old[2], 0.1, float(STEP))):
                    out[i, l : l + 1] = new

    return clock.call(kernel, (sums, more, *states), specs("vvvvv"), [shape(a.shape) for a in states], specs("vvv"), vmem=24)


def prepare(s, clock, jobs, weights):
    pairs = [(l, {"a": 0, "f": 2}[kind]) for l, kind in jobs]

    def kernel(*refs):
        ins, outs, bufs, sems = refs[:4], refs[4 : 4 + len(jobs)], refs[4 + len(jobs) : -1], refs[-1]
        copies = [
            pltpu.make_async_copy(ins[i + k].at[l], bufs[2 * j + k], sems.at[j, k])
            for j, (l, i) in enumerate(pairs)
            for k in range(2)
        ]
        for c in copies:
            c.start()
        for j, (_, i) in enumerate(pairs):
            for c in copies[2 * j : 2 * j + 2]:
                c.wait()
            first, second = bufs[2 * j : 2 * j + 2]
            if i == 0:
                outs[j][0, :, : s.qc] = first[...].astype(bf16)
                outs[j][0, :, s.qc :] = second[...].T.astype(bf16)
            else:
                outs[j][0] = first[...].astype(bf16)
                outs[j][1] = second[...].astype(bf16)

    sizes = [(1, s.u, s.an) if i == 0 else (2, s.u, s.fc) for _, i in pairs]
    return clock.call(
        kernel,
        weights,
        specs("aaaa"),
        [shape(k, bf16) for k in sizes],
        specs("v" * len(jobs)),
        [VMEM(weights[i + k].shape[1:], f32) for _, i in pairs for k in range(2)]
        + [pltpu.SemaphoreType.DMA((len(jobs), 2))],
    )


def adamw(weight, gradient, first, second, rate, step_count):
    first_new = beta_one * first + (1.0 - beta_one) * gradient
    second_new = beta_two * second + (1.0 - beta_two) * gradient * gradient
    first_hat = first_new / (1.0 - beta_one**step_count)
    second_hat = second_new / (1.0 - beta_two**step_count)
    weight_new = weight - rate * (first_hat / (jnp.sqrt(second_hat) + adam_eps) + decay_rate * weight)
    return (weight_new, first_new, second_new)


def update(clock, arrays, jobs, states, before):
    more = [] if before is None else list(before)
    n, na = len(states), len(arrays)
    wanted = [sorted({j for job in jobs for a, j in job[4] if a == i}) for i in range(na)]
    moves = [(k, i) for k, job in enumerate(jobs) for i in range(3 * job[1], 3 * job[1] + 3)]

    def kernel(*refs):
        grads, refs = refs[:na], refs[na:]
        ins, refs = refs[:n], refs[n + len(more) :]
        outs, refs = refs[:n], refs[n:]
        g_bufs, refs = refs[:na], refs[na:]
        bufs, news, sems = refs[: len(moves)], refs[len(moves) : 2 * len(moves)], refs[-1]
        first = [
            pltpu.make_async_copy(grads[i].at[j], g_bufs[i].at[at], sems.at[0, i, at])
            for i, js in enumerate(wanted)
            for at, j in enumerate(js)
        ]
        loads = [pltpu.make_async_copy(ins[i].at[jobs[k][0]], b, sems.at[1, q, 0]) for q, ((k, i), b) in enumerate(zip(moves, bufs))]
        saves = [pltpu.make_async_copy(b, outs[i].at[jobs[k][0]], sems.at[1, q, 1]) for q, ((k, i), b) in enumerate(zip(moves, news))]
        for c in first + loads:
            c.start()
        for c in first:
            c.wait()
        for k, (_, _, turned, rate, terms, part, columns) in enumerate(jobs):
            grad = sum(g_bufs[i][wanted[i].index(j), part].astype(f32) for i, j in terms)[:, columns]
            grad = grad.T if turned else grad
            for c in loads[3 * k : 3 * k + 3]:
                c.wait()
            w, m, v = (r[...] for r in bufs[3 * k : 3 * k + 3])
            for ref, new in zip(news[3 * k : 3 * k + 3], adamw(w, grad, m, v, rate, float(STEP))):
                ref[...] = new
            for c in saves[3 * k : 3 * k + 3]:
                c.start()
        for c in saves:
            c.wait()

    sizes = [VMEM(states[i].shape[1:], f32) for _, i in moves]
    return clock.call(
        kernel,
        (*arrays, *states, *more),
        [pl.BlockSpec(memory_space=pl.ANY)] * na + specs("a" * (n + len(more))),
        [shape(a.shape) for a in states],
        specs("a" * n),
        [VMEM((len(js),) + a.shape[1:], a.dtype) for js, a in zip(wanted, arrays)]
        + sizes
        + sizes
        + [pltpu.SemaphoreType.DMA((2, max(len(moves), na), max(2, *(len(js) for js in wanted))))],
        {na + n + i: i for i in range(len(more))},
    )


def rotary_tables(segment_ids):
    seg = segment_ids[0]
    start = jnp.sum((seg[:, None] < seg[None, :]).astype(jnp.int32), axis=0)
    places = jnp.arange(seg.shape[0], dtype=jnp.int32) - start
    freq_index = jnp.arange(HEAD_DIM // 2, dtype=f32)
    inverse = jnp.exp(freq_index * (-2.0 * math.log(10000.0) / HEAD_DIM))
    angles = inverse[:, None] * places.astype(f32)[None, :]
    return jnp.cos(angles), jnp.sin(angles)


def shards(
    rows,
    cols,
    residues,
    segment_ids,
    cotangent,
    qkv_weight,
    qkv_first,
    qkv_second,
    out_weight,
    out_first,
    out_second,
    up_weight,
    up_first,
    up_second,
    down_weight,
    down_first,
    down_second,
    vectors,
    vector_first,
    vector_second,
):
    net = Net(rows, cols)
    tok, d = residues.shape
    s = Sizes(net, tok, d, up_weight.shape[2] * cols)
    me = jnp.stack([lax.axis_index("rows"), lax.axis_index("cols")]).astype(jnp.int32)
    down_weight, down_first, down_second = (jnp.swapaxes(a, 1, 2) for a in (down_weight, down_first, down_second))
    cos, sin = rotary_tables(segment_ids)
    act = (tok, d)
    g = net.g
    sem = pltpu.SemaphoreType.DMA((cols,))
    packed = (2 * LAYERS, 4 + cols, 1, d)
    clock = Clock()

    def grads(unit, puts):
        sizes = [(rows * cols,)] if puts is None else [(len(p),) for p in puts]
        return [shape(k + unit, bf16) for k in sizes]

    def attend_forward(l, places, full, hidden):
        n = len(full)
        return clock.call(
            functools.partial(attend_in, s, l, places, n),
            (me, hidden, vec, qb, cos, sin, mask, *full),
            specs("s" + "v" * 6 + "a" * n),
            [shape(act), shape(act, bf16), shape((3 * d, tok), bf16), shape((d, tok), bf16), shape((s.heads, 1, tok))],
            specs("vvvvv"),
            [VMEM((cols, 1, d, s.an), bf16), VMEM((3 * d, tok), f32), sem],
        )

    def feed_forward(l, places, full, mid, ffn):
        n = len(full)
        return clock.call(
            functools.partial(ffn_forward, s, l, places, n),
            (me, mid, ffn, vec, hb, *full),
            specs("s" + "v" * 4 + "a" * n),
            [shape(act), shape((cols, tok, s.fc), bf16), shape((cols, tok, s.fc))],
            specs("vvv"),
            [VMEM((cols, 2, d, s.fc), bf16), sem],
        )

    def feed_back(l, places, puts, full, gx, mid, ffn, sums, kept):
        last, n = not kept, len(full)
        parts = grads((2 if last else 3, s.u, s.fc), puts)
        return clock.call(
            functools.partial(ffn_backward, s, l, places, puts, n, last),
            (me, gx, mid, ffn, vec, hb, sums, *full, *kept),
            specs("s" + "v" * 6 + "a" * n + ("" if last else "vvaa")),
            ([shape(act)] if last else []) + [shape(act), shape(packed)] + parts,
            specs(("v" if last else "") + "vv" + "a" * len(parts)),
            [VMEM((cols, 2, d, s.fc), bf16), VMEM((cols, 2, d, s.fc), bf16), sem, sem],
            {} if last else {n + 9: 2, n + 10: 3},
        )

    def attend_backward(l, places, puts, full, g_mid, hidden_in, qkv_t, ctx_t, lse, sums):
        n = len(full)
        parts = grads((1 if l == 0 else 3, s.u, s.an), puts)
        return clock.call(
            functools.partial(attend_back, s, l, places, puts, n),
            (me, g_mid, hidden_in, vec, cos, sin, mask, qkv_t, ctx_t, lse, sums, *full),
            specs("s" + "v" * 10 + "a" * n),
            [shape(act), shape(packed)] + parts,
            specs("vv" + "a" * len(parts)),
            [
                VMEM((cols, 1, d, s.an), bf16),
                VMEM((cols, 1, d, s.an), bf16),
                VMEM((3 * d, tok), bf16),
                VMEM((d, tok), bf16),
                VMEM((2 * d, tok), f32),
                sem,
                sem,
            ],
        )

    a_states = (qkv_weight, qkv_first, qkv_second, out_weight, out_first, out_second)
    f_states = (up_weight, up_first, up_second, down_weight, down_first, down_second)
    rate_qkv = 0.5 / math.sqrt(d)
    rate_out = 0.5 / math.sqrt(max(d * 4 // TOK_DEV, 1))
    rate_down = 0.5 / math.sqrt(s.ff)

    states = a_states + f_states

    def jobs_a(l, terms):
        return [(l, 0, False, rate_qkv, terms, 0, slice(0, s.qc)), (l, 1, True, rate_out, terms, 0, slice(s.qc, s.an))]

    def jobs_f(l, terms, part):
        whole = slice(0, s.fc)
        return [(l, 2, False, rate_qkv, terms, part, whole), (l, 3, False, rate_down, terms, part + 1, whole)]

    def steps(gen, n):
        for _ in range(n):
            out = next(gen)
        return out

    def finish(gen):
        for out in gen:
            if out is not None:
                return out

    weights = (qkv_weight, out_weight, up_weight, down_weight)
    (a0,) = prepare(s, clock, [(0, "a")], weights)
    at, at_last = net.gather_rels(), net.gather_rels(True)
    near = len(net.steps)
    a0 = net.gather(clock, a0[None], None)
    vec_states = [jnp.swapaxes(a, 0, 1) for a in (vectors, vector_first, vector_second)]
    steps(a0, 1)
    mask, vec, qb, hb = set_up(s, clock, segment_ids, vec_states[0])
    steps(a0, near - 1)
    f0, a1, f1 = prepare(s, clock, [(0, "f"), (1, "a"), (1, "f")], weights)
    f0, a1, f1 = net.gather(clock, f0[None]), net.gather(clock, a1[None]), net.gather(clock, f1[None], LONG, True)
    steps(f0, 1)
    steps(a1, 1)
    steps(a0, 1)
    steps(f0, near - 1)
    steps(a0, 1)
    steps(a1, near - 1)
    steps(a0, 1)
    steps(f0, 1)
    steps(f1, 1)
    steps(a1, 1)
    a0_full = finish(a0)
    mid0, ffn0, qkv0, ctx0, lse0 = attend_forward(0, at, a0_full, residues)
    steps(f0, 1)
    steps(f1, near - 1)
    steps(a1, 1)
    steps(f0, 1)
    steps(f1, 1)
    f0_full = finish(f0)
    hidden1, value0, slope0 = feed_forward(0, at, f0_full, mid0, ffn0)
    steps(a1, 1)
    a1_full = finish(a1)
    steps(f1, 1)
    mid1, ffn1, qkv1, ctx1, lse1 = attend_forward(1, at, a1_full, hidden1)
    f1_full = finish(f1)

    put = net.reduce_rels()
    none = jnp.zeros((1, d), f32)
    block_out, g_mid1, sums, *parts = feed_back(1, at_last, put, f1_full, cotangent, mid1, ffn1, none, ())
    f1 = net.reduce(clock, *parts, slow=(LONGER, LONG), vmem=(60, 60))
    steps(f1, 1)
    gx1, sums, *parts = attend_backward(1, at, put, a1_full, g_mid1, hidden1, qkv1, ctx1, lse1, sums)
    steps(f1, 1)
    g_mid0, sums, *parts = feed_back(0, at, put, f0_full, gx1, mid0, ffn0, sums, (value0, slope0, *parts))
    mixed = net.reduce(clock, *parts, slow=(LONGER, None), vmem=(60, 24))
    steps(mixed, 1)
    steps(f1, 2)
    steps(mixed, 1)
    gx0, sums, *parts = attend_backward(0, at, put, a0_full, g_mid0, residues, qkv0, ctx0, lse0, sums)
    a0 = net.reduce(clock, *parts, True)
    vec_sum = net.sum_all(clock, sums)
    steps(a0, 1)
    steps(f1, 1)
    steps(mixed, 1)
    steps(f1, near - 1)
    steps(mixed, 1)
    steps(a0, 1)
    steps(vec_sum, 2)
    f1_arrays, f1_terms = finish(f1)
    steps(vec_sum, near)
    steps(mixed, 1)
    steps(a0, 1)
    steps(a0, 1)
    steps(mixed, near - 1)
    steps(vec_sum, 1)
    arrays, terms = finish(a0)
    jobs = jobs_a(0, terms) + jobs_f(1, [(len(arrays) + a, i) for a, i in f1_terms], 0)
    states_new = update(clock, [*arrays, *f1_arrays], jobs, states, None)
    vec_new = update_vectors(s, clock, *finish(vec_sum), vec_states)
    arrays, terms = finish(mixed)
    states_new = list(update(clock, arrays, jobs_a(1, terms) + jobs_f(0, terms, 1), states, states_new))
    states_new[9:] = [jnp.swapaxes(a, 1, 2) for a in states_new[9:]]
    return (block_out, gx0, *states_new, *(jnp.swapaxes(a, 0, 1) for a in vec_new))


def solution(mesh):
    rows, cols = mesh.shape["rows"], mesh.shape["cols"]
    tokens = P(("rows", "cols"), None)
    wide, tall = P(None, "rows", "cols"), P(None, "cols", "rows")
    states = (wide,) * 3 + (tall,) * 3 + (wide,) * 3 + (tall,) * 3
    return jax.shard_map(
        functools.partial(shards, rows, cols),
        mesh=mesh,
        in_specs=(tokens, tokens, tokens) + states + (P(),) * 3,
        out_specs=(tokens, tokens) + states + (P(),) * 3,
        check_vma=False,
    )
```

```python
import functools
import math

import jax
import jax.numpy as jnp
from jax import lax
from jax.experimental import pallas as pl
from jax.experimental.pallas import tpu as pltpu
from jax.sharding import PartitionSpec as P

HEAD_DIM = 32
LAYERS = 2
STEP = 5
TOK_DEV = 256

norm_eps = 1e-05
beta_one = 0.5
beta_two = 0.55
adam_eps = 1e-08
decay_rate = 0.01

f32 = jnp.float32
bf16 = jnp.bfloat16
VMEM = pltpu.VMEM
HBM = pltpu.HBM
SQRT_HALF = math.sqrt(0.5)
INV_SQRT_2PI = 1.0 / math.sqrt(2.0 * math.pi)
HEADS_A_STEP = 20
LONG, LONGER = 2 * 10**10, 10**12


class Clock:
    def __init__(self):
        self.before = []

    def wait(self, *xs):
        self.before += list(xs)
        return list(xs)

    def call(self, kernel, args, in_specs, outs, out_specs, scratch=(), aliases=None, flops=10**6, vmem=60):
        known = {id(x) for x in args}
        more = [x for x in self.before if id(x) not in known]
        n, extra = len(args), len(more)

        def body(*refs):
            kernel(*refs[:n], *refs[n + extra :])

        results = pl.pallas_call(
            body,
            in_specs=list(in_specs) + [pl.BlockSpec(memory_space=pl.ANY)] * extra,
            out_specs=list(out_specs),
            out_shape=list(outs),
            scratch_shapes=list(scratch),
            input_output_aliases=aliases or {},
            compiler_params=pltpu.CompilerParams(vmem_limit_bytes=vmem * 2**20),
            cost_estimate=pl.CostEstimate(flops=flops, bytes_accessed=10**5, transcendentals=0),
        )(*args, *more)
        self.before = [results[0]]
        return results

    def combine(self, arrays, outs, dtype=bf16, long=None, vmem=16):
        wanted = [sorted({j for o in outs for terms in o for a, j in terms if a == i}) for i in range(len(arrays))]
        runs = []
        for i, js in enumerate(wanted):
            for at, j in enumerate(js):
                if at and js[at - 1] == j - 1:
                    runs[-1][3] += 1
                else:
                    runs.append([i, j, at, 1])
        unit = arrays[0].shape[1:]

        def kernel(*refs):
            ins, out_refs = refs[: len(arrays)], refs[len(arrays) : len(arrays) + len(outs)]
            bufs, sems = refs[-1 - len(arrays) : -1], refs[-1]
            copies = [
                pltpu.make_async_copy(ins[i].at[pl.ds(j, k)], bufs[i].at[pl.ds(at, k)], sems.at[r])
                for r, (i, j, at, k) in enumerate(runs)
            ]
            for c in copies:
                c.start()
            for c in copies:
                c.wait()
            for ref, units in zip(out_refs, outs):
                for to, terms in enumerate(units):
                    values = [bufs[i][wanted[i].index(j)] for i, j in terms]
                    if len(values) > 1:
                        values = [sum(v.astype(f32) for v in values)]
                    ref[to] = values[0].astype(dtype)

        return self.call(
            kernel,
            arrays,
            [pl.BlockSpec(memory_space=pl.ANY)] * len(arrays),
            [shape((len(o),) + unit, dtype) for o in outs],
            [pl.BlockSpec(memory_space=VMEM)] * len(outs),
            [VMEM((len(js),) + unit, a.dtype) for js, a in zip(wanted, arrays)] + [pltpu.SemaphoreType.DMA((len(runs),))],
            flops=long or 10**6,
            vmem=vmem,
        )


class Net:
    def __init__(self, rows, cols):
        self.rows, self.cols = rows, cols
        bits = [(0, 1 << k) for k in range(2, cols.bit_length() - 1)] + [(1 << k, 0) for k in range(1, rows.bit_length() - 1)]
        self.steps = bits[::-1]
        self.group = [(0, 0)]
        for rr, rc in self.steps:
            self.group += [(r ^ rr, c ^ rc) for r, c in self.group]
        self.g = len(self.group)
        self.half = self.g // 2

    def send(self, x, rr, rc):
        mask = rr * self.cols + rc
        pairs = [(i, i ^ mask) for i in range(self.rows * self.cols)]
        return lax.ppermute(x, ("rows", "cols"), pairs)

    def rels(self, kind, core):
        dr, dc = {"o": (0, 0), "x": (1, 0), "y": (0, 2), "d": (1, 2)}[kind]
        return [(rr ^ dr, rc ^ dc ^ core) for rr, rc in self.group]

    def gather(self, clock, x, slow=LONG, one=False):
        g, h = self.g, self.half
        for rr, rc in self.steps:
            got = self.send(x, rr, rc)
            yield
            clock.wait(got)
            k = x.shape[0]
            (x,) = clock.combine([x, got], [[[(0, i)] for i in range(k)] + [[(1, i)] for i in range(k)]], long=slow)
        own = x
        xr, yr = self.send(own, 1, 0), self.send(own, 0, 2)
        yield
        clock.wait(xr, yr)
        xh, yh = clock.combine([xr, yr], [[[(0, i)] for i in range(h)], [[(1, i)] for i in range(h, g)]], long=slow)
        d0, d1 = self.send(xh, 0, 2), self.send(yh, 1, 0)
        (near,) = clock.combine([own, xr, yr], [[[(a, i)] for a in range(3) for i in range(g)]])
        far = self.send(near, 0, 1)
        yield
        clock.wait(d0, d1)
        rest = [d0, d1]
        if one:
            rest = clock.combine(rest, [[[(a, i)] for a in range(2) for i in range(h)]])
        far_rest = [self.send(r, 0, 1) for r in rest]
        yield
        clock.wait(far, *far_rest)
        yield [near, *rest, far, *far_rest]

    def gather_rels(self, one=False):
        places = []
        for core in (0, 1):
            o, x, y, d = (self.rels(k, core) for k in "oxyd")
            places += [o + x + y, d] if one else [o + x + y, d[: self.half], d[self.half :]]
        return places

    def reduce_rels(self):
        return [sum([self.rels(k, core) for k in "dxyo"], []) for core in (1, 0)]

    def reduce(self, clock, far, keep, fast=False, slow=(None, None), vmem=(24, 24)):
        g, h = self.g, self.half
        got = self.send(far, 0, 1)
        yield
        clock.wait(got)

        def both(at, n):
            return [[(0, i), (1, i)] for i in range(at, at + n)]

        away = [both(0, h) + both(g, h), both(h, h) + both(2 * g + h, h)]
        stay = [both(g + h, g) + both(3 * g, g)]
        if fast:
            to_x, to_y, rest = clock.combine([keep, got], away + stay, vmem=vmem[0])
        else:
            to_x, to_y = clock.combine([keep, got], away, vmem=vmem[0])
        from_x, from_y = self.send(to_x, 1, 0), self.send(to_y, 0, 2)
        yield
        if not fast:
            (rest,) = clock.combine([keep, got], stay, vmem=vmem[0])
            yield
        clock.wait(from_x, from_y)
        x1, y0 = clock.combine(
            [rest, from_x, from_y],
            [[[(0, i), (2, i)] for i in range(h)], [[(0, h + i), (1, i)] for i in range(h)]],
            long=slow[0],
            vmem=vmem[1],
        )
        x1, y0 = self.send(x1, 1, 0), self.send(y0, 0, 2)
        yield
        clock.wait(x1, y0)
        held = [rest, from_x, from_y, x1, y0]

        def parts(i):
            near = [(1, h + i), (4, i)] if i < h else [(3, i - h), (2, i)]
            return [(0, g + i)] + near

        if fast:
            sent = clock.combine(held, [[parts(i)] for i in range(1, g)], vmem=vmem[1])
            more = [self.send(t, rr, rc) for t, (rr, rc) in zip(sent, self.group[1:])]
            yield
            clock.wait(*more)
        else:
            n, more = g, []
            for rr, rc in reversed(self.steps):
                n //= 2
                units = [parts(i) + [(5 + m, i) for m in range(len(more))] for i in range(n, 2 * n)]
                (x,) = clock.combine(held + more, [units], long=None if more else slow[1], vmem=vmem[1])
                more.append(self.send(x, rr, rc))
                yield
                clock.wait(more[-1])
        yield held + more, parts(0) + [(5 + m, 0) for m in range(len(more))]

    def sum_all(self, clock, v):
        for rr, rc in [(0, 1), *self.steps, (1, 0), (0, 2)]:
            got = self.send(v, rr, rc)
            yield
            clock.wait(got)
            if (rr, rc) != (0, 2):
                (v,) = clock.combine([v, got], [[[(0, i), (1, i)] for i in range(v.shape[0])]], f32)
        yield v, got


def shape(dims, dtype=f32):
    return jax.ShapeDtypeStruct(tuple(dims), dtype)


def dot(a, b, ca=1, cb=0):
    return lax.dot_general(a, b, (((ca,), (cb,)), ((), ())), preferred_element_type=f32)


def norm_parts(x):
    mean = jnp.mean(x, axis=-1, keepdims=True)
    centered = x - mean
    scale = lax.rsqrt(jnp.mean(centered * centered, axis=-1, keepdims=True) + norm_eps)
    return centered * scale, scale


def norm_back(x, gain, grad):
    unit, scale = norm_parts(x)
    gain_grad = jnp.sum(grad * unit, axis=0, keepdims=True)
    shift_grad = jnp.sum(grad, axis=0, keepdims=True)
    g = grad * gain
    moved = g - jnp.mean(g, axis=-1, keepdims=True) - unit * jnp.mean(g * unit, axis=-1, keepdims=True)
    return moved * scale, gain_grad, shift_grad


class Load:
    def __init__(self, s, me, refs, places, w, sems):
        self.w, self.sems = w, sems
        if places is None:
            for r in range(s.R):
                for c in range(s.C):
                    rc = me[1] ^ c
                    part = refs[0].at[r * s.C + c]
                    pltpu.make_async_copy(part, w.at[rc, :, pl.ds(r * s.u, s.u)], sems.at[rc]).start()
            return
        for ref, rels in zip(refs, places):
            for i, (rr, rc) in enumerate(rels):
                row = pl.multiple_of((me[0] ^ rr) * s.u, s.u)
                pltpu.make_async_copy(ref.at[i], w.at[rc, :, pl.ds(row, s.u)], sems.at[rc]).start()

    def wait(self, rc):
        pltpu.make_async_copy(self.w.at[rc], self.w.at[rc], self.sems.at[rc]).wait()


class Store:
    def __init__(self, s, me, refs, places, w, sems, first=0):
        self.first = first
        self.s, self.me, self.refs, self.places, self.w, self.sems = s, me, refs, places, w, sems

    def start(self, now):
        s, me = self.s, self.me
        if self.places is None:
            for r in range(s.R):
                to = self.refs[0].at[r * s.C + (me[1] ^ now)]
                pltpu.make_async_copy(self.w.at[now, :, pl.ds(r * s.u, s.u)], to, self.sems.at[now]).start()
            return
        for ref, rels in zip(self.refs, self.places):
            for i, (rr, rc) in enumerate(rels):
                if rc == now:
                    row = pl.multiple_of((me[0] ^ rr) * s.u, s.u)
                    to = ref.at[i, pl.ds(self.first, self.w.shape[1])]
                    pltpu.make_async_copy(self.w.at[rc, :, pl.ds(row, s.u)], to, self.sems.at[rc]).start()

    def wait(self, rc):
        pltpu.make_async_copy(self.w.at[rc], self.w.at[rc], self.sems.at[rc]).wait()


class Sizes:
    def __init__(self, net, tok, d, ff):
        self.net, self.tok, self.d, self.ff = net, tok, d, ff
        self.R, self.C = net.rows, net.cols
        self.u = d // self.R
        self.qc, self.oc, self.fc = 3 * d // self.C, d // self.C, ff // self.C
        self.an = self.qc + self.oc
        self.heads = d // HEAD_DIM


def attend_in(s, layer, places, n, me, x, vec, qb, cos, sin, mask, *refs):
    pieces, refs = refs[:n], refs[n:]
    mid, ffn, qkv_t, ctx_t, lse, w, proj_t, sems = refs
    load = Load(s, me, pieces, places, w, sems)
    hidden = x[...].astype(f32)
    unit, _ = norm_parts(hidden)
    normed = (unit * vec[layer, 0:1] + vec[layer, 1:2]).astype(bf16)
    for rc in range(s.C):
        load.wait(rc)
        c = me[1] ^ rc
        part = dot(normed, w[rc, 0, :, : s.qc]) + qb[layer, c]
        proj_t[pl.ds(pl.multiple_of(c * s.qc, 8), s.qc), :] = part.T
    cosine, sine = cos[...], sin[...]
    hh = HEAD_DIM // 2
    scaling = HEAD_DIM ** (-0.5)
    for h in range(2 * s.heads):
        a = h * HEAD_DIM
        u1, u2 = proj_t[a : a + hh, :], proj_t[a + hh : a + 2 * hh, :]
        r1, r2 = u1 * cosine - u2 * sine, u2 * cosine + u1 * sine
        if h < s.heads:
            r1, r2 = r1 * scaling, r2 * scaling
        qkv_t[a : a + HEAD_DIM, :] = jnp.concatenate([r1, r2], axis=0).astype(bf16)
    qkv_t[2 * s.d :, :] = proj_t[2 * s.d :, :].astype(bf16)

    def heads(step, carry):
        for k in range(HEADS_A_STEP):
            h = step * HEADS_A_STEP + k
            at = pl.multiple_of(h * HEAD_DIM, HEAD_DIM)
            q = qkv_t[pl.ds(at, HEAD_DIM), :]
            key = qkv_t[pl.ds(s.d + at, HEAD_DIM), :]
            val = qkv_t[pl.ds(2 * s.d + at, HEAD_DIM), :]
            scores = dot(key, q, 0, 0) + mask[...]
            peak = jnp.max(scores, axis=0, keepdims=True)
            e = jnp.exp(scores - peak)
            total = jnp.sum(e, axis=0, keepdims=True)
            out = dot(val, e.astype(bf16)) * (1.0 / total)
            ctx_t[pl.ds(at, HEAD_DIM), :] = out.astype(bf16)
            lse[h] = peak + jnp.log(total)
        return carry

    lax.fori_loop(0, s.heads // HEADS_A_STEP, heads, 0)
    att_t = jnp.zeros((s.d, s.tok), f32)
    for rc in range(s.C):
        c = me[1] ^ rc
        att_t += dot(w[rc, 0, :, s.qc :], ctx_t[pl.ds(pl.multiple_of(c * s.oc, 8), s.oc), :])
    middle = hidden + att_t.T + vec[layer, 5:6]
    mid[...] = middle
    unit, _ = norm_parts(middle)
    ffn[...] = (unit * vec[layer, 6:7] + vec[layer, 7:8]).astype(bf16)


def put_row(ref, at, row):
    n = row.shape[1]
    if n % 128:
        row = jnp.concatenate([row, jnp.zeros((1, -n % 128), f32)], axis=1)
    ref[at, :, : row.shape[1]] = row


def copy_sums(old, new):
    if len(old.shape) == 4:
        new[...] = old[...]
    else:
        new[...] = jnp.zeros(new.shape, f32)


def gelu_parts(pre):
    phi = 0.5 * (1.0 + lax.erf(pre * SQRT_HALF))
    return pre * phi, phi + pre * (INV_SQRT_2PI * jnp.exp(-0.5 * pre * pre))


def ffn_forward(s, layer, places, n, me, mid, ffn, vec, hb, *refs):
    pieces, refs = refs[:n], refs[n:]
    out, act, slope, w, sems = refs
    load = Load(s, me, pieces, places, w, sems)
    total = mid[...] + vec[layer, 12:13]
    for rc in range(s.C):
        load.wait(rc)
        pre = dot(ffn[...], w[rc, 0]) + hb[layer, me[1] ^ rc]
        value, back = gelu_parts(pre)
        value = value.astype(bf16)
        act[rc], slope[rc] = value, back
        total += dot(value, w[rc, 1], 1, 1)
    out[...] = total


def ffn_backward(s, layer, places, puts, n, with_forward, me, gx, mid, ffn, vec, hb, sums, *refs):
    pieces, refs = refs[:n], refs[n:]
    if with_forward:
        out, refs = refs[0], refs[1:]
    else:
        act, slope, refs = refs[0], refs[1], refs[4:]
    g_mid, new_sums, *parts, w, dw, sems, out_sems = refs
    copy_sums(sums, new_sums)
    vec_grad = new_sums.at[2 * layer + 1]
    load = Load(s, me, pieces, places, w, sems)
    store = Store(s, me, parts, puts, dw, out_sems, 0 if with_forward else 1)
    g_in = gx[...].astype(f32)
    g = g_in.astype(bf16)
    g_t, ffn_t = g_in.T.astype(bf16), ffn[...].T
    total = mid[...] + vec[layer, 12:13] if with_forward else None
    g_ffn = jnp.zeros((s.tok, s.d), f32)
    for rc in range(s.C):
        load.wait(rc)
        up, down = w[rc, 0], w[rc, 1]
        if with_forward:
            value, back = gelu_parts(dot(ffn[...], up) + hb[layer, me[1] ^ rc])
            value = value.astype(bf16)
            total += dot(value, down, 1, 1)
        else:
            value, back = act[rc], slope[rc]
        g_pre = (dot(g, down) * back).astype(bf16)
        put_row(vec_grad, 4 + (me[1] ^ rc), jnp.sum(g_pre.astype(f32), axis=0, keepdims=True))
        dw[rc, 0] = dot(ffn_t, g_pre).astype(bf16)
        dw[rc, 1] = dot(g_t, value).astype(bf16)
        store.start(rc)
        g_ffn += dot(g_pre, up, 1, 1)
    if with_forward:
        out[...] = total
    moved, gain_grad, shift_grad = norm_back(mid[...], vec[layer, 6:7], g_ffn)
    middle_grad = g_in + moved
    g_mid[...] = middle_grad
    vec_grad[0] = jnp.sum(g.astype(f32), axis=0, keepdims=True)
    vec_grad[1] = gain_grad
    vec_grad[2] = shift_grad
    vec_grad[3] = jnp.sum(middle_grad.astype(bf16).astype(f32), axis=0, keepdims=True)
    for rc in range(s.C):
        store.wait(rc)


def attend_back(s, layer, places, puts, n, me, g_mid, x, vec, cos, sin, mask, qkv_t, ctx_t, lse, sums, *refs):
    pieces, refs = refs[:n], refs[n:]
    g_in, new_sums, *parts, w, dw, gp_t, gctx_t, graw, sems, out_sems = refs
    copy_sums(sums, new_sums)
    vec_grad = new_sums.at[2 * layer]
    load = Load(s, me, pieces, places, w, sems)
    store = Store(s, me, parts, puts, dw, out_sems)
    hidden = x[...].astype(f32)
    unit, _ = norm_parts(hidden)
    normed_t = (unit * vec[layer, 0:1] + vec[layer, 1:2]).T.astype(bf16)
    g_att = g_mid[...].astype(bf16)
    g_att_t = g_mid[...].T.astype(bf16)
    for rc in range(s.C):
        load.wait(rc)
        at = pl.multiple_of((me[1] ^ rc) * s.oc, 8)
        dw[rc, 0, :, s.qc :] = dot(g_att_t, ctx_t[pl.ds(at, s.oc), :], 1, 1).astype(bf16)
        gctx_t[pl.ds(at, s.oc), :] = dot(g_att, w[rc, 0, :, s.qc :]).T.astype(bf16)

    def heads(step, carry):
        for k in range(HEADS_A_STEP):
            h = step * HEADS_A_STEP + k
            at = pl.multiple_of(h * HEAD_DIM, HEAD_DIM)
            q = qkv_t[pl.ds(at, HEAD_DIM), :]
            key = qkv_t[pl.ds(s.d + at, HEAD_DIM), :]
            val = qkv_t[pl.ds(2 * s.d + at, HEAD_DIM), :]
            gc = gctx_t[pl.ds(at, HEAD_DIM), :]
            p = jnp.exp(dot(key, q, 0, 0) + mask[...] - lse[h])
            g_p = dot(val, gc, 0, 0)
            inner = jnp.sum(g_p * p, axis=0, keepdims=True)
            g_s = (p * (g_p - inner)).astype(bf16)
            graw[pl.ds(at, HEAD_DIM), :] = dot(key, g_s)
            graw[pl.ds(s.d + at, HEAD_DIM), :] = dot(q, g_s, 1, 1)
            gp_t[pl.ds(2 * s.d + at, HEAD_DIM), :] = dot(gc, p.astype(bf16), 1, 1).astype(bf16)
        return carry

    lax.fori_loop(0, s.heads // HEADS_A_STEP, heads, 0)
    cosine, sine = cos[...], sin[...]
    hh = HEAD_DIM // 2
    scaling = HEAD_DIM ** (-0.5)
    for h in range(2 * s.heads):
        a = h * HEAD_DIM
        u1, u2 = graw[a : a + hh, :], graw[a + hh : a + 2 * hh, :]
        if h < s.heads:
            u1, u2 = u1 * scaling, u2 * scaling
        both = jnp.concatenate([u1 * cosine + u2 * sine, u2 * cosine - u1 * sine], axis=0)
        gp_t[a : a + HEAD_DIM, :] = both.astype(bf16)
    g_normed_t = jnp.zeros((s.d, s.tok), f32)
    ones = jnp.ones((8, s.tok), bf16)
    for rc in range(s.C):
        c = me[1] ^ rc
        part = gp_t[pl.ds(pl.multiple_of(c * s.qc, 8), s.qc), :]
        dw[rc, 0, :, : s.qc] = dot(normed_t, part, 1, 1).astype(bf16)
        store.start(rc)
        put_row(vec_grad, 4 + c, dot(ones, part, 1, 1)[0:1])
        g_normed_t += dot(w[rc, 0, :, : s.qc], part)
    moved, gain_grad, shift_grad = norm_back(hidden, vec[layer, 0:1], g_normed_t.T)
    g_in[...] = g_mid[...] + moved
    vec_grad[0] = gain_grad
    vec_grad[1] = shift_grad
    for rc in range(s.C):
        store.wait(rc)


SPACES = {"s": pltpu.SMEM, "v": VMEM, "a": HBM}


def specs(kinds):
    return [pl.BlockSpec(memory_space=SPACES[k]) for k in kinds]


def set_up(s, clock, segment_ids, vectors):
    def kernel(seg, vec_in, mask, vec, qb, hb):
        row = jnp.broadcast_to(seg[...].astype(f32), mask.shape)
        mask[...] = jnp.where(row == row.T, 0.0, -1e30)
        for l in range(LAYERS):
            for i in range(13):
                vec[l, i : i + 1] = vec_in[i, l : l + 1]
            rows = jnp.concatenate([vec_in[i, l : l + 1] for i in range(2, 5)], axis=1)
            hidden = jnp.concatenate([vec_in[i, l : l + 1] for i in range(8, 12)], axis=1)
            for c in range(s.C):
                qb[l, c] = rows[:, c * s.qc : (c + 1) * s.qc]
                hb[l, c] = hidden[:, c * s.fc : (c + 1) * s.fc]

    kinds = [(s.tok, s.tok), (LAYERS, 13, s.d), (LAYERS, s.C, 1, s.qc), (LAYERS, s.C, 1, s.fc)]
    return clock.call(kernel, (segment_ids, vectors), specs("vv"), [shape(k) for k in kinds], specs("vvvv"))


def update_vectors(s, clock, sums, more, states):
    def kernel(a, b, w, m, v, *outs):
        total = a[...] + b[...]
        for l in range(LAYERS):
            at, ff = total[2 * l], total[2 * l + 1]
            qkv = jnp.concatenate([at[4 + c, :, : s.qc] for c in range(s.C)], axis=1)
            hid = jnp.concatenate([ff[4 + c, :, : s.fc] for c in range(s.C)], axis=1)
            rows = [at[0], at[1]] + [qkv[:, i * s.d : (i + 1) * s.d] for i in range(3)]
            rows += [ff[3], ff[1], ff[2]] + [hid[:, i * s.d : (i + 1) * s.d] for i in range(4)] + [ff[0]]
            for i, grad in enumerate(rows):
                old = [r[i, l : l + 1] for r in (w, m, v)]
                for out, new in zip(outs, adamw(old[0], grad, old[1], old[2], 0.1, float(STEP))):
                    out[i, l : l + 1] = new

    return clock.call(kernel, (sums, more, *states), specs("vvvvv"), [shape(a.shape) for a in states], specs("vvv"), vmem=24)


def prepare(s, clock, jobs, weights):
    pairs = [(l, {"a": 0, "f": 2}[kind]) for l, kind in jobs]

    def kernel(*refs):
        ins, outs, bufs, sems = refs[:4], refs[4 : 4 + len(jobs)], refs[4 + len(jobs) : -1], refs[-1]
        copies = [
            pltpu.make_async_copy(ins[i + k].at[l], bufs[2 * j + k], sems.at[j, k])
            for j, (l, i) in enumerate(pairs)
            for k in range(2)
        ]
        for c in copies:
            c.start()
        for j, (_, i) in enumerate(pairs):
            for c in copies[2 * j : 2 * j + 2]:
                c.wait()
            first, second = bufs[2 * j : 2 * j + 2]
            if i == 0:
                outs[j][0, :, : s.qc] = first[...].astype(bf16)
                outs[j][0, :, s.qc :] = second[...].T.astype(bf16)
            else:
                outs[j][0] = first[...].astype(bf16)
                outs[j][1] = second[...].astype(bf16)

    sizes = [(1, s.u, s.an) if i == 0 else (2, s.u, s.fc) for _, i in pairs]
    return clock.call(
        kernel,
        weights,
        specs("aaaa"),
        [shape(k, bf16) for k in sizes],
        specs("v" * len(jobs)),
        [VMEM(weights[i + k].shape[1:], f32) for _, i in pairs for k in range(2)]
        + [pltpu.SemaphoreType.DMA((len(jobs), 2))],
    )


def adamw(weight, gradient, first, second, rate, step_count):
    first_new = beta_one * first + (1.0 - beta_one) * gradient
    second_new = beta_two * second + (1.0 - beta_two) * gradient * gradient
    first_hat = first_new / (1.0 - beta_one**step_count)
    second_hat = second_new / (1.0 - beta_two**step_count)
    weight_new = weight - rate * (first_hat / (jnp.sqrt(second_hat) + adam_eps) + decay_rate * weight)
    return (weight_new, first_new, second_new)


def update(clock, arrays, jobs, states, before):
    more = [] if before is None else list(before)
    n, na = len(states), len(arrays)
    wanted = [sorted({j for job in jobs for a, j in job[4] if a == i}) for i in range(na)]
    moves = [(k, i) for k, job in enumerate(jobs) for i in range(3 * job[1], 3 * job[1] + 3)]

    def kernel(*refs):
        grads, refs = refs[:na], refs[na:]
        ins, refs = refs[:n], refs[n + len(more) :]
        outs, refs = refs[:n], refs[n:]
        g_bufs, refs = refs[:na], refs[na:]
        bufs, news, sems = refs[: len(moves)], refs[len(moves) : 2 * len(moves)], refs[-1]
        first = [
            pltpu.make_async_copy(grads[i].at[j], g_bufs[i].at[at], sems.at[0, i, at])
            for i, js in enumerate(wanted)
            for at, j in enumerate(js)
        ]
        loads = [pltpu.make_async_copy(ins[i].at[jobs[k][0]], b, sems.at[1, q, 0]) for q, ((k, i), b) in enumerate(zip(moves, bufs))]
        saves = [pltpu.make_async_copy(b, outs[i].at[jobs[k][0]], sems.at[1, q, 1]) for q, ((k, i), b) in enumerate(zip(moves, news))]
        for c in first + loads:
            c.start()
        for c in first:
            c.wait()
        for k, (_, _, turned, rate, terms, part, columns) in enumerate(jobs):
            grad = sum(g_bufs[i][wanted[i].index(j), part].astype(f32) for i, j in terms)[:, columns]
            grad = grad.T if turned else grad
            for c in loads[3 * k : 3 * k + 3]:
                c.wait()
            w, m, v = (r[...] for r in bufs[3 * k : 3 * k + 3])
            for ref, new in zip(news[3 * k : 3 * k + 3], adamw(w, grad, m, v, rate, float(STEP))):
                ref[...] = new
            for c in saves[3 * k : 3 * k + 3]:
                c.start()
        for c in saves:
            c.wait()

    sizes = [VMEM(states[i].shape[1:], f32) for _, i in moves]
    return clock.call(
        kernel,
        (*arrays, *states, *more),
        [pl.BlockSpec(memory_space=pl.ANY)] * na + specs("a" * (n + len(more))),
        [shape(a.shape) for a in states],
        specs("a" * n),
        [VMEM((len(js),) + a.shape[1:], a.dtype) for js, a in zip(wanted, arrays)]
        + sizes
        + sizes
        + [pltpu.SemaphoreType.DMA((2, max(len(moves), na), max(2, *(len(js) for js in wanted))))],
        {na + n + i: i for i in range(len(more))},
    )


def rotary_tables(segment_ids):
    seg = segment_ids[0]
    start = jnp.sum((seg[:, None] < seg[None, :]).astype(jnp.int32), axis=0)
    places = jnp.arange(seg.shape[0], dtype=jnp.int32) - start
    freq_index = jnp.arange(HEAD_DIM // 2, dtype=f32)
    inverse = jnp.exp(freq_index * (-2.0 * math.log(10000.0) / HEAD_DIM))
    angles = inverse[:, None] * places.astype(f32)[None, :]
    return jnp.cos(angles), jnp.sin(angles)


def shards(
    rows,
    cols,
    residues,
    segment_ids,
    cotangent,
    qkv_weight,
    qkv_first,
    qkv_second,
    out_weight,
    out_first,
    out_second,
    up_weight,
    up_first,
    up_second,
    down_weight,
    down_first,
    down_second,
    vectors,
    vector_first,
    vector_second,
):
    net = Net(rows, cols)
    tok, d = residues.shape
    s = Sizes(net, tok, d, up_weight.shape[2] * cols)
    me = jnp.stack([lax.axis_index("rows"), lax.axis_index("cols")]).astype(jnp.int32)
    down_weight, down_first, down_second = (jnp.swapaxes(a, 1, 2) for a in (down_weight, down_first, down_second))
    cos, sin = rotary_tables(segment_ids)
    act = (tok, d)
    g = net.g
    sem = pltpu.SemaphoreType.DMA((cols,))
    packed = (2 * LAYERS, 4 + cols, 1, d)
    clock = Clock()

    def grads(unit, puts):
        sizes = [(rows * cols,)] if puts is None else [(len(p),) for p in puts]
        return [shape(k + unit, bf16) for k in sizes]

    def attend_forward(l, places, full, hidden):
        n = len(full)
        return clock.call(
            functools.partial(attend_in, s, l, places, n),
            (me, hidden, vec, qb, cos, sin, mask, *full),
            specs("s" + "v" * 6 + "a" * n),
            [shape(act), shape(act, bf16), shape((3 * d, tok), bf16), shape((d, tok), bf16), shape((s.heads, 1, tok))],
            specs("vvvvv"),
            [VMEM((cols, 1, d, s.an), bf16), VMEM((3 * d, tok), f32), sem],
        )

    def feed_forward(l, places, full, mid, ffn):
        n = len(full)
        return clock.call(
            functools.partial(ffn_forward, s, l, places, n),
            (me, mid, ffn, vec, hb, *full),
            specs("s" + "v" * 4 + "a" * n),
            [shape(act), shape((cols, tok, s.fc), bf16), shape((cols, tok, s.fc))],
            specs("vvv"),
            [VMEM((cols, 2, d, s.fc), bf16), sem],
        )

    def feed_back(l, places, puts, full, gx, mid, ffn, sums, kept):
        last, n = not kept, len(full)
        parts = grads((2 if last else 3, s.u, s.fc), puts)
        return clock.call(
            functools.partial(ffn_backward, s, l, places, puts, n, last),
            (me, gx, mid, ffn, vec, hb, sums, *full, *kept),
            specs("s" + "v" * 6 + "a" * n + ("" if last else "vvaa")),
            ([shape(act)] if last else []) + [shape(act), shape(packed)] + parts,
            specs(("v" if last else "") + "vv" + "a" * len(parts)),
            [VMEM((cols, 2, d, s.fc), bf16), VMEM((cols, 2, d, s.fc), bf16), sem, sem],
            {} if last else {n + 9: 2, n + 10: 3},
        )

    def attend_backward(l, places, puts, full, g_mid, hidden_in, qkv_t, ctx_t, lse, sums):
        n = len(full)
        parts = grads((1 if l == 0 else 3, s.u, s.an), puts)
        return clock.call(
            functools.partial(attend_back, s, l, places, puts, n),
            (me, g_mid, hidden_in, vec, cos, sin, mask, qkv_t, ctx_t, lse, sums, *full),
            specs("s" + "v" * 10 + "a" * n),
            [shape(act), shape(packed)] + parts,
            specs("vv" + "a" * len(parts)),
            [
                VMEM((cols, 1, d, s.an), bf16),
                VMEM((cols, 1, d, s.an), bf16),
                VMEM((3 * d, tok), bf16),
                VMEM((d, tok), bf16),
                VMEM((2 * d, tok), f32),
                sem,
                sem,
            ],
        )

    a_states = (qkv_weight, qkv_first, qkv_second, out_weight, out_first, out_second)
    f_states = (up_weight, up_first, up_second, down_weight, down_first, down_second)
    rate_qkv = 0.5 / math.sqrt(d)
    rate_out = 0.5 / math.sqrt(max(d * 4 // TOK_DEV, 1))
    rate_down = 0.5 / math.sqrt(s.ff)

    states = a_states + f_states

    def jobs_a(l, terms):
        return [(l, 0, False, rate_qkv, terms, 0, slice(0, s.qc)), (l, 1, True, rate_out, terms, 0, slice(s.qc, s.an))]

    def jobs_f(l, terms, part):
        whole = slice(0, s.fc)
        return [(l, 2, False, rate_qkv, terms, part, whole), (l, 3, False, rate_down, terms, part + 1, whole)]

    def steps(gen, n):
        for _ in range(n):
            out = next(gen)
        return out

    def finish(gen):
        for out in gen:
            if out is not None:
                return out

    weights = (qkv_weight, out_weight, up_weight, down_weight)
    (a0,) = prepare(s, clock, [(0, "a")], weights)
    at, at_last = net.gather_rels(), net.gather_rels(True)
    near = len(net.steps)
    a0 = net.gather(clock, a0[None], None)
    vec_states = [jnp.swapaxes(a, 0, 1) for a in (vectors, vector_first, vector_second)]
    steps(a0, 1)
    mask, vec, qb, hb = set_up(s, clock, segment_ids, vec_states[0])
    steps(a0, near - 1)
    f0, a1, f1 = prepare(s, clock, [(0, "f"), (1, "a"), (1, "f")], weights)
    f0, a1, f1 = net.gather(clock, f0[None]), net.gather(clock, a1[None]), net.gather(clock, f1[None], LONG, True)
    steps(f0, 1)
    steps(a1, 1)
    steps(a0, 1)
    steps(f0, near - 1)
    steps(a0, 1)
    steps(a1, near - 1)
    steps(a0, 1)
    steps(f0, 1)
    steps(f1, 1)
    steps(a1, 1)
    a0_full = finish(a0)
    mid0, ffn0, qkv0, ctx0, lse0 = attend_forward(0, at, a0_full, residues)
    steps(f0, 1)
    steps(f1, near - 1)
    steps(a1, 1)
    steps(f0, 1)
    steps(f1, 1)
    f0_full = finish(f0)
    hidden1, value0, slope0 = feed_forward(0, at, f0_full, mid0, ffn0)
    steps(a1, 1)
    a1_full = finish(a1)
    steps(f1, 1)
    mid1, ffn1, qkv1, ctx1, lse1 = attend_forward(1, at, a1_full, hidden1)
    f1_full = finish(f1)

    put = net.reduce_rels()
    none = jnp.zeros((1, d), f32)
    block_out, g_mid1, sums, *parts = feed_back(1, at_last, put, f1_full, cotangent, mid1, ffn1, none, ())
    f1 = net.reduce(clock, *parts, slow=(LONGER, LONG), vmem=(60, 60))
    steps(f1, 1)
    gx1, sums, *parts = attend_backward(1, at, put, a1_full, g_mid1, hidden1, qkv1, ctx1, lse1, sums)
    steps(f1, 1)
    g_mid0, sums, *parts = feed_back(0, at, put, f0_full, gx1, mid0, ffn0, sums, (value0, slope0, *parts))
    mixed = net.reduce(clock, *parts, slow=(LONGER, None), vmem=(60, 24))
    steps(mixed, 1)
    steps(f1, 2)
    steps(mixed, 1)
    gx0, sums, *parts = attend_backward(0, at, put, a0_full, g_mid0, residues, qkv0, ctx0, lse0, sums)
    a0 = net.reduce(clock, *parts, True)
    vec_sum = net.sum_all(clock, sums)
    steps(a0, 1)
    steps(f1, 1)
    steps(mixed, 2)
    steps(f1, near - 1)
    steps(a0, 1)
    steps(vec_sum, 2)
    f1_arrays, f1_terms = finish(f1)
    steps(vec_sum, near - 1)
    steps(mixed, 1)
    steps(a0, 1)
    steps(a0, 1)
    steps(mixed, near - 1)
    steps(vec_sum, 2)
    states_new = update(clock, f1_arrays, jobs_f(1, f1_terms, 0), states, None)
    vec_new = update_vectors(s, clock, *finish(vec_sum), vec_states)
    arrays, terms = finish(a0)
    more_arrays, more_terms = finish(mixed)
    more_terms = [(len(arrays) + a, i) for a, i in more_terms]
    jobs = jobs_a(0, terms) + jobs_a(1, more_terms) + jobs_f(0, more_terms, 1)
    states_new = list(update(clock, [*arrays, *more_arrays], jobs, states, states_new))
    states_new[9:] = [jnp.swapaxes(a, 1, 2) for a in states_new[9:]]
    return (block_out, gx0, *states_new, *(jnp.swapaxes(a, 0, 1) for a in vec_new))


def solution(mesh):
    rows, cols = mesh.shape["rows"], mesh.shape["cols"]
    tokens = P(("rows", "cols"), None)
    wide, tall = P(None, "rows", "cols"), P(None, "cols", "rows")
    states = (wide,) * 3 + (tall,) * 3 + (wide,) * 3 + (tall,) * 3
    return jax.shard_map(
        functools.partial(shards, rows, cols),
        mesh=mesh,
        in_specs=(tokens, tokens, tokens) + states + (P(),) * 3,
        out_specs=(tokens, tokens) + states + (P(),) * 3,
        check_vma=False,
    )
```

```python
import functools
import math

import jax
import jax.numpy as jnp
from jax import lax
from jax.experimental import pallas as pl
from jax.experimental.pallas import tpu as pltpu
from jax.sharding import PartitionSpec as P

HEAD_DIM = 32
LAYERS = 2
STEP = 5
TOK_DEV = 256

norm_eps = 1e-05
beta_one = 0.5
beta_two = 0.55
adam_eps = 1e-08
decay_rate = 0.01

f32 = jnp.float32
bf16 = jnp.bfloat16
VMEM = pltpu.VMEM
HBM = pltpu.HBM
SQRT_HALF = math.sqrt(0.5)
INV_SQRT_2PI = 1.0 / math.sqrt(2.0 * math.pi)
HEADS_A_STEP = 20
LONG, LONGER = 2 * 10**10, 10**12


class Clock:
    def __init__(self):
        self.before = []

    def wait(self, *xs):
        self.before += list(xs)
        return list(xs)

    def call(self, kernel, args, in_specs, outs, out_specs, scratch=(), aliases=None, flops=10**6, vmem=60):
        known = {id(x) for x in args}
        more = [x for x in self.before if id(x) not in known]
        n, extra = len(args), len(more)

        def body(*refs):
            kernel(*refs[:n], *refs[n + extra :])

        results = pl.pallas_call(
            body,
            in_specs=list(in_specs) + [pl.BlockSpec(memory_space=pl.ANY)] * extra,
            out_specs=list(out_specs),
            out_shape=list(outs),
            scratch_shapes=list(scratch),
            input_output_aliases=aliases or {},
            compiler_params=pltpu.CompilerParams(vmem_limit_bytes=vmem * 2**20),
            cost_estimate=pl.CostEstimate(flops=flops, bytes_accessed=10**5, transcendentals=0),
        )(*args, *more)
        self.before = [results[0]]
        return results

    def combine(self, arrays, outs, dtype=bf16, long=None, vmem=16):
        wanted = [sorted({j for o in outs for terms in o for a, j in terms if a == i}) for i in range(len(arrays))]
        runs = []
        for i, js in enumerate(wanted):
            for at, j in enumerate(js):
                if at and js[at - 1] == j - 1:
                    runs[-1][3] += 1
                else:
                    runs.append([i, j, at, 1])
        unit = arrays[0].shape[1:]

        def kernel(*refs):
            ins, out_refs = refs[: len(arrays)], refs[len(arrays) : len(arrays) + len(outs)]
            bufs, sems = refs[-1 - len(arrays) : -1], refs[-1]
            copies = [
                pltpu.make_async_copy(ins[i].at[pl.ds(j, k)], bufs[i].at[pl.ds(at, k)], sems.at[r])
                for r, (i, j, at, k) in enumerate(runs)
            ]
            for c in copies:
                c.start()
            for c in copies:
                c.wait()
            for ref, units in zip(out_refs, outs):
                for to, terms in enumerate(units):
                    values = [bufs[i][wanted[i].index(j)] for i, j in terms]
                    if len(values) > 1:
                        values = [sum(v.astype(f32) for v in values)]
                    ref[to] = values[0].astype(dtype)

        return self.call(
            kernel,
            arrays,
            [pl.BlockSpec(memory_space=pl.ANY)] * len(arrays),
            [shape((len(o),) + unit, dtype) for o in outs],
            [pl.BlockSpec(memory_space=VMEM)] * len(outs),
            [VMEM((len(js),) + unit, a.dtype) for js, a in zip(wanted, arrays)] + [pltpu.SemaphoreType.DMA((len(runs),))],
            flops=long or 10**6,
            vmem=vmem,
        )


class Net:
    def __init__(self, rows, cols):
        self.rows, self.cols = rows, cols
        bits = [(0, 1 << k) for k in range(2, cols.bit_length() - 1)] + [(1 << k, 0) for k in range(1, rows.bit_length() - 1)]
        self.steps = bits[::-1]
        self.group = [(0, 0)]
        for rr, rc in self.steps:
            self.group += [(r ^ rr, c ^ rc) for r, c in self.group]
        self.g = len(self.group)
        self.half = self.g // 2

    def send(self, x, rr, rc):
        mask = rr * self.cols + rc
        pairs = [(i, i ^ mask) for i in range(self.rows * self.cols)]
        return lax.ppermute(x, ("rows", "cols"), pairs)

    def rels(self, kind, core):
        dr, dc = {"o": (0, 0), "x": (1, 0), "y": (0, 2), "d": (1, 2)}[kind]
        return [(rr ^ dr, rc ^ dc ^ core) for rr, rc in self.group]

    def gather(self, clock, x, slow=LONG, one=False):
        g, h = self.g, self.half
        for rr, rc in self.steps:
            got = self.send(x, rr, rc)
            yield
            clock.wait(got)
            k = x.shape[0]
            (x,) = clock.combine([x, got], [[[(0, i)] for i in range(k)] + [[(1, i)] for i in range(k)]], long=slow)
        own = x
        xr, yr = self.send(own, 1, 0), self.send(own, 0, 2)
        yield
        clock.wait(xr, yr)
        xh, yh = clock.combine([xr, yr], [[[(0, i)] for i in range(h)], [[(1, i)] for i in range(h, g)]], long=slow)
        d0, d1 = self.send(xh, 0, 2), self.send(yh, 1, 0)
        (near,) = clock.combine([own, xr, yr], [[[(a, i)] for a in range(3) for i in range(g)]])
        far = self.send(near, 0, 1)
        yield
        clock.wait(d0, d1)
        rest = [d0, d1]
        if one:
            rest = clock.combine(rest, [[[(a, i)] for a in range(2) for i in range(h)]])
        far_rest = [self.send(r, 0, 1) for r in rest]
        yield
        clock.wait(far, *far_rest)
        yield [near, *rest, far, *far_rest]

    def gather_rels(self, one=False):
        places = []
        for core in (0, 1):
            o, x, y, d = (self.rels(k, core) for k in "oxyd")
            places += [o + x + y, d] if one else [o + x + y, d[: self.half], d[self.half :]]
        return places

    def reduce_rels(self):
        return [sum([self.rels(k, core) for k in "dxyo"], []) for core in (1, 0)]

    def reduce(self, clock, far, keep, fast=False, slow=(None, None), vmem=(24, 24)):
        g, h = self.g, self.half
        got = self.send(far, 0, 1)
        yield
        clock.wait(got)

        def both(at, n):
            return [[(0, i), (1, i)] for i in range(at, at + n)]

        away = [both(0, h) + both(g, h), both(h, h) + both(2 * g + h, h)]
        stay = [both(g + h, g) + both(3 * g, g)]
        if fast:
            to_x, to_y, rest = clock.combine([keep, got], away + stay, vmem=vmem[0])
        else:
            to_x, to_y = clock.combine([keep, got], away, vmem=vmem[0])
        from_x, from_y = self.send(to_x, 1, 0), self.send(to_y, 0, 2)
        yield
        if not fast:
            (rest,) = clock.combine([keep, got], stay, vmem=vmem[0])
            yield
        clock.wait(from_x, from_y)
        x1, y0 = clock.combine(
            [rest, from_x, from_y],
            [[[(0, i), (2, i)] for i in range(h)], [[(0, h + i), (1, i)] for i in range(h)]],
            long=slow[0],
            vmem=vmem[1],
        )
        x1, y0 = self.send(x1, 1, 0), self.send(y0, 0, 2)
        yield
        clock.wait(x1, y0)
        held = [rest, from_x, from_y, x1, y0]

        def parts(i):
            near = [(1, h + i), (4, i)] if i < h else [(3, i - h), (2, i)]
            return [(0, g + i)] + near

        if fast:
            sent = clock.combine(held, [[parts(i)] for i in range(1, g)], vmem=vmem[1])
            more = [self.send(t, rr, rc) for t, (rr, rc) in zip(sent, self.group[1:])]
            yield
            clock.wait(*more)
        else:
            n, more = g, []
            for rr, rc in reversed(self.steps):
                n //= 2
                units = [parts(i) + [(5 + m, i) for m in range(len(more))] for i in range(n, 2 * n)]
                (x,) = clock.combine(held + more, [units], long=None if more else slow[1], vmem=vmem[1])
                more.append(self.send(x, rr, rc))
                yield
                clock.wait(more[-1])
        yield held + more, parts(0) + [(5 + m, 0) for m in range(len(more))]

    def sum_all(self, clock, v):
        for rr, rc in [(0, 1), *self.steps, (1, 0), (0, 2)]:
            got = self.send(v, rr, rc)
            yield
            clock.wait(got)
            if (rr, rc) != (0, 2):
                (v,) = clock.combine([v, got], [[[(0, i), (1, i)] for i in range(v.shape[0])]], f32)
        yield v, got


def shape(dims, dtype=f32):
    return jax.ShapeDtypeStruct(tuple(dims), dtype)


def dot(a, b, ca=1, cb=0):
    return lax.dot_general(a, b, (((ca,), (cb,)), ((), ())), preferred_element_type=f32)


def norm_parts(x):
    mean = jnp.mean(x, axis=-1, keepdims=True)
    centered = x - mean
    scale = lax.rsqrt(jnp.mean(centered * centered, axis=-1, keepdims=True) + norm_eps)
    return centered * scale, scale


def norm_back(x, gain, grad):
    unit, scale = norm_parts(x)
    gain_grad = jnp.sum(grad * unit, axis=0, keepdims=True)
    shift_grad = jnp.sum(grad, axis=0, keepdims=True)
    g = grad * gain
    moved = g - jnp.mean(g, axis=-1, keepdims=True) - unit * jnp.mean(g * unit, axis=-1, keepdims=True)
    return moved * scale, gain_grad, shift_grad


class Load:
    def __init__(self, s, me, refs, places, w, sems):
        self.w, self.sems = w, sems
        if places is None:
            for r in range(s.R):
                for c in range(s.C):
                    rc = me[1] ^ c
                    part = refs[0].at[r * s.C + c]
                    pltpu.make_async_copy(part, w.at[rc, :, pl.ds(r * s.u, s.u)], sems.at[rc]).start()
            return
        for ref, rels in zip(refs, places):
            for i, (rr, rc) in enumerate(rels):
                row = pl.multiple_of((me[0] ^ rr) * s.u, s.u)
                pltpu.make_async_copy(ref.at[i], w.at[rc, :, pl.ds(row, s.u)], sems.at[rc]).start()

    def wait(self, rc):
        pltpu.make_async_copy(self.w.at[rc], self.w.at[rc], self.sems.at[rc]).wait()


class Store:
    def __init__(self, s, me, refs, places, w, sems, first=0):
        self.first = first
        self.s, self.me, self.refs, self.places, self.w, self.sems = s, me, refs, places, w, sems

    def start(self, now):
        s, me = self.s, self.me
        if self.places is None:
            for r in range(s.R):
                to = self.refs[0].at[r * s.C + (me[1] ^ now)]
                pltpu.make_async_copy(self.w.at[now, :, pl.ds(r * s.u, s.u)], to, self.sems.at[now]).start()
            return
        for ref, rels in zip(self.refs, self.places):
            for i, (rr, rc) in enumerate(rels):
                if rc == now:
                    row = pl.multiple_of((me[0] ^ rr) * s.u, s.u)
                    to = ref.at[i, pl.ds(self.first, self.w.shape[1])]
                    pltpu.make_async_copy(self.w.at[rc, :, pl.ds(row, s.u)], to, self.sems.at[rc]).start()

    def wait(self, rc):
        pltpu.make_async_copy(self.w.at[rc], self.w.at[rc], self.sems.at[rc]).wait()


class Sizes:
    def __init__(self, net, tok, d, ff):
        self.net, self.tok, self.d, self.ff = net, tok, d, ff
        self.R, self.C = net.rows, net.cols
        self.u = d // self.R
        self.qc, self.oc, self.fc = 3 * d // self.C, d // self.C, ff // self.C
        self.an = self.qc + self.oc
        self.heads = d // HEAD_DIM


def attend_in(s, layer, places, n, me, x, vec, qb, cos, sin, mask, *refs):
    pieces, refs = refs[:n], refs[n:]
    mid, ffn, qkv_t, ctx_t, lse, w, proj_t, sems = refs
    load = Load(s, me, pieces, places, w, sems)
    hidden = x[...].astype(f32)
    unit, _ = norm_parts(hidden)
    normed = (unit * vec[layer, 0:1] + vec[layer, 1:2]).astype(bf16)
    for rc in range(s.C):
        load.wait(rc)
        c = me[1] ^ rc
        part = dot(normed, w[rc, 0, :, : s.qc]) + qb[layer, c]
        proj_t[pl.ds(pl.multiple_of(c * s.qc, 8), s.qc), :] = part.T
    cosine, sine = cos[...], sin[...]
    hh = HEAD_DIM // 2
    scaling = HEAD_DIM ** (-0.5)
    for h in range(2 * s.heads):
        a = h * HEAD_DIM
        u1, u2 = proj_t[a : a + hh, :], proj_t[a + hh : a + 2 * hh, :]
        r1, r2 = u1 * cosine - u2 * sine, u2 * cosine + u1 * sine
        if h < s.heads:
            r1, r2 = r1 * scaling, r2 * scaling
        qkv_t[a : a + HEAD_DIM, :] = jnp.concatenate([r1, r2], axis=0).astype(bf16)
    qkv_t[2 * s.d :, :] = proj_t[2 * s.d :, :].astype(bf16)

    def heads(step, carry):
        for k in range(HEADS_A_STEP):
            h = step * HEADS_A_STEP + k
            at = pl.multiple_of(h * HEAD_DIM, HEAD_DIM)
            q = qkv_t[pl.ds(at, HEAD_DIM), :]
            key = qkv_t[pl.ds(s.d + at, HEAD_DIM), :]
            val = qkv_t[pl.ds(2 * s.d + at, HEAD_DIM), :]
            scores = dot(key, q, 0, 0) + mask[...]
            peak = jnp.max(scores, axis=0, keepdims=True)
            e = jnp.exp(scores - peak)
            total = jnp.sum(e, axis=0, keepdims=True)
            out = dot(val, e.astype(bf16)) * (1.0 / total)
            ctx_t[pl.ds(at, HEAD_DIM), :] = out.astype(bf16)
            lse[h] = peak + jnp.log(total)
        return carry

    lax.fori_loop(0, s.heads // HEADS_A_STEP, heads, 0)
    att_t = jnp.zeros((s.d, s.tok), f32)
    for rc in range(s.C):
        c = me[1] ^ rc
        att_t += dot(w[rc, 0, :, s.qc :], ctx_t[pl.ds(pl.multiple_of(c * s.oc, 8), s.oc), :])
    middle = hidden + att_t.T + vec[layer, 5:6]
    mid[...] = middle
    unit, _ = norm_parts(middle)
    ffn[...] = (unit * vec[layer, 6:7] + vec[layer, 7:8]).astype(bf16)


def put_row(ref, at, row):
    n = row.shape[1]
    if n % 128:
        row = jnp.concatenate([row, jnp.zeros((1, -n % 128), f32)], axis=1)
    ref[at, :, : row.shape[1]] = row


def copy_sums(old, new):
    if len(old.shape) == 4:
        new[...] = old[...]
    else:
        new[...] = jnp.zeros(new.shape, f32)


def gelu_parts(pre):
    phi = 0.5 * (1.0 + lax.erf(pre * SQRT_HALF))
    return pre * phi, phi + pre * (INV_SQRT_2PI * jnp.exp(-0.5 * pre * pre))


def ffn_forward(s, layer, places, n, me, mid, ffn, vec, hb, *refs):
    pieces, refs = refs[:n], refs[n:]
    out, act, slope, w, sems = refs
    load = Load(s, me, pieces, places, w, sems)
    total = mid[...] + vec[layer, 12:13]
    for rc in range(s.C):
        load.wait(rc)
        pre = dot(ffn[...], w[rc, 0]) + hb[layer, me[1] ^ rc]
        value, back = gelu_parts(pre)
        value = value.astype(bf16)
        act[rc], slope[rc] = value, back
        total += dot(value, w[rc, 1], 1, 1)
    out[...] = total


def ffn_backward(s, layer, places, puts, n, with_forward, me, gx, mid, ffn, vec, hb, sums, *refs):
    pieces, refs = refs[:n], refs[n:]
    if with_forward:
        out, refs = refs[0], refs[1:]
    else:
        act, slope, refs = refs[0], refs[1], refs[4:]
    g_mid, new_sums, *parts, w, dw, sems, out_sems = refs
    copy_sums(sums, new_sums)
    vec_grad = new_sums.at[2 * layer + 1]
    load = Load(s, me, pieces, places, w, sems)
    store = Store(s, me, parts, puts, dw, out_sems, 0 if with_forward else 1)
    g_in = gx[...].astype(f32)
    g = g_in.astype(bf16)
    g_t, ffn_t = g_in.T.astype(bf16), ffn[...].T
    total = mid[...] + vec[layer, 12:13] if with_forward else None
    g_ffn = jnp.zeros((s.tok, s.d), f32)
    for rc in range(s.C):
        load.wait(rc)
        up, down = w[rc, 0], w[rc, 1]
        if with_forward:
            value, back = gelu_parts(dot(ffn[...], up) + hb[layer, me[1] ^ rc])
            value = value.astype(bf16)
            total += dot(value, down, 1, 1)
        else:
            value, back = act[rc], slope[rc]
        g_pre = (dot(g, down) * back).astype(bf16)
        put_row(vec_grad, 4 + (me[1] ^ rc), jnp.sum(g_pre.astype(f32), axis=0, keepdims=True))
        dw[rc, 0] = dot(ffn_t, g_pre).astype(bf16)
        dw[rc, 1] = dot(g_t, value).astype(bf16)
        store.start(rc)
        g_ffn += dot(g_pre, up, 1, 1)
    if with_forward:
        out[...] = total
    moved, gain_grad, shift_grad = norm_back(mid[...], vec[layer, 6:7], g_ffn)
    middle_grad = g_in + moved
    g_mid[...] = middle_grad
    vec_grad[0] = jnp.sum(g.astype(f32), axis=0, keepdims=True)
    vec_grad[1] = gain_grad
    vec_grad[2] = shift_grad
    vec_grad[3] = jnp.sum(middle_grad.astype(bf16).astype(f32), axis=0, keepdims=True)
    for rc in range(s.C):
        store.wait(rc)


def attend_back(s, layer, places, puts, n, me, g_mid, x, vec, cos, sin, mask, qkv_t, ctx_t, lse, sums, *refs):
    pieces, refs = refs[:n], refs[n:]
    g_in, new_sums, *parts, w, dw, gp_t, gctx_t, graw, sems, out_sems = refs
    copy_sums(sums, new_sums)
    vec_grad = new_sums.at[2 * layer]
    load = Load(s, me, pieces, places, w, sems)
    store = Store(s, me, parts, puts, dw, out_sems)
    hidden = x[...].astype(f32)
    unit, _ = norm_parts(hidden)
    normed_t = (unit * vec[layer, 0:1] + vec[layer, 1:2]).T.astype(bf16)
    g_att = g_mid[...].astype(bf16)
    g_att_t = g_mid[...].T.astype(bf16)
    for rc in range(s.C):
        load.wait(rc)
        at = pl.multiple_of((me[1] ^ rc) * s.oc, 8)
        dw[rc, 0, :, s.qc :] = dot(g_att_t, ctx_t[pl.ds(at, s.oc), :], 1, 1).astype(bf16)
        gctx_t[pl.ds(at, s.oc), :] = dot(g_att, w[rc, 0, :, s.qc :]).T.astype(bf16)

    def heads(step, carry):
        for k in range(HEADS_A_STEP):
            h = step * HEADS_A_STEP + k
            at = pl.multiple_of(h * HEAD_DIM, HEAD_DIM)
            q = qkv_t[pl.ds(at, HEAD_DIM), :]
            key = qkv_t[pl.ds(s.d + at, HEAD_DIM), :]
            val = qkv_t[pl.ds(2 * s.d + at, HEAD_DIM), :]
            gc = gctx_t[pl.ds(at, HEAD_DIM), :]
            p = jnp.exp(dot(key, q, 0, 0) + mask[...] - lse[h])
            g_p = dot(val, gc, 0, 0)
            inner = jnp.sum(g_p * p, axis=0, keepdims=True)
            g_s = (p * (g_p - inner)).astype(bf16)
            graw[pl.ds(at, HEAD_DIM), :] = dot(key, g_s)
            graw[pl.ds(s.d + at, HEAD_DIM), :] = dot(q, g_s, 1, 1)
            gp_t[pl.ds(2 * s.d + at, HEAD_DIM), :] = dot(gc, p.astype(bf16), 1, 1).astype(bf16)
        return carry

    lax.fori_loop(0, s.heads // HEADS_A_STEP, heads, 0)
    cosine, sine = cos[...], sin[...]
    hh = HEAD_DIM // 2
    scaling = HEAD_DIM ** (-0.5)
    for h in range(2 * s.heads):
        a = h * HEAD_DIM
        u1, u2 = graw[a : a + hh, :], graw[a + hh : a + 2 * hh, :]
        if h < s.heads:
            u1, u2 = u1 * scaling, u2 * scaling
        both = jnp.concatenate([u1 * cosine + u2 * sine, u2 * cosine - u1 * sine], axis=0)
        gp_t[a : a + HEAD_DIM, :] = both.astype(bf16)
    g_normed_t = jnp.zeros((s.d, s.tok), f32)
    ones = jnp.ones((8, s.tok), bf16)
    for rc in range(s.C):
        c = me[1] ^ rc
        part = gp_t[pl.ds(pl.multiple_of(c * s.qc, 8), s.qc), :]
        dw[rc, 0, :, : s.qc] = dot(normed_t, part, 1, 1).astype(bf16)
        store.start(rc)
        put_row(vec_grad, 4 + c, dot(ones, part, 1, 1)[0:1])
        g_normed_t += dot(w[rc, 0, :, : s.qc], part)
    moved, gain_grad, shift_grad = norm_back(hidden, vec[layer, 0:1], g_normed_t.T)
    g_in[...] = g_mid[...] + moved
    vec_grad[0] = gain_grad
    vec_grad[1] = shift_grad
    for rc in range(s.C):
        store.wait(rc)


SPACES = {"s": pltpu.SMEM, "v": VMEM, "a": HBM}


def specs(kinds):
    return [pl.BlockSpec(memory_space=SPACES[k]) for k in kinds]


def set_up(s, clock, segment_ids, vectors):
    def kernel(seg, vec_in, mask, vec, qb, hb):
        row = jnp.broadcast_to(seg[...].astype(f32), mask.shape)
        mask[...] = jnp.where(row == row.T, 0.0, -1e30)
        for l in range(LAYERS):
            for i in range(13):
                vec[l, i : i + 1] = vec_in[i, l : l + 1]
            rows = jnp.concatenate([vec_in[i, l : l + 1] for i in range(2, 5)], axis=1)
            hidden = jnp.concatenate([vec_in[i, l : l + 1] for i in range(8, 12)], axis=1)
            for c in range(s.C):
                qb[l, c] = rows[:, c * s.qc : (c + 1) * s.qc]
                hb[l, c] = hidden[:, c * s.fc : (c + 1) * s.fc]

    kinds = [(s.tok, s.tok), (LAYERS, 13, s.d), (LAYERS, s.C, 1, s.qc), (LAYERS, s.C, 1, s.fc)]
    return clock.call(kernel, (segment_ids, vectors), specs("vv"), [shape(k) for k in kinds], specs("vvvv"))


def update_vectors(s, clock, sums, more, states):
    def kernel(a, b, w, m, v, *outs):
        total = a[...] + b[...]
        for l in range(LAYERS):
            at, ff = total[2 * l], total[2 * l + 1]
            qkv = jnp.concatenate([at[4 + c, :, : s.qc] for c in range(s.C)], axis=1)
            hid = jnp.concatenate([ff[4 + c, :, : s.fc] for c in range(s.C)], axis=1)
            rows = [at[0], at[1]] + [qkv[:, i * s.d : (i + 1) * s.d] for i in range(3)]
            rows += [ff[3], ff[1], ff[2]] + [hid[:, i * s.d : (i + 1) * s.d] for i in range(4)] + [ff[0]]
            for i, grad in enumerate(rows):
                old = [r[i, l : l + 1] for r in (w, m, v)]
                for out, new in zip(outs, adamw(old[0], grad, old[1], old[2], 0.1, float(STEP))):
                    out[i, l : l + 1] = new

    return clock.call(kernel, (sums, more, *states), specs("vvvvv"), [shape(a.shape) for a in states], specs("vvv"), vmem=24)


def prepare(s, clock, jobs, weights):
    pairs = [(l, {"a": 0, "f": 2}[kind]) for l, kind in jobs]

    def kernel(*refs):
        ins, outs, bufs, sems = refs[:4], refs[4 : 4 + len(jobs)], refs[4 + len(jobs) : -1], refs[-1]
        copies = [
            pltpu.make_async_copy(ins[i + k].at[l], bufs[2 * j + k], sems.at[j, k])
            for j, (l, i) in enumerate(pairs)
            for k in range(2)
        ]
        for c in copies:
            c.start()
        for j, (_, i) in enumerate(pairs):
            for c in copies[2 * j : 2 * j + 2]:
                c.wait()
            first, second = bufs[2 * j : 2 * j + 2]
            if i == 0:
                outs[j][0, :, : s.qc] = first[...].astype(bf16)
                outs[j][0, :, s.qc :] = second[...].T.astype(bf16)
            else:
                outs[j][0] = first[...].astype(bf16)
                outs[j][1] = second[...].astype(bf16)

    sizes = [(1, s.u, s.an) if i == 0 else (2, s.u, s.fc) for _, i in pairs]
    return clock.call(
        kernel,
        weights,
        specs("aaaa"),
        [shape(k, bf16) for k in sizes],
        specs("v" * len(jobs)),
        [VMEM(weights[i + k].shape[1:], f32) for _, i in pairs for k in range(2)]
        + [pltpu.SemaphoreType.DMA((len(jobs), 2))],
    )


def adamw(weight, gradient, first, second, rate, step_count):
    first_new = beta_one * first + (1.0 - beta_one) * gradient
    second_new = beta_two * second + (1.0 - beta_two) * gradient * gradient
    first_hat = first_new / (1.0 - beta_one**step_count)
    second_hat = second_new / (1.0 - beta_two**step_count)
    weight_new = weight - rate * (first_hat / (jnp.sqrt(second_hat) + adam_eps) + decay_rate * weight)
    return (weight_new, first_new, second_new)


def update(clock, arrays, jobs, states, before):
    more = [] if before is None else list(before)
    n, na = len(states), len(arrays)
    wanted = [sorted({j for job in jobs for a, j in job[4] if a == i}) for i in range(na)]
    moves = [(k, i) for k, job in enumerate(jobs) for i in range(3 * job[1], 3 * job[1] + 3)]

    def kernel(*refs):
        grads, refs = refs[:na], refs[na:]
        ins, refs = refs[:n], refs[n + len(more) :]
        outs, refs = refs[:n], refs[n:]
        g_bufs, refs = refs[:na], refs[na:]
        bufs, news, sems = refs[: len(moves)], refs[len(moves) : 2 * len(moves)], refs[-1]
        first = [
            pltpu.make_async_copy(grads[i].at[j], g_bufs[i].at[at], sems.at[0, i, at])
            for i, js in enumerate(wanted)
            for at, j in enumerate(js)
        ]
        loads = [pltpu.make_async_copy(ins[i].at[jobs[k][0]], b, sems.at[1, q, 0]) for q, ((k, i), b) in enumerate(zip(moves, bufs))]
        saves = [pltpu.make_async_copy(b, outs[i].at[jobs[k][0]], sems.at[1, q, 1]) for q, ((k, i), b) in enumerate(zip(moves, news))]
        for c in first + loads:
            c.start()
        for c in first:
            c.wait()
        for k, (_, _, turned, rate, terms, part, columns) in enumerate(jobs):
            grad = sum(g_bufs[i][wanted[i].index(j), part].astype(f32) for i, j in terms)[:, columns]
            grad = grad.T if turned else grad
            for c in loads[3 * k : 3 * k + 3]:
                c.wait()
            w, m, v = (r[...] for r in bufs[3 * k : 3 * k + 3])
            for ref, new in zip(news[3 * k : 3 * k + 3], adamw(w, grad, m, v, rate, float(STEP))):
                ref[...] = new
            for c in saves[3 * k : 3 * k + 3]:
                c.start()
        for c in saves:
            c.wait()

    sizes = [VMEM(states[i].shape[1:], f32) for _, i in moves]
    return clock.call(
        kernel,
        (*arrays, *states, *more),
        [pl.BlockSpec(memory_space=pl.ANY)] * na + specs("a" * (n + len(more))),
        [shape(a.shape) for a in states],
        specs("a" * n),
        [VMEM((len(js),) + a.shape[1:], a.dtype) for js, a in zip(wanted, arrays)]
        + sizes
        + sizes
        + [pltpu.SemaphoreType.DMA((2, max(len(moves), na), max(2, *(len(js) for js in wanted))))],
        {na + n + i: i for i in range(len(more))},
    )


def rotary_tables(segment_ids):
    seg = segment_ids[0]
    start = jnp.sum((seg[:, None] < seg[None, :]).astype(jnp.int32), axis=0)
    places = jnp.arange(seg.shape[0], dtype=jnp.int32) - start
    freq_index = jnp.arange(HEAD_DIM // 2, dtype=f32)
    inverse = jnp.exp(freq_index * (-2.0 * math.log(10000.0) / HEAD_DIM))
    angles = inverse[:, None] * places.astype(f32)[None, :]
    return jnp.cos(angles), jnp.sin(angles)


def shards(
    rows,
    cols,
    residues,
    segment_ids,
    cotangent,
    qkv_weight,
    qkv_first,
    qkv_second,
    out_weight,
    out_first,
    out_second,
    up_weight,
    up_first,
    up_second,
    down_weight,
    down_first,
    down_second,
    vectors,
    vector_first,
    vector_second,
):
    net = Net(rows, cols)
    tok, d = residues.shape
    s = Sizes(net, tok, d, up_weight.shape[2] * cols)
    me = jnp.stack([lax.axis_index("rows"), lax.axis_index("cols")]).astype(jnp.int32)
    down_weight, down_first, down_second = (jnp.swapaxes(a, 1, 2) for a in (down_weight, down_first, down_second))
    cos, sin = rotary_tables(segment_ids)
    act = (tok, d)
    g = net.g
    sem = pltpu.SemaphoreType.DMA((cols,))
    packed = (2 * LAYERS, 4 + cols, 1, d)
    clock = Clock()

    def grads(unit, puts):
        sizes = [(rows * cols,)] if puts is None else [(len(p),) for p in puts]
        return [shape(k + unit, bf16) for k in sizes]

    def attend_forward(l, places, full, hidden):
        n = len(full)
        return clock.call(
            functools.partial(attend_in, s, l, places, n),
            (me, hidden, vec, qb, cos, sin, mask, *full),
            specs("s" + "v" * 6 + "a" * n),
            [shape(act), shape(act, bf16), shape((3 * d, tok), bf16), shape((d, tok), bf16), shape((s.heads, 1, tok))],
            specs("vvvvv"),
            [VMEM((cols, 1, d, s.an), bf16), VMEM((3 * d, tok), f32), sem],
        )

    def feed_forward(l, places, full, mid, ffn):
        n = len(full)
        return clock.call(
            functools.partial(ffn_forward, s, l, places, n),
            (me, mid, ffn, vec, hb, *full),
            specs("s" + "v" * 4 + "a" * n),
            [shape(act), shape((cols, tok, s.fc), bf16), shape((cols, tok, s.fc))],
            specs("vvv"),
            [VMEM((cols, 2, d, s.fc), bf16), sem],
        )

    def feed_back(l, places, puts, full, gx, mid, ffn, sums, kept):
        last, n = not kept, len(full)
        parts = grads((2 if last else 3, s.u, s.fc), puts)
        return clock.call(
            functools.partial(ffn_backward, s, l, places, puts, n, last),
            (me, gx, mid, ffn, vec, hb, sums, *full, *kept),
            specs("s" + "v" * 6 + "a" * n + ("" if last else "vvaa")),
            ([shape(act)] if last else []) + [shape(act), shape(packed)] + parts,
            specs(("v" if last else "") + "vv" + "a" * len(parts)),
            [VMEM((cols, 2, d, s.fc), bf16), VMEM((cols, 2, d, s.fc), bf16), sem, sem],
            {} if last else {n + 9: 2, n + 10: 3},
        )

    def attend_backward(l, places, puts, full, g_mid, hidden_in, qkv_t, ctx_t, lse, sums):
        n = len(full)
        parts = grads((1 if l == 0 else 3, s.u, s.an), puts)
        return clock.call(
            functools.partial(attend_back, s, l, places, puts, n),
            (me, g_mid, hidden_in, vec, cos, sin, mask, qkv_t, ctx_t, lse, sums, *full),
            specs("s" + "v" * 10 + "a" * n),
            [shape(act), shape(packed)] + parts,
            specs("vv" + "a" * len(parts)),
            [
                VMEM((cols, 1, d, s.an), bf16),
                VMEM((cols, 1, d, s.an), bf16),
                VMEM((3 * d, tok), bf16),
                VMEM((d, tok), bf16),
                VMEM((2 * d, tok), f32),
                sem,
                sem,
            ],
        )

    a_states = (qkv_weight, qkv_first, qkv_second, out_weight, out_first, out_second)
    f_states = (up_weight, up_first, up_second, down_weight, down_first, down_second)
    rate_qkv = 0.5 / math.sqrt(d)
    rate_out = 0.5 / math.sqrt(max(d * 4 // TOK_DEV, 1))
    rate_down = 0.5 / math.sqrt(s.ff)

    states = a_states + f_states

    def jobs_a(l, terms):
        return [(l, 0, False, rate_qkv, terms, 0, slice(0, s.qc)), (l, 1, True, rate_out, terms, 0, slice(s.qc, s.an))]

    def jobs_f(l, terms, part):
        whole = slice(0, s.fc)
        return [(l, 2, False, rate_qkv, terms, part, whole), (l, 3, False, rate_down, terms, part + 1, whole)]

    def steps(gen, n):
        for _ in range(n):
            out = next(gen)
        return out

    def finish(gen):
        for out in gen:
            if out is not None:
                return out

    weights = (qkv_weight, out_weight, up_weight, down_weight)
    (a0,) = prepare(s, clock, [(0, "a")], weights)
    at, at_last = net.gather_rels(), net.gather_rels(True)
    near = len(net.steps)
    a0 = net.gather(clock, a0[None], None)
    vec_states = [jnp.swapaxes(a, 0, 1) for a in (vectors, vector_first, vector_second)]
    steps(a0, 1)
    mask, vec, qb, hb = set_up(s, clock, segment_ids, vec_states[0])
    steps(a0, near - 1)
    f0, a1, f1 = prepare(s, clock, [(0, "f"), (1, "a"), (1, "f")], weights)
    f0, a1, f1 = net.gather(clock, f0[None]), net.gather(clock, a1[None]), net.gather(clock, f1[None], LONG, True)
    steps(f0, 1)
    steps(a1, 1)
    steps(a0, 1)
    steps(f0, near - 1)
    steps(a0, 1)
    steps(a1, near - 1)
    steps(a0, 1)
    steps(f0, 1)
    steps(f1, 1)
    steps(a1, 1)
    a0_full = finish(a0)
    mid0, ffn0, qkv0, ctx0, lse0 = attend_forward(0, at, a0_full, residues)
    steps(f0, 1)
    steps(f1, near - 1)
    steps(a1, 1)
    steps(f0, 1)
    steps(f1, 1)
    f0_full = finish(f0)
    hidden1, value0, slope0 = feed_forward(0, at, f0_full, mid0, ffn0)
    steps(a1, 1)
    a1_full = finish(a1)
    steps(f1, 1)
    mid1, ffn1, qkv1, ctx1, lse1 = attend_forward(1, at, a1_full, hidden1)
    f1_full = finish(f1)

    put = net.reduce_rels()
    none = jnp.zeros((1, d), f32)
    block_out, g_mid1, sums, *parts = feed_back(1, at_last, put, f1_full, cotangent, mid1, ffn1, none, ())
    f1 = net.reduce(clock, *parts, slow=(LONGER, LONG), vmem=(60, 60))
    steps(f1, 1)
    gx1, sums, *parts = attend_backward(1, at, put, a1_full, g_mid1, hidden1, qkv1, ctx1, lse1, sums)
    steps(f1, 1)
    g_mid0, sums, *parts = feed_back(0, at, put, f0_full, gx1, mid0, ffn0, sums, (value0, slope0, *parts))
    mixed = net.reduce(clock, *parts, slow=(LONGER, None), vmem=(60, 24))
    steps(mixed, 1)
    steps(f1, 2)
    steps(mixed, 1)
    gx0, sums, *parts = attend_backward(0, at, put, a0_full, g_mid0, residues, qkv0, ctx0, lse0, sums)
    a0 = net.reduce(clock, *parts, True)
    vec_sum = net.sum_all(clock, sums)
    steps(a0, 1)
    steps(f1, 1)
    steps(mixed, 2)
    steps(f1, near - 1)
    steps(a0, 1)
    steps(vec_sum, 2)
    f1_arrays, f1_terms = finish(f1)
    steps(vec_sum, near - 1)
    steps(mixed, 1)
    steps(a0, 1)
    steps(a0, 1)
    steps(mixed, near - 1)
    states_new = update(clock, f1_arrays, jobs_f(1, f1_terms, 0), states, None)
    steps(vec_sum, 2)
    vec_new = update_vectors(s, clock, *finish(vec_sum), vec_states)
    arrays, terms = finish(a0)
    more_arrays, more_terms = finish(mixed)
    more_terms = [(len(arrays) + a, i) for a, i in more_terms]
    jobs = jobs_a(0, terms) + jobs_a(1, more_terms) + jobs_f(0, more_terms, 1)
    states_new = list(update(clock, [*arrays, *more_arrays], jobs, states, states_new))
    states_new[9:] = [jnp.swapaxes(a, 1, 2) for a in states_new[9:]]
    return (block_out, gx0, *states_new, *(jnp.swapaxes(a, 0, 1) for a in vec_new))


def solution(mesh):
    rows, cols = mesh.shape["rows"], mesh.shape["cols"]
    tokens = P(("rows", "cols"), None)
    wide, tall = P(None, "rows", "cols"), P(None, "cols", "rows")
    states = (wide,) * 3 + (tall,) * 3 + (wide,) * 3 + (tall,) * 3
    return jax.shard_map(
        functools.partial(shards, rows, cols),
        mesh=mesh,
        in_specs=(tokens, tokens, tokens) + states + (P(),) * 3,
        out_specs=(tokens, tokens) + states + (P(),) * 3,
        check_vma=False,
    )
```
